32 devices in a mesh: dp: 16 (over z, y, core), tensor: 2 (over x).
Axes of the slice: x: 2, y: 2, z: 4, core: 2. Of those that a mesh axis runs over, the one named last changes fastest.
Arguments:
- tokens: bfloat16 [8192, 768], P('dp'), may hold values from -6 to 6
- lengths: int32 [16], P('dp'), may hold values from 128 to 512, as said below
- positions: int32 [16, 76], P('dp'), may hold values from 0 to 512, as said below
- swap_ids: int32 [16, 76], P('dp'), may hold values from 0 to 255
- swap_rows: bfloat16 [256, 768], replicated, may hold values from -6 to 6
- w_query: bfloat16 [768, 768], P(None, 'tensor'), may hold values from -0.21875 to 0.21875
- b_query: bfloat16 [768], P('tensor'), may hold values from -3 to 3
- w_key: bfloat16 [768, 768], P(None, 'tensor'), may hold values from -0.21875 to 0.21875
- w_value: bfloat16 [768, 768], P(None, 'tensor'), may hold values from -0.21875 to 0.21875
- b_value: bfloat16 [768], P('tensor'), may hold values from -3 to 3
- w_out: bfloat16 [768, 768], P('tensor'), may hold values from -1.25 to 1.25
- b_out: bfloat16 [768], replicated, may hold values from -3 to 3
- first_gain: bfloat16 [768], replicated, may hold values from 0.5 to 1.5
- first_shift: bfloat16 [768], replicated, may hold values from -2.5 to 2.5
- w_up: bfloat16 [768, 3072], P(None, 'tensor'), may hold values from -0.21875 to 0.21875
- b_up: bfloat16 [3072], P('tensor'), may hold values from -3 to 3
- w_down: bfloat16 [3072, 768], P('tensor'), may hold values from -0.109375 to 0.109375
- b_down: bfloat16 [768], replicated, may hold values from -3 to 3
- second_gain: bfloat16 [768], replicated, may hold values from 0.5 to 1.5
- second_shift: bfloat16 [768], replicated, may hold values from -2.5 to 2.5
- cotangent: bfloat16 [8192, 768], P('dp'), may hold values from -6 to 6
Outputs:
- layer_out: bfloat16 [8192, 768], P('dp')
- grad_tokens: float32 [8192, 768], P('dp')
- grad_swap_rows: float32 [256, 768], replicated
- grad_w_query: float32 [768, 768], P(None, 'tensor')
- grad_b_query: float32 [768], P('tensor')
- grad_w_key: float32 [768, 768], P(None, 'tensor')
- grad_w_value: float32 [768, 768], P(None, 'tensor')
- grad_b_value: float32 [768], P('tensor')
- grad_w_out: float32 [768, 768], P('tensor')
- grad_b_out: float32 [768], replicated
- grad_first_gain: float32 [768], replicated
- grad_first_shift: float32 [768], replicated
- grad_w_up: float32 [768, 3072], P(None, 'tensor')
- grad_b_up: float32 [3072], P('tensor')
- grad_w_down: float32 [3072, 768], P('tensor')
- grad_b_down: float32 [768], replicated
- grad_second_gain: float32 [768], replicated
- grad_second_shift: float32 [768], replicated
The draws below stay inside these ranges and needn't reach their ends.
Inputs may be any that keep to these rules, and one draw needn't show every extreme that they name: `lengths`: at least one page has exactly 512 valid tokens and one has exactly 128. `positions`: slot s of page p holds a position below lengths[p], distinct within the page, when s < lengths[p] * 3 // 20, and 512 (no replacement) otherwise. `swap_ids`: read only where the slot's position is below 512.
All inputs are finite; a program needn't handle non-finite values.
Results may differ from the reference program's by a relative error of at most 0.013.
The reference program's roundings to bfloat16 on the way count: a program that leaves them out, or rounds other values in their place, can miss the bound.
Values sent between devices are 32-bit elements; how exact they have to be, the bound alone decides.
A program may use at most 128 MiB of HBM per device.

```python
import math
import jax
import jax.numpy as jnp
from jax import lax

D = 768
HEADS = 12
HEAD_DIM = 64
FF = 3072
SEQ = 512
REPL = 256
SLOTS = 76
PAGES = 16
TOKENS = 8192


def page_lengths(key):
    length_key, high_key, low_key = jax.random.split(jax.random.fold_in(key, 101), 3)
    drawn_lengths = jax.random.randint(length_key, (PAGES,), SEQ // 4, SEQ + 1)
    high_page = jax.random.randint(high_key, (), 0, PAGES)
    low_page = (high_page + 1 + jax.random.randint(low_key, (), 0, PAGES - 1)) % PAGES
    page_index = jnp.arange(PAGES)
    drawn_lengths = jnp.where(page_index == high_page, SEQ, drawn_lengths)
    return jnp.where(page_index == low_page, SEQ // 4, drawn_lengths).astype(jnp.int32)


def draw_lengths(key, part):
    base_lengths = page_lengths(key)
    return base_lengths


def draw_positions(key, part):
    base_lengths = page_lengths(key)
    key = jax.random.fold_in(key, 2)
    noise_bits = jax.random.randint(key, (PAGES, SEQ), 0, 2 ** 20)
    slot_place = jnp.arange(SEQ, dtype=jnp.int32)[None, :]
    rank_score = jnp.where(slot_place < base_lengths[:, None], noise_bits * SEQ + slot_place, 2 ** 30 + slot_place)
    ranked = jnp.argsort(rank_score, axis=-1, stable=True)[:, :SLOTS].astype(jnp.int32)
    live_slot = jnp.arange(SLOTS)[None, :] < (base_lengths * 3 // 20)[:, None]
    return jnp.where(live_slot, ranked, SEQ).astype(jnp.int32)


def touch_ends(array, own_key, smallest, high):
    extent = array.shape
    place = [jax.random.randint(jax.random.fold_in(own_key, axis), (), 0, extent[axis]) for axis in range(len(extent))]
    array = array.at[tuple(place)].set(smallest)
    longest = extent.index(max(extent))
    place[longest] = (place[longest] + 1) % extent[longest]
    return array.at[tuple(place)].set(high)


def steps_of(own_key, extent, shards, least, top_value):
    level, own = 1.0, jax.random.fold_in(own_key, 6)
    for dim, parts in shards:
        heights = jnp.exp(jax.random.uniform(jax.random.fold_in(own, dim), (parts,), jnp.float32, least / len(shards), top_value / len(shards)))
        level = level * jnp.repeat(heights, extent[dim] // parts).reshape([-1 if axis == dim else 1 for axis in range(len(extent))])
    return level


def scatter_about(key, shape, scale, most, pieces=(), kind=jnp.bfloat16):
    drawn = jax.random.normal(key, shape, jnp.float32) * scale
    if len(pieces) > 0:
        drawn = steps_of(key, shape, pieces, -0.22, 0.18) * drawn
    return jnp.clip(drawn, min=-most, max=most).astype(kind)


def setup_inputs(seed: int = 0) -> dict:
    keys = jax.random.split(jax.random.key(seed), 22)
    tokens = scatter_about(keys[0], (TOKENS, D), 1.0, 6.0, ((0, 16),))
    lengths = draw_lengths(jax.random.fold_in(keys[21], 71), 0)
    positions = draw_positions(jax.random.fold_in(keys[21], 71), 0)
    swap_ids = touch_ends(jax.random.randint(keys[3], (PAGES, SLOTS), 0, REPL), jax.random.fold_in(keys[3], 1), 0, REPL - 1).astype(jnp.int32)
    swap_rows = scatter_about(keys[4], (REPL, D), 1.0, 6.0)
    w_query = scatter_about(keys[5], (D, D), D ** -0.5, 0.21875, ((1, 2),))
    b_query = scatter_about(keys[6], (D,), 0.5, 3.0, ((0, 2),))
    w_key = scatter_about(keys[7], (D, D), D ** -0.5, 0.21875, ((1, 2),))
    w_value = scatter_about(keys[8], (D, D), D ** -0.5, 0.21875, ((1, 2),))
    b_value = scatter_about(keys[9], (D,), 0.5, 3.0, ((0, 2),))
    w_out = scatter_about(keys[10], (D, D), (max(1, D * 16 // SEQ)) ** -0.5, 1.25, ((0, 2),))
    b_out = scatter_about(keys[11], (D,), 0.5, 3.0)
    first_gain = jnp.clip(1.0 + 0.1 * jax.random.normal(keys[12], (D,), jnp.float32), 0.5, 1.5).astype(jnp.bfloat16)
    first_shift = scatter_about(keys[13], (D,), 0.3, 2.5)
    w_up = scatter_about(keys[14], (D, FF), D ** -0.5, 0.21875, ((1, 2),))
    b_up = scatter_about(keys[15], (FF,), 0.5, 3.0, ((0, 2),))
    w_down = scatter_about(keys[16], (FF, D), FF ** -0.5, 0.109375, ((0, 2),))
    b_down = scatter_about(keys[17], (D,), 0.5, 3.0)
    second_gain = jnp.clip(1.0 + 0.1 * jax.random.normal(keys[18], (D,), jnp.float32), 0.5, 1.5).astype(jnp.bfloat16)
    second_shift = scatter_about(keys[19], (D,), 0.3, 2.5)
    cotangent = scatter_about(keys[20], (TOKENS, D), 1.0, 6.0, ((0, 16),))
    return {"tokens": tokens, "lengths": lengths, "positions": positions, "swap_ids": swap_ids, "swap_rows": swap_rows, "w_query": w_query, "b_query": b_query, "w_key": w_key, "w_value": w_value, "b_value": b_value, "w_out": w_out, "b_out": b_out, "first_gain": first_gain, "first_shift": first_shift, "w_up": w_up, "b_up": b_up, "w_down": w_down, "b_down": b_down, "second_gain": second_gain, "second_shift": second_shift, "cotangent": cotangent}


@jax.custom_vjp
def low(v):
    return lax.optimization_barrier(v.astype(jnp.bfloat16)).astype(jnp.float32)

@jax.custom_vjp
def low_back(v):
    return v

def low_keep(v):
    return (low(v), None)

def low_pass(kept, grad):
    return (grad,)

def back_keep(v):
    return (v, None)

def back_low(kept, grad):
    return (low(grad),)
low.defvjp(low_keep, low_pass)
low_back.defvjp(back_keep, back_low)
norm_eps = 1e-12
mask_fill = -1000000000.0
highest = lax.Precision.HIGHEST

def product(left, right):
    return jnp.dot(left, right, precision=highest)

def normalize(hidden, norm_gain, norm_shift):
    row_mean = lax.optimization_barrier(jnp.mean(hidden, axis=-1, keepdims=True))
    centred = hidden - row_mean
    row_var = lax.optimization_barrier(jnp.mean(centred * centred, axis=-1, keepdims=True))
    return centred * lax.rsqrt(row_var + norm_eps) * norm_gain + norm_shift

def group_layer(token_rows, swap_table, params, lengths, positions, swap_ids):
    w_query, b_query, w_key, w_value, b_value, w_out, b_out, first_gain, first_shift, w_up, b_up, w_down, b_down, second_gain, second_shift = params
    group_size = token_rows.shape[0]
    chosen = swap_table[swap_ids]
    placed = jax.vmap(lambda page_tok, page_pos, page_new: page_tok.at[page_pos].set(page_new, mode='drop'))(token_rows, positions, chosen)
    flat_rows = placed.reshape(group_size * SEQ, D)
    query_scale = HEAD_DIM ** (-0.5)
    queries = low(low_back((product(flat_rows, w_query) + b_query) * query_scale))
    keys_all = low(low_back(product(flat_rows, w_key)))
    values_all = low(low_back(product(flat_rows, w_value) + b_value))

    def shaped(flat_part):
        return flat_part.reshape(group_size, SEQ, HEADS, HEAD_DIM)
    key_mask = jnp.where(jnp.arange(SEQ)[None, :] < lengths[:, None], 0.0, mask_fill).astype(jnp.float32)
    scores = jnp.einsum('gqhe,gkhe->ghqk', shaped(queries), shaped(keys_all), precision=highest)
    scores = low_back(scores + key_mask[:, None, None, :])
    probs = low(jax.nn.softmax(scores, axis=-1))
    mixed = jnp.einsum('ghqk,gkhe->gqhe', probs, shaped(values_all), precision=highest)
    mixed = low(low_back(mixed.reshape(group_size * SEQ, D)))
    branch = low_back(product(mixed, w_out) + b_out)
    first_out = normalize(flat_rows + branch, first_gain, first_shift)
    up_pre = low_back(product(low(first_out), w_up) + b_up)
    up_act = low(jax.nn.gelu(up_pre, approximate=False))
    down_out = low_back(product(up_act, w_down) + b_down)
    result = normalize(first_out + down_out, second_gain, second_shift)
    return result.reshape(group_size, SEQ, D)

def reference(tokens, lengths, positions, swap_ids, swap_rows, w_query, b_query, w_key, w_value, b_value, w_out, b_out, first_gain, first_shift, w_up, b_up, w_down, b_down, second_gain, second_shift, cotangent):
    params = tuple((weight.astype(jnp.float32) for weight in (w_query, b_query, w_key, w_value, b_value, w_out, b_out, first_gain, first_shift, w_up, b_up, w_down, b_down, second_gain, second_shift)))
    swap_table = swap_rows.astype(jnp.float32)
    page_count = lengths.shape[0]
    group_size = math.gcd(page_count, 8)
    group_count = page_count // group_size
    token_groups = tokens.astype(jnp.float32).reshape(group_count, group_size, SEQ, D)
    cot_groups = cotangent.astype(jnp.float32).reshape(group_count, group_size, SEQ, D)

    def group_step(running, group_block):
        group_tokens, group_cot, group_lengths, group_positions, group_ids = group_block

        def layer_fn(tokens_in, table_in, params_in):
            return group_layer(tokens_in, table_in, params_in, group_lengths, group_positions, group_ids)
        result, pullback = jax.vjp(layer_fn, group_tokens, swap_table, params)
        grad_tok, grad_table, grad_params = pullback(group_cot)
        total_table, total_params = running
        return ((total_table + grad_table, jax.tree.map(jnp.add, total_params, grad_params)), (result, grad_tok))
    zeros_init = (jnp.zeros_like(swap_table), jax.tree.map(jnp.zeros_like, params))
    (grad_table, grad_params), (results, grad_toks) = lax.scan(group_step, zeros_init, (token_groups, cot_groups, lengths.reshape(group_count, group_size), positions.reshape(group_count, group_size, -1), swap_ids.reshape(group_count, group_size, -1)))
    return (results.reshape(-1, D).astype(jnp.bfloat16), grad_toks.reshape(-1, D), grad_table, grad_params[0], grad_params[1], grad_params[2], grad_params[3], grad_params[4], grad_params[5], grad_params[6], grad_params[7], grad_params[8], grad_params[9], grad_params[10], grad_params[11], grad_params[12], grad_params[13], grad_params[14])
```

```python
import jax
import jax.numpy as jnp
from jax import lax
from jax.experimental import pallas as pl
from jax.experimental.pallas import tpu as pltpu
from jax.sharding import PartitionSpec as P

F32 = jnp.float32
MESH = pl.DeviceIdType.MESH

HEAD_DIM = 64


norm_eps = 1e-12
mask_fill = -1000000000.0
half_root = 0.7071067811865476
gauss_norm = 0.3989422804014327


def to_bf(value):
    return value.astype(jnp.bfloat16)


def product(left, right):
    return jnp.dot(left, right, preferred_element_type=jnp.float32)


def left_product(left, right):
    return lax.dot_general(
        left, right, (((0,), (0,)), ((), ())), preferred_element_type=jnp.float32
    )


def right_product(left, right):
    return lax.dot_general(
        left, right, (((1,), (1,)), ((), ())), preferred_element_type=jnp.float32
    )


def layer_norm(hidden, norm_gain, norm_shift):
    row_mean = jnp.mean(hidden, axis=-1, keepdims=True)
    centred = hidden - row_mean
    inv_std = lax.rsqrt(jnp.mean(centred * centred, axis=-1, keepdims=True) + norm_eps)
    normed = centred * inv_std
    return (normed * norm_gain + norm_shift, normed, inv_std)


def norm_back(upstream, normed, inv_std, norm_gain):
    scaled = upstream * norm_gain
    return inv_std * (
        scaled
        - jnp.mean(scaled, axis=-1, keepdims=True)
        - normed * jnp.mean(scaled * normed, axis=-1, keepdims=True)
    )


def gelu_slope(pre_act):
    return (
        0.5 * (1.0 + lax.erf(pre_act * half_root))
        + pre_act * jnp.exp(-0.5 * pre_act * pre_act) * gauss_norm
    )


def page_scores(queries, keys_page, length):
    key_bias = jnp.where(jnp.arange(keys_page.shape[0]) < length, 0.0, mask_fill).astype(
        jnp.float32
    )
    scores = jnp.einsum("qhe,khe->hqk", queries, keys_page, preferred_element_type=jnp.float32)
    return scores + key_bias[None, None, :]


def page_forward(page_block):
    queries, keys_page, values_page, length = page_block
    scores = page_scores(queries, keys_page, length)
    row_max = jnp.max(scores, axis=-1, keepdims=True)
    exponent = jnp.exp(scores - row_max)
    row_total = jnp.sum(exponent, axis=-1, keepdims=True)
    probs_low = to_bf(exponent / row_total)
    mixed_page = jnp.einsum(
        "hqk,khe->qhe", probs_low, values_page, preferred_element_type=jnp.float32
    )
    return (mixed_page, (row_max + jnp.log(row_total))[:, :, 0])


def page_backward(page_block):
    queries, keys_page, values_page, length, log_total, grad_mixed = page_block
    scores = page_scores(queries, keys_page, length)
    probs = jnp.exp(scores - log_total[:, :, None])
    grad_probs = jnp.einsum(
        "qhe,khe->hqk", grad_mixed, values_page, preferred_element_type=jnp.float32
    )
    grad_scores = to_bf(probs * (grad_probs - jnp.sum(probs * grad_probs, axis=-1, keepdims=True)))
    grad_queries = to_bf(
        jnp.einsum("hqk,khe->qhe", grad_scores, keys_page, preferred_element_type=jnp.float32)
    )
    grad_keys = to_bf(
        jnp.einsum("hqk,qhe->khe", grad_scores, queries, preferred_element_type=jnp.float32)
    )
    grad_values = to_bf(
        jnp.einsum("hqk,qhe->khe", to_bf(probs), grad_mixed, preferred_element_type=jnp.float32)
    )
    return (grad_queries, grad_keys, grad_values)


def split_pages(flat_part, page_count):
    return flat_part.reshape(page_count, -1, flat_part.shape[1] // HEAD_DIM, HEAD_DIM)


def forward(inputs, lengths, weights_all):
    (
        w_query,
        b_query,
        w_key,
        w_value,
        b_value,
        w_out,
        b_out,
        first_gain,
        first_shift,
        w_up,
        b_up,
        w_down,
        b_down,
        second_gain,
        second_shift,
    ) = weights_all
    page_count = lengths.shape[0]
    row_count = inputs.shape[0]
    query_scale = HEAD_DIM ** (-0.5)
    queries = to_bf((product(inputs, w_query) + b_query) * query_scale)
    keys_all = to_bf(product(inputs, w_key))
    values_all = to_bf(product(inputs, w_value) + b_value)
    mixed_heads, log_total = lax.map(
        page_forward,
        (
            split_pages(queries, page_count),
            split_pages(keys_all, page_count),
            split_pages(values_all, page_count),
            lengths,
        ),
    )
    mixed_heads = to_bf(mixed_heads.reshape(row_count, -1))
    branch = lax.psum(product(mixed_heads, w_out), "tensor") + b_out
    first_out, first_normed, first_inv = layer_norm(
        inputs.astype(jnp.float32) + branch, first_gain, first_shift
    )
    first_low = to_bf(first_out)
    up_pre = product(first_low, w_up) + b_up
    up_act = to_bf(jax.nn.gelu(up_pre, approximate=False))
    down_out = lax.psum(product(up_act, w_down), "tensor") + b_down
    result, second_normed, second_inv = layer_norm(first_out + down_out, second_gain, second_shift)
    kept_values = (
        queries,
        keys_all,
        values_all,
        mixed_heads,
        log_total,
        first_normed,
        first_inv,
        first_low,
        up_pre,
        up_act,
        second_normed,
        second_inv,
    )
    return (result, kept_values)


class Ring:
    RECV = ("rc", "rya", "rzb", "rza", "rma", "rmb", "ryb", "zoa", "yoa", "mob", "zob", "zoc", "co", "la", "lb")
    def __init__(self, chunks, eighth, width, offsets=(0,1,2,3,4,5,6,7)):
        self.offsets=offsets
        self.n, self.e, self.w = chunks, eighth, width
    def scratch(self):
        n,e,w=self.n,self.e,self.w
        V=lambda *s: pltpu.VMEM(s+(e,w),F32)
        bufs=[V(n,8), V(n,4), V(n), V(n,2), V(n), V(n), V(n), V(n)]
        return bufs+[pltpu.SemaphoreType.DMA((len(self.RECV), n)), pltpu.SemaphoreType.DMA((13,))]
    def bind(self, out, g, rc, rya, rzb, rza, rma, rmb, ryb, recv, sent):
        self.out,self.g,self.rc,self.rya,self.rzb,self.rza,self.rma,self.rmb,self.ryb=out,g,rc,rya,rzb,rza,rma,rmb,ryb
        self.recv,self.sent=recv,sent
        dp=lax.axis_index("dp"); self.dp=dp
        self.c=dp%2; self.y=(dp//2)%2; self.z=(dp//4)%4
        self.inner=((self.z+1)//2)==1
        self.s=self.z//2
        flip=lambda unit, bit: dp + unit*(1-2*bit)
        self.to_c=flip(1,self.c); self.to_y=flip(2,self.y); self.to_z=flip(4,self.z%2)
        self.to_m=dp+4*(3-2*self.z)
        self.t=lax.axis_index("tensor")
    def remote(self, name, k, src, dst, to):
        i=self.RECV.index(name)
        return pltpu.make_async_remote_copy(src, dst, self.sent.at[i], self.recv.at[i,k], device_id=(to,self.t), device_id_type=MESH)
    def wait(self, name, k, like):
        i=self.RECV.index(name)
        pltpu.make_async_copy(like, like, self.recv.at[i,k]).wait()
    def local(self, name, k, src, dst):
        return pltpu.make_async_copy(src, dst, self.recv.at[self.RECV.index(name),k])
    def barrier(self):
        bar=pltpu.get_barrier_semaphore()
        def signal(to): pl.semaphore_signal(bar, inc=1, device_id=(to,self.t), device_id_type=MESH)
        signal(self.to_c); signal(self.to_y); signal(self.to_z)
        @pl.when(self.inner)
        def _():
            signal(self.to_m)
            pl.semaphore_wait(bar,4)
        @pl.when(jnp.logical_not(self.inner))
        def _():
            pl.semaphore_wait(bar,3)
    def half(self,k): return self.out.at[k, pl.ds(self.c*4,4)]
    def oa(self,k,y): return self.out.at[k, self.c*4+y]
    def ob(self,k,s): return self.out.at[k, self.c*4+2+s]
    def stage0(self,k):
        self.remote("rc",k,self.g.at[k,pl.ds((1-self.c)*4,4)],self.rc.at[k],self.to_c).start()
    def stage1(self,k):
        g,c=self.g,self.c
        self.wait("rc",k,self.rc.at[k])
        for i in range(4):
            g[k,c*4+i]=g[k,c*4+i]+self.rc[k,i]
        self.remote("rya",k,g.at[k,c*4+1-self.y],self.rya.at[k],self.to_y).start()
        @pl.when(jnp.logical_not(self.inner))
        def _(): self.remote("rzb",k,g.at[k,pl.ds(c*4+2,2)],self.rzb.at[k],self.to_z).start()
    def stage2(self,k):
        g,c,y,s=self.g,self.c,self.y,self.s
        self.wait("rya",k,self.rya.at[k])
        g[k,c*4+y]=g[k,c*4+y]+self.rya[k]
        @pl.when(jnp.logical_not(self.inner))
        def _(): self.remote("rza",k,g.at[k,c*4+y],self.rza.at[k],self.to_z).start()
        @pl.when(self.inner)
        def _():
            self.wait("rzb",k,self.rzb.at[k])
            for i in range(2):
                g[k,c*4+2+i]=g[k,c*4+2+i]+self.rzb[k,i]
            self.remote("rmb",k,g.at[k,c*4+2+1-s],self.rmb.at[k],self.to_m).start()
    def stage3(self,k):
        g,c,y,s=self.g,self.c,self.y,self.s
        @pl.when(self.inner)
        def _():
            self.wait("rza",k,self.rza.at[k])
            g[k,c*4+y]=g[k,c*4+y]+self.rza[k]
            self.remote("rma",k,g.at[k,c*4+y],self.rma.at[k],self.to_m).start()
            self.wait("rmb",k,self.rmb.at[k])
            g[k,c*4+2+s]=g[k,c*4+2+s]+self.rmb[k]
            self.remote("ryb",k,g.at[k,c*4+2+s],self.ryb.at[k],self.to_y).start()
    def stage4(self,k):
        g,c,y,s=self.g,self.c,self.y,self.s
        @pl.when(self.inner)
        def _():
            self.wait("rma",k,self.rma.at[k])
            self.rma[k]=self.rma[k]+g[k,c*4+y]
            self.remote("zoa",k,self.rma.at[k],self.oa(k,y),self.to_z).start()
            self.remote("yoa",k,self.rma.at[k],self.oa(k,y),self.to_y).start()
            self.local("la",k,self.rma.at[k],self.oa(k,y)).start()
            self.wait("ryb",k,self.ryb.at[k])
            self.ryb[k]=self.ryb[k]+g[k,c*4+2+s]
            self.remote("mob",k,self.ryb.at[k],self.ob(k,s),self.to_m).start()
            self.remote("zob",k,self.ryb.at[k],self.ob(k,s),self.to_z).start()
            self.local("lb",k,self.ryb.at[k],self.ob(k,s)).start()
    def stage5(self,k):
        y,s=self.y,self.s
        @pl.when(jnp.logical_not(self.inner))
        def _():
            self.wait("zoa",k,self.oa(k,y))
            self.remote("yoa",k,self.oa(k,y),self.oa(k,y),self.to_y).start()
        @pl.when(self.inner)
        def _():
            self.wait("mob",k,self.ob(k,1-s))
            self.remote("zoc",k,self.ob(k,1-s),self.ob(k,1-s),self.to_z).start()
    def stage6(self,k):
        y,s=self.y,self.s
        self.wait("yoa",k,self.oa(k,1-y))
        @pl.when(self.inner)
        def _():
            self.wait("la",k,self.oa(k,y))
            self.wait("lb",k,self.ob(k,s))
        @pl.when(jnp.logical_not(self.inner))
        def _():
            self.wait("zob",k,self.ob(k,s))
            self.wait("zoc",k,self.ob(k,1-s))
        self.remote("co",k,self.half(k),self.half(k),self.to_c).start()
    def stage7(self,k):
        self.wait("co",k,self.half(k))
    def stages(self):
        return (self.stage7,self.stage6,self.stage5,self.stage4,self.stage3,self.stage2,self.stage1,self.stage0)
    def tick(self,t):
        for j,stage in zip(self.offsets[::-1],self.stages()):
            k=t-j
            if isinstance(k,int):
                if 0<=k<self.n: stage(k)
            else:
                @pl.when(jnp.logical_and(k>=0,k<self.n))
                def _(): stage(k)
    def finish(self):
        def drain(name, like):
            i=self.RECV.index(name)
            pltpu.make_async_copy(like,like,self.sent.at[i]).wait()
        drain("rc",self.rc); drain("rya",self.rya); drain("yoa",self.rya); drain("co",self.rc)
        @pl.when(self.inner)
        def _():
            for name in ("rmb","rma","ryb","zoa","mob","zob","zoc"): drain(name,self.rya)
        @pl.when(jnp.logical_not(self.inner))
        def _():
            drain("rzb",self.rzb); drain("rza",self.rza)

def comm_only(ring, grads, cid=3):
    n,e,w=ring.n,ring.e,ring.w
    def kern(in_ref, out_ref, *scr):
        *rs, insem = scr
        ring.bind(out_ref,*rs)
        for k in range(n): pltpu.make_async_copy(in_ref.at[k], ring.g.at[k], insem.at[k]).start()
        ring.barrier()
        def body(t,c):
            @pl.when(t<n)
            def _(): pltpu.make_async_copy(in_ref.at[t], ring.g.at[t], insem.at[t]).wait()
            ring.tick(t)
            return c
        lax.fori_loop(0,n+ring.offsets[-1],body,0)
        ring.finish()
    return pl.pallas_call(kern, out_shape=jax.ShapeDtypeStruct((n,8,e,w),F32),
        in_specs=[pl.BlockSpec(memory_space=pl.ANY)], out_specs=pl.BlockSpec(memory_space=pl.ANY),
        scratch_shapes=ring.scratch()+[pltpu.SemaphoreType.DMA((n,))], name="sum_dp",
        compiler_params=pltpu.CompilerParams(collective_id=cid, has_side_effects=True, vmem_limit_bytes=60*2**20))(grads)


def local(
    tokens,
    lengths,
    positions,
    swap_ids,
    swap_rows,
    w_query,
    b_query,
    w_key,
    w_value,
    b_value,
    w_out,
    b_out,
    first_gain,
    first_shift,
    w_up,
    b_up,
    w_down,
    b_down,
    second_gain,
    second_shift,
    cotangent,
    dp_count,
):
    page_count = lengths.shape[0]
    row_count, model_width = tokens.shape
    page_rows = row_count // page_count
    hit_table = positions[:, None, :] == jnp.arange(page_rows)[None, :, None]
    pick_table = swap_ids[:, :, None] == jnp.arange(swap_rows.shape[0])[None, None, :]
    chosen = to_bf(
        jnp.einsum(
            "psr,rd->psd",
            pick_table.astype(jnp.bfloat16),
            swap_rows,
            preferred_element_type=jnp.float32,
        )
    )
    placed = jnp.einsum(
        "pts,psd->ptd", hit_table.astype(jnp.bfloat16), chosen, preferred_element_type=jnp.float32
    )
    replaced = jnp.any(hit_table, axis=-1)[:, :, None]
    inputs = jnp.where(replaced, to_bf(placed), tokens.reshape(page_count, page_rows, model_width))
    inputs = inputs.reshape(row_count, model_width)
    weights_all = (
        w_query,
        b_query,
        w_key,
        w_value,
        b_value,
        w_out,
        b_out,
        first_gain,
        first_shift,
        w_up,
        b_up,
        w_down,
        b_down,
        second_gain,
        second_shift,
    )
    result, kept_values = forward(inputs, lengths, weights_all)
    (
        queries,
        keys_all,
        values_all,
        mixed_heads,
        log_total,
        first_normed,
        first_inv,
        first_low,
        up_pre,
        up_act,
        second_normed,
        second_inv,
    ) = kept_values
    grad_out = cotangent.astype(jnp.float32)
    grad_second_gain = jnp.sum(grad_out * second_normed, axis=0)
    grad_second_shift = jnp.sum(grad_out, axis=0)
    grad_second = norm_back(grad_out, second_normed, second_inv, second_gain)
    grad_down = to_bf(grad_second)
    grad_b_down = jnp.sum(grad_down.astype(jnp.float32), axis=0)
    grad_w_down = left_product(up_act, grad_down)
    grad_pre = to_bf(right_product(grad_down, w_down) * gelu_slope(up_pre))
    grad_b_up = jnp.sum(grad_pre.astype(jnp.float32), axis=0)
    grad_w_up = left_product(first_low, grad_pre)
    grad_first = grad_second + lax.psum(right_product(grad_pre, w_up), "tensor")
    grad_first_gain = jnp.sum(grad_first * first_normed, axis=0)
    grad_first_shift = jnp.sum(grad_first, axis=0)
    grad_resid = norm_back(grad_first, first_normed, first_inv, first_gain)
    grad_branch = to_bf(grad_resid)
    grad_b_out = jnp.sum(grad_branch.astype(jnp.float32), axis=0)
    grad_w_out = left_product(mixed_heads, grad_branch)
    grad_mixed = to_bf(right_product(grad_branch, w_out))
    grad_queries, grad_keys, grad_values = lax.map(
        page_backward,
        (
            split_pages(queries, page_count),
            split_pages(keys_all, page_count),
            split_pages(values_all, page_count),
            lengths,
            log_total,
            split_pages(grad_mixed, page_count),
        ),
    )
    grad_queries = grad_queries.reshape(row_count, -1) * HEAD_DIM ** (-0.5)
    grad_keys = grad_keys.reshape(row_count, -1)
    grad_values = grad_values.reshape(row_count, -1)
    grad_w_query = left_product(inputs, grad_queries)
    grad_b_query = jnp.sum(grad_queries.astype(jnp.float32), axis=0)
    grad_w_key = left_product(inputs, grad_keys)
    grad_w_value = left_product(inputs, grad_values)
    grad_b_value = jnp.sum(grad_values.astype(jnp.float32), axis=0)
    input_terms = (
        right_product(grad_queries, w_query)
        + right_product(grad_keys, w_key)
        + right_product(grad_values, w_value)
    )
    grad_inputs = grad_resid + lax.psum(input_terms, "tensor")
    grad_grid = grad_inputs.reshape(page_count, page_rows, model_width)
    grad_tokens = jnp.where(replaced, 0.0, grad_grid).reshape(row_count, model_width)
    place_table = product(
        hit_table[0].astype(jnp.bfloat16), pick_table[0].astype(jnp.bfloat16)
    )
    place_table = to_bf(place_table)
    tensor = lax.axis_index("tensor")
    half = model_width // 2

    def our_half(value):
        return lax.dynamic_slice(value, (0, tensor * half), (value.shape[0], half))

    at_half = our_half(grad_inputs)
    high = to_bf(at_half)
    low = to_bf(at_half - high.astype(F32))
    grad_swap = left_product(place_table, high) + left_product(place_table, low)
    shared = our_half(
        jnp.stack(
            [
                grad_b_out,
                grad_first_gain,
                grad_first_shift,
                grad_b_down,
                grad_second_gain,
                grad_second_shift,
            ]
        )
    )
    private = jnp.concatenate([grad_b_query, grad_b_value, grad_b_up]).reshape(-1, half)
    heads_width = w_query.shape[1]
    packed = jnp.concatenate([grad_swap, shared, private], axis=0)
    packed = packed.reshape(-1, model_width)
    stack = jnp.concatenate(
        [
            grad_w_down,
            grad_w_up[:, :model_width],
            grad_w_up[:, model_width:],
            grad_w_out,
            jnp.concatenate([grad_w_query, grad_w_key], axis=1),
            jnp.concatenate([grad_w_value[:half], grad_w_value[half:]], axis=1),
            packed,
        ],
        axis=0,
    )
    eighth = 24
    rows = stack.shape[0]
    chunks = -(-rows // (8 * eighth))
    stack = jnp.pad(stack, ((0, chunks * 8 * eighth - rows), (0, 0)))
    ring = Ring(chunks, eighth, model_width)
    summed = comm_only(ring, stack.reshape(chunks, 8, eighth, model_width))
    summed = summed.reshape(-1, model_width)
    if dp_count > 16:
        groups = [list(range(i, dp_count, 16)) for i in range(16)]
        summed = lax.psum(summed, "dp", axis_index_groups=groups)
    at = 0

    def take(count):
        nonlocal at
        at += count
        return summed[at - count : at]

    sum_down = take(grad_w_down.shape[0])
    sum_up = jnp.concatenate([take(model_width), take(model_width)], axis=1)
    sum_out = take(heads_width)
    sum_qk = take(model_width)
    value_part = take(half)
    sum_value = jnp.concatenate([value_part[:, :half], value_part[:, half:]], axis=0)
    small = take(packed.shape[0]).reshape(-1, half)
    repl = swap_rows.shape[0]
    count = repl + shared.shape[0]
    both = small[: count + (-count % 8)]
    other_half = lax.ppermute(both, "tensor", [(0, 1), (1, 0)])
    left = jnp.where(tensor == 0, both, other_half)
    right = jnp.where(tensor == 0, other_half, both)
    whole = jnp.concatenate([left, right], axis=1)
    vectors = small[count : count + private.shape[0]].reshape(-1)
    return (
        to_bf(result),
        grad_tokens,
        whole[:repl],
        sum_qk[:, :heads_width],
        vectors[:heads_width],
        sum_qk[:, heads_width:],
        sum_value,
        vectors[heads_width : 2 * heads_width],
        sum_out,
        whole[repl],
        whole[repl + 1],
        whole[repl + 2],
        sum_up,
        vectors[2 * heads_width :],
        sum_down,
        whole[repl + 3],
        whole[repl + 4],
        whole[repl + 5],
    )


def solution(mesh):
    in_specs = (
        P("dp", None),
        P("dp"),
        P("dp", None),
        P("dp", None),
        P(),
        P(None, "tensor"),
        P("tensor"),
        P(None, "tensor"),
        P(None, "tensor"),
        P("tensor"),
        P("tensor", None),
        P(),
        P(),
        P(),
        P(None, "tensor"),
        P("tensor"),
        P("tensor", None),
        P(),
        P(),
        P(),
        P("dp", None),
    )
    out_specs = (
        P("dp", None),
        P("dp", None),
        P(),
        P(None, "tensor"),
        P("tensor"),
        P(None, "tensor"),
        P(None, "tensor"),
        P("tensor"),
        P("tensor", None),
        P(),
        P(),
        P(),
        P(None, "tensor"),
        P("tensor"),
        P("tensor", None),
        P(),
        P(),
        P(),
    )
    count = mesh.shape["dp"]

    def run(*arrays):
        return local(*arrays, dp_count=count)

    return jax.shard_map(run, mesh=mesh, in_specs=in_specs, out_specs=out_specs, check_vma=False)
```

```python
import jax
import jax.numpy as jnp
from jax import lax
from jax.experimental import pallas as pl
from jax.experimental.pallas import tpu as pltpu
from jax.sharding import PartitionSpec as P

F32 = jnp.float32
MESH = pl.DeviceIdType.MESH

HEAD_DIM = 64


norm_eps = 1e-12
mask_fill = -1000000000.0
half_root = 0.7071067811865476
gauss_norm = 0.3989422804014327


def to_bf(value):
    return value.astype(jnp.bfloat16)


def product(left, right):
    return jnp.dot(left, right, preferred_element_type=jnp.float32)


def left_product(left, right):
    return lax.dot_general(
        left, right, (((0,), (0,)), ((), ())), preferred_element_type=jnp.float32
    )


def right_product(left, right):
    return lax.dot_general(
        left, right, (((1,), (1,)), ((), ())), preferred_element_type=jnp.float32
    )


def layer_norm(hidden, norm_gain, norm_shift):
    row_mean = jnp.mean(hidden, axis=-1, keepdims=True)
    centred = hidden - row_mean
    inv_std = lax.rsqrt(jnp.mean(centred * centred, axis=-1, keepdims=True) + norm_eps)
    normed = centred * inv_std
    return (normed * norm_gain + norm_shift, normed, inv_std)


def norm_back(upstream, normed, inv_std, norm_gain):
    scaled = upstream * norm_gain
    return inv_std * (
        scaled
        - jnp.mean(scaled, axis=-1, keepdims=True)
        - normed * jnp.mean(scaled * normed, axis=-1, keepdims=True)
    )


class Ring:
    RECV = ("rc", "rya", "rzb", "rza", "rma", "rmb", "ryb", "zoa", "yoa", "mob", "zob", "zoc", "co", "la", "lb")
    def __init__(self, chunks, eighth, width, offsets=(0,1,2,3,4,5,6,7)):
        self.offsets=offsets
        self.n, self.e, self.w = chunks, eighth, width
    def scratch(self):
        n,e,w=self.n,self.e,self.w
        V=lambda *s: pltpu.VMEM(s+(e,w),F32)
        bufs=[V(n,8), V(n,4), V(n), V(n,2), V(n), V(n), V(n), V(n)]
        return bufs+[pltpu.SemaphoreType.DMA((len(self.RECV), n)), pltpu.SemaphoreType.DMA((13,))]
    def bind(self, out, g, rc, rya, rzb, rza, rma, rmb, ryb, recv, sent):
        self.out,self.g,self.rc,self.rya,self.rzb,self.rza,self.rma,self.rmb,self.ryb=out,g,rc,rya,rzb,rza,rma,rmb,ryb
        self.recv,self.sent=recv,sent
        dp=lax.axis_index("dp"); self.dp=dp
        self.c=dp%2; self.y=(dp//2)%2; self.z=(dp//4)%4
        self.inner=((self.z+1)//2)==1
        self.s=self.z//2
        flip=lambda unit, bit: dp + unit*(1-2*bit)
        self.to_c=flip(1,self.c); self.to_y=flip(2,self.y); self.to_z=flip(4,self.z%2)
        self.to_m=dp+4*(3-2*self.z)
        self.t=lax.axis_index("tensor")
    def remote(self, name, k, src, dst, to):
        i=self.RECV.index(name)
        return pltpu.make_async_remote_copy(src, dst, self.sent.at[i], self.recv.at[i,k], device_id=(to,self.t), device_id_type=MESH)
    def wait(self, name, k, like):
        i=self.RECV.index(name)
        pltpu.make_async_copy(like, like, self.recv.at[i,k]).wait()
    def local(self, name, k, src, dst):
        return pltpu.make_async_copy(src, dst, self.recv.at[self.RECV.index(name),k])
    def barrier(self):
        bar=pltpu.get_barrier_semaphore()
        def signal(to): pl.semaphore_signal(bar, inc=1, device_id=(to,self.t), device_id_type=MESH)
        signal(self.to_c); signal(self.to_y); signal(self.to_z)
        @pl.when(self.inner)
        def _():
            signal(self.to_m)
            pl.semaphore_wait(bar,4)
        @pl.when(jnp.logical_not(self.inner))
        def _():
            pl.semaphore_wait(bar,3)
    def half(self,k): return self.out.at[k, pl.ds(self.c*4,4)]
    def oa(self,k,y): return self.out.at[k, self.c*4+y]
    def ob(self,k,s): return self.out.at[k, self.c*4+2+s]
    def stage0(self,k):
        self.remote("rc",k,self.g.at[k,pl.ds((1-self.c)*4,4)],self.rc.at[k],self.to_c).start()
    def stage1(self,k):
        g,c=self.g,self.c
        self.wait("rc",k,self.rc.at[k])
        for i in range(4):
            g[k,c*4+i]=g[k,c*4+i]+self.rc[k,i]
        self.remote("rya",k,g.at[k,c*4+1-self.y],self.rya.at[k],self.to_y).start()
        @pl.when(jnp.logical_not(self.inner))
        def _(): self.remote("rzb",k,g.at[k,pl.ds(c*4+2,2)],self.rzb.at[k],self.to_z).start()
    def stage2(self,k):
        g,c,y,s=self.g,self.c,self.y,self.s
        self.wait("rya",k,self.rya.at[k])
        g[k,c*4+y]=g[k,c*4+y]+self.rya[k]
        @pl.when(jnp.logical_not(self.inner))
        def _(): self.remote("rza",k,g.at[k,c*4+y],self.rza.at[k],self.to_z).start()
        @pl.when(self.inner)
        def _():
            self.wait("rzb",k,self.rzb.at[k])
            for i in range(2):
                g[k,c*4+2+i]=g[k,c*4+2+i]+self.rzb[k,i]
            self.remote("rmb",k,g.at[k,c*4+2+1-s],self.rmb.at[k],self.to_m).start()
    def stage3(self,k):
        g,c,y,s=self.g,self.c,self.y,self.s
        @pl.when(self.inner)
        def _():
            self.wait("rza",k,self.rza.at[k])
            g[k,c*4+y]=g[k,c*4+y]+self.rza[k]
            self.remote("rma",k,g.at[k,c*4+y],self.rma.at[k],self.to_m).start()
            self.wait("rmb",k,self.rmb.at[k])
            g[k,c*4+2+s]=g[k,c*4+2+s]+self.rmb[k]
            self.remote("ryb",k,g.at[k,c*4+2+s],self.ryb.at[k],self.to_y).start()
    def stage4(self,k):
        g,c,y,s=self.g,self.c,self.y,self.s
        @pl.when(self.inner)
        def _():
            self.wait("rma",k,self.rma.at[k])
            self.rma[k]=self.rma[k]+g[k,c*4+y]
            self.remote("zoa",k,self.rma.at[k],self.oa(k,y),self.to_z).start()
            self.remote("yoa",k,self.rma.at[k],self.oa(k,y),self.to_y).start()
            self.local("la",k,self.rma.at[k],self.oa(k,y)).start()
            self.wait("ryb",k,self.ryb.at[k])
            self.ryb[k]=self.ryb[k]+g[k,c*4+2+s]
            self.remote("mob",k,self.ryb.at[k],self.ob(k,s),self.to_m).start()
            self.remote("zob",k,self.ryb.at[k],self.ob(k,s),self.to_z).start()
            self.local("lb",k,self.ryb.at[k],self.ob(k,s)).start()
    def stage5(self,k):
        y,s=self.y,self.s
        @pl.when(jnp.logical_not(self.inner))
        def _():
            self.wait("zoa",k,self.oa(k,y))
            self.remote("yoa",k,self.oa(k,y),self.oa(k,y),self.to_y).start()
        @pl.when(self.inner)
        def _():
            self.wait("mob",k,self.ob(k,1-s))
            self.remote("zoc",k,self.ob(k,1-s),self.ob(k,1-s),self.to_z).start()
    def stage6(self,k):
        y,s=self.y,self.s
        self.wait("yoa",k,self.oa(k,1-y))
        @pl.when(self.inner)
        def _():
            self.wait("la",k,self.oa(k,y))
            self.wait("lb",k,self.ob(k,s))
        @pl.when(jnp.logical_not(self.inner))
        def _():
            self.wait("zob",k,self.ob(k,s))
            self.wait("zoc",k,self.ob(k,1-s))
        self.remote("co",k,self.half(k),self.half(k),self.to_c).start()
    def stage7(self,k):
        self.wait("co",k,self.half(k))
    def stages(self):
        return (self.stage7,self.stage6,self.stage5,self.stage4,self.stage3,self.stage2,self.stage1,self.stage0)
    def tick(self,t):
        for j,stage in zip(self.offsets[::-1],self.stages()):
            k=t-j
            if isinstance(k,int):
                if 0<=k<self.n: stage(k)
            else:
                @pl.when(jnp.logical_and(k>=0,k<self.n))
                def _(): stage(k)
    def finish(self):
        def drain(name, like):
            i=self.RECV.index(name)
            pltpu.make_async_copy(like,like,self.sent.at[i]).wait()
        drain("rc",self.rc); drain("rya",self.rya); drain("yoa",self.rya); drain("co",self.rc)
        @pl.when(self.inner)
        def _():
            for name in ("rmb","rma","ryb","zoa","mob","zob","zoc"): drain(name,self.rya)
        @pl.when(jnp.logical_not(self.inner))
        def _():
            drain("rzb",self.rzb); drain("rza",self.rza)

def comm_only(ring, grads, cid=3):
    n,e,w=ring.n,ring.e,ring.w
    def kern(in_ref, out_ref, *scr):
        *rs, insem = scr
        ring.bind(out_ref,*rs)
        for k in range(n): pltpu.make_async_copy(in_ref.at[k], ring.g.at[k], insem.at[k]).start()
        ring.barrier()
        def body(t,c):
            @pl.when(t<n)
            def _(): pltpu.make_async_copy(in_ref.at[t], ring.g.at[t], insem.at[t]).wait()
            ring.tick(t)
            return c
        lax.fori_loop(0,n+ring.offsets[-1],body,0)
        ring.finish()
    return pl.pallas_call(kern, out_shape=jax.ShapeDtypeStruct((n,8,e,w),F32),
        in_specs=[pl.BlockSpec(memory_space=pl.ANY)], out_specs=pl.BlockSpec(memory_space=pl.ANY),
        scratch_shapes=ring.scratch()+[pltpu.SemaphoreType.DMA((n,))], name="sum_dp",
        compiler_params=pltpu.CompilerParams(collective_id=cid, has_side_effects=True, vmem_limit_bytes=60*2**20))(grads)


class Forward:
    PARTS = 4
    SENDS = ("x", "z", "y", "cx", "cz", "cy")

    def __init__(self, rows, width, heads_width, hidden):
        self.rows, self.width, self.heads_width, self.hidden = rows, width, heads_width, hidden
        self.heads = heads_width // HEAD_DIM
        self.third_hidden = hidden // 3
        self.blocks = hidden // 256
        self.per_core = self.third_hidden // 256
        self.panels = 2 + 2 * self.per_core
        self.chunks = self.panels * self.PARTS
        self.part_rows = width // self.PARTS

    def outs(self):
        r, w, hw, hid = self.rows, self.width, self.heads_width, self.hidden
        bf = jnp.bfloat16
        S = jax.ShapeDtypeStruct
        return dict(
            layer=S((r, w), bf),
            wq=S((w, hw), bf), wk=S((w, hw), bf), wv=S((w, hw), bf), wo=S((hw, w), bf),
            wu=S((w, hid), bf), wd=S((hid, w), bf),
            inp=S((r, w), bf), place=S((r, 256), bf),
            q=S((2 * self.heads, r, HEAD_DIM), bf), k=S((2 * self.heads, r, HEAD_DIM), bf),
            v=S((2 * self.heads, r, HEAD_DIM), bf), lse=S((2 * self.heads, 1, r), F32),
            mixed=S((r, hw), bf),
            first_low=S((r, w), bf), first_normed=S((r, w), F32), first_inv=S((r, 1), F32),
            act=S((self.blocks, r, 256), bf), slope=S((2 * self.blocks, r, 256), bf),
            grad_second=S((r, w), F32), grad_down=S((r, w), bf), sums=S((8, w), F32),
        )

    def call(self, *args):
        outs = self.outs()
        names = list(outs)
        n = self.chunks
        panel = pltpu.VMEM((n, self.part_rows, 128), F32)
        scratch = [pltpu.VMEM(o.shape, o.dtype) for o in outs.values()]
        scratch += [panel] * 7
        scratch += [
            pltpu.VMEM((8, 2 * self.heads_width + self.hidden), F32),
            pltpu.VMEM((self.rows, self.width), F32),
            pltpu.VMEM((self.rows, self.width), F32),
            pltpu.VMEM((self.rows, self.width), F32),
            pltpu.SemaphoreType.DMA((len(self.SENDS), n)),
            pltpu.SemaphoreType.DMA((len(self.SENDS) + 1,)),
            pltpu.SemaphoreType.DMA((1,)),
            pltpu.SemaphoreType.DMA((len(names),)),
        ]
        vm = pl.BlockSpec(memory_space=pltpu.VMEM)
        specs = [pl.BlockSpec(memory_space=pltpu.SMEM)] + [vm] * (len(args) - 1)

        def kern(*refs):
            ins = refs[: len(args)]
            out_refs = dict(zip(names, refs[len(args) : len(args) + len(names)]))
            rest = refs[len(args) + len(names) :]
            held = dict(zip(names, rest[: len(names)]))
            self.body(ins, out_refs, held, *rest[len(names) :])

        got = pl.pallas_call(
            kern,
            out_shape=tuple(outs.values()),
            in_specs=specs,
            out_specs=tuple(pl.BlockSpec(memory_space=pl.ANY) for _ in names),
            scratch_shapes=scratch,
            name="forward_gather",
            compiler_params=pltpu.CompilerParams(
                collective_id=4, has_side_effects=True, vmem_limit_bytes=62 * 2**20
            ),
        )(*args)
        return dict(zip(names, got))

    def body(self, ins, out_refs, held, xs, lx, lz, ly, sx, sz, sy, bias_o, acc, acc_o, first_out, recv, sent, brecv, saved):
        (length, tokens, positions, swap_ids, swap_rows, wq, wk, wv, wo, wu, wd, bias, vectors, cot) = ins
        rows, width, hw, hidden = self.rows, self.width, self.heads_width, self.hidden
        n, parts, part_rows = self.chunks, self.PARTS, self.part_rows
        bf = jnp.bfloat16
        dp = lax.axis_index("dp")
        tensor = lax.axis_index("tensor")
        c, y, low = dp % 2, (dp // 2) % 2, (dp // 4) % 2

        def flip(unit, bit):
            return dp + unit * (1 - 2 * bit)

        to = {"x": (dp, 1 - tensor), "z": (flip(4, low), tensor), "y": (flip(2, y), tensor)}
        to["cx"] = to["cz"] = to["cy"] = (flip(1, c), tensor)
        own_third = jnp.where(low == 0, y, 2)
        z_third = jnp.where(low == 0, 2, y)
        y_third = 1 - y

        def remote(name, i, src, dst):
            s = self.SENDS.index(name)
            return pltpu.make_async_remote_copy(
                src.at[i], dst.at[i], sent.at[s], recv.at[s, i], device_id=to[name], device_id_type=MESH
            )

        def wait(name, i, dst):
            pltpu.make_async_copy(dst.at[i], dst.at[i], recv.at[self.SENDS.index(name), i]).wait()

        def save(name):
            pltpu.make_async_copy(
                held[name], out_refs[name], saved.at[list(held).index(name)]
            ).start()

        bar = pltpu.get_barrier_semaphore()
        for name in ("x", "z", "y", "cx"):
            pl.semaphore_signal(bar, inc=1, device_id=to[name], device_id_type=MESH)

        def put(p, value):
            xs[p * parts : (p + 1) * parts] = value.astype(F32).reshape(parts, part_rows, 128)

        def put_blocks(p, ref, at):
            for b in range(width // 128):
                lo = b * 128
                block = ref[pl.ds(pl.multiple_of(at, 128), 128), lo : lo + 128].astype(F32)
                done = 0
                while done < 128:
                    i, r = divmod(lo + done, part_rows)
                    take = min(128 - done, part_rows - r)
                    xs[p * parts + i, r : r + take] = block[done : done + take]
                    done += take

        def start_x(p):
            for i in range(p * parts, (p + 1) * parts):
                remote("x", i, xs, lx).start()

        def col(at):
            return pl.ds(pl.multiple_of(at, 128), 128)

        at = own_third * 128

        @pl.when(c == 0)
        def _():
            put(0, wq[:, col(at)])
            put(1, wk[:, col(at)])

        @pl.when(c == 1)
        def _():
            put(0, wv[:, col(at)])
            put_blocks(1, wo, at)

        pl.semaphore_wait(bar, 4)
        pltpu.make_async_remote_copy(
            bias, bias_o, sent.at[len(self.SENDS)], brecv.at[0], device_id=to["x"], device_id_type=MESH
        ).start()
        start_x(0)
        start_x(1)
        pc = self.per_core
        for j in range(pc):
            put(2 + j, wu[:, col(own_third * self.third_hidden + (pc * c + j) * 128)])
            start_x(2 + j)
        for j in range(pc):
            put_blocks(2 + pc + j, wd, own_third * self.third_hidden + (pc * c + j) * 128)
            start_x(2 + pc + j)

        def relay_x(i):
            wait("x", i, lx)
            remote("z", i, lx, lz).start()
            remote("cx", i, lx, sx).start()

            @pl.when(low == 0)
            def _():
                remote("y", i, lx, ly).start()

        def relay_z(i):
            wait("z", i, lz)
            remote("cz", i, lz, sz).start()

            @pl.when(low == 1)
            def _():
                remote("y", i, lz, ly).start()

        def relay_y(i):
            wait("y", i, ly)
            remote("cy", i, ly, sy).start()

        def tick(t):
            for relay, k in ((relay_x, t), (relay_z, t - 1), (relay_y, t - 2)):
                if isinstance(k, int):
                    if 0 <= k < n:
                        relay(k)
                else:

                    @pl.when(jnp.logical_and(k >= 0, k < n))
                    def _():
                        relay(k)

        place_rows = lax.broadcasted_iota(jnp.int32, (rows, positions.shape[1]), 0)
        hit = jnp.where(place_rows == positions[...], 1.0, 0.0).astype(bf)
        repl_rows = lax.broadcasted_iota(jnp.int32, (swap_rows.shape[0], positions.shape[1]), 0)
        chosen = jnp.where(repl_rows == swap_ids[...], 1.0, 0.0).astype(bf)
        place = right_product(hit, chosen)
        held["place"][...] = to_bf(place)
        save("place")
        swapped = product(held["place"][...], swap_rows[...])
        is_swapped = jnp.sum(place, axis=1, keepdims=True) > 0.5
        held["inp"][...] = to_bf(jnp.where(is_swapped, swapped, tokens[...].astype(F32)))
        save("inp")
        tick(0)
        inp = held["inp"]
        scale = HEAD_DIM ** (-0.5)
        qh, kh, vh, lse = held["q"], held["k"], held["v"], held["lse"]
        heads = self.heads

        def project(first_head, w_q, w_k, w_v, b_ref):
            part = to_bf((product(inp[...], w_q[...]) + b_ref[0:1, :hw]) * scale)
            for h in range(heads):
                qh[first_head + h] = part[:, h * HEAD_DIM : (h + 1) * HEAD_DIM]
            part = to_bf(product(inp[...], w_k[...]))
            for h in range(heads):
                kh[first_head + h] = part[:, h * HEAD_DIM : (h + 1) * HEAD_DIM]
            part = to_bf(product(inp[...], w_v[...]) + b_ref[0:1, hw : 2 * hw])
            for h in range(heads):
                vh[first_head + h] = part[:, h * HEAD_DIM : (h + 1) * HEAD_DIM]

        key_bias = jnp.where(
            lax.broadcasted_iota(jnp.int32, (rows, 1), 0) < length[0], 0.0, mask_fill
        ).astype(F32)

        def attend(h):
            scores = right_product(kh[h], qh[h]) + key_bias
            top = jnp.max(scores, axis=0, keepdims=True)
            exponent = jnp.exp(scores - top)
            total = jnp.sum(exponent, axis=0, keepdims=True)
            lse[h] = top + jnp.log(total)
            probs = to_bf(exponent * (1.0 / total))
            return to_bf(left_product(probs, vh[h]))

        def attend_pairs(first_head, mixed_ref, t0):
            for p in range(heads // 2):
                tick(t0 + 2 * p)
                one = attend(first_head + 2 * p)
                tick(t0 + 2 * p + 1)
                two = attend(first_head + 2 * p + 1)
                mixed_ref[:, p * 128 : (p + 1) * 128] = jnp.concatenate([one, two], axis=1)

        project(0, wq, wk, wv, bias)
        tick(1)
        tick(2)
        attend_pairs(0, held["mixed"], 3)
        save("mixed")
        acc[...] = product(held["mixed"][...], wo[...])
        attn = 2 * parts
        t = 3 + heads
        while t < attn + 2:
            tick(t)
            t += 1
        thirds = ((own_third, lx, sx, "cx"), (z_third, lz, sz, "cz"), (y_third, ly, sy, "cy"))

        def panel_of(ref, p):
            return to_bf(ref[p * parts : (p + 1) * parts].reshape(width, 128))

        def unblock(ref, value, at):
            for b in range(width // 128):
                ref[pl.ds(pl.multiple_of(at, 128), 128), b * 128 : (b + 1) * 128] = value[
                    b * 128 : (b + 1) * 128
                ]

        for third, mine, theirs, name in thirds:
            for i in range(attn):
                wait(name, i, theirs)

            def assemble(first, second):
                held["wq"][:, col(third * 128)] = panel_of(first, 0)
                held["wk"][:, col(third * 128)] = panel_of(first, 1)
                held["wv"][:, col(third * 128)] = panel_of(second, 0)
                unblock(held["wo"], panel_of(second, 1), third * 128)

            @pl.when(c == 0)
            def _():
                assemble(mine, theirs)

            @pl.when(c == 1)
            def _():
                assemble(theirs, mine)

        for name in ("wq", "wk", "wv", "wo"):
            save(name)
        pltpu.make_async_copy(bias_o, bias_o, brecv.at[0]).wait()
        tick(t)
        t += 1
        project(heads, held["wq"], held["wk"], held["wv"], bias_o)
        mixed_o = first_out
        other_parts = []
        for p in range(heads // 2):
            tick(t)
            one = attend(heads + 2 * p)
            tick(t + 1)
            two = attend(heads + 2 * p + 1)
            t += 2
            mixed_o[:, p * 128 : (p + 1) * 128] = jnp.concatenate([one, two], axis=1).astype(F32)
        for name in ("q", "k", "v", "lse"):
            save(name)
        acc_o[...] = product(to_bf(mixed_o[:, :hw]), held["wo"][...])
        branch = (acc[...] + acc_o[...]) + vectors[0:1]
        first, normed, inv = layer_norm(inp[...].astype(F32) + branch, vectors[1:2], vectors[2:3])
        first_out[...] = first
        held["first_low"][...] = to_bf(first)
        held["first_normed"][...] = normed
        held["first_inv"][...] = inv
        for name in ("first_low", "first_normed", "first_inv"):
            save(name)
        tick(t)
        t += 1
        act, slope = held["act"], held["slope"]

        def feed(b, at, w_ref, b_ref):
            up = (
                product(held["first_low"][...], w_ref[:, b * 256 : (b + 1) * 256])
                + b_ref[0:1, 2 * hw + b * 256 : 2 * hw + (b + 1) * 256]
            )
            cdf = 0.5 * (1.0 + lax.erf(up * half_root))
            slope[at] = to_bf(cdf + up * jnp.exp(-0.5 * up * up) * gauss_norm)
            return to_bf(up * cdf)

        for b in range(self.blocks):
            act[b] = feed(b, b, wu, bias)
            tick(t)
            t += 1
        save("act")
        acc[...] = product(act[0], wd[0:256])
        for b in range(1, self.blocks):
            acc[...] += product(act[b], wd[b * 256 : (b + 1) * 256])
        while t < n + 2:
            tick(t)
            t += 1
        for third, mine, theirs, name in thirds:
            for i in range(attn, attn + pc * parts):
                wait(name, i, theirs)
            for j in range(pc):
                at = third * self.third_hidden + (pc * c + j) * 128
                held["wu"][:, col(at)] = panel_of(mine, 2 + j)
                at = third * self.third_hidden + (pc * (1 - c) + j) * 128
                held["wu"][:, col(at)] = panel_of(theirs, 2 + j)
        save("wu")
        other_act = []
        for b in range(self.blocks):
            other_act.append(feed(b, self.blocks + b, held["wu"], bias_o))
        save("slope")
        for third, mine, theirs, name in thirds:
            for i in range(attn + pc * parts, n):
                wait(name, i, theirs)
            for j in range(pc):
                at = third * self.third_hidden + (pc * c + j) * 128
                unblock(held["wd"], panel_of(mine, 2 + pc + j), at)
                at = third * self.third_hidden + (pc * (1 - c) + j) * 128
                unblock(held["wd"], panel_of(theirs, 2 + pc + j), at)
        save("wd")
        acc_o[...] = product(other_act[0], held["wd"][0:256])
        for b in range(1, self.blocks):
            acc_o[...] += product(other_act[b], held["wd"][b * 256 : (b + 1) * 256])
        down = (acc[...] + acc_o[...]) + vectors[3:4]
        result, normed, inv = layer_norm(first_out[...] + down, vectors[4:5], vectors[5:6])
        held["layer"][...] = to_bf(result)
        save("layer")
        grad_out = cot[...].astype(F32)
        grad = norm_back(grad_out, normed, inv, vectors[4:5])
        held["grad_second"][...] = grad
        save("grad_second")
        low_grad = to_bf(grad)
        held["grad_down"][...] = low_grad
        save("grad_down")
        sums = held["sums"]
        sums[...] = jnp.zeros_like(sums)
        sums[0:1] = jnp.sum(grad_out * normed, axis=0, keepdims=True)
        sums[1:2] = jnp.sum(grad_out, axis=0, keepdims=True)
        sums[2:3] = jnp.sum(low_grad.astype(F32), axis=0, keepdims=True)
        save("sums")
        for name, like in (("x", xs), ("z", lx), ("y", lx), ("cx", lx), ("cz", lx), ("cy", lx)):
            pltpu.make_async_copy(like, like, sent.at[self.SENDS.index(name)]).wait()
        pltpu.make_async_copy(bias_o, bias_o, sent.at[len(self.SENDS)]).wait()
        for i, name in enumerate(held):
            pltpu.make_async_copy(held[name], out_refs[name], saved.at[i]).wait()


def local(
    tokens,
    lengths,
    positions,
    swap_ids,
    swap_rows,
    w_query,
    b_query,
    w_key,
    w_value,
    b_value,
    w_out,
    b_out,
    first_gain,
    first_shift,
    w_up,
    b_up,
    w_down,
    b_down,
    second_gain,
    second_shift,
    cotangent,
    dp_count,
):
    row_count, model_width = tokens.shape
    heads_width = w_query.shape[1]
    hidden = w_up.shape[1]
    bias = jnp.concatenate([b_query, b_value, b_up]).astype(F32)
    bias = jnp.broadcast_to(bias[None, :], (8, bias.shape[0]))
    vectors = jnp.stack(
        [b_out, first_gain, first_shift, b_down, second_gain, second_shift, b_out, b_out]
    ).astype(F32)
    fw = Forward(row_count, model_width, heads_width, hidden).call(
        lengths, tokens, positions, swap_ids, swap_rows, w_query, w_key, w_value, w_out, w_up, w_down,
        bias, vectors, cotangent,
    )
    result = fw["layer"]
    place_table = fw["place"]
    inputs = fw["inp"]
    heads = heads_width // HEAD_DIM
    grad_second_gain, grad_second_shift, grad_b_down = fw["sums"][0], fw["sums"][1], fw["sums"][2]
    grad_second, grad_down = fw["grad_second"], fw["grad_down"]
    blocks = hidden // 256
    act_own = fw["act"].transpose(1, 0, 2).reshape(row_count, hidden)
    slope_own = fw["slope"][:blocks].transpose(1, 0, 2).reshape(row_count, hidden)
    slope_other = fw["slope"][blocks:].transpose(1, 0, 2).reshape(row_count, hidden)
    first_low, first_normed, first_inv = fw["first_low"], fw["first_normed"], fw["first_inv"]
    grad_w_down = left_product(act_own, grad_down)
    pre_own = to_bf(right_product(grad_down, w_down) * slope_own)
    pre_other = to_bf(right_product(grad_down, fw["wd"]) * slope_other)
    grad_b_up = jnp.sum(pre_own.astype(F32), axis=0)
    grad_w_up = left_product(first_low, pre_own)
    grad_first = grad_second + (right_product(pre_own, w_up) + right_product(pre_other, fw["wu"]))
    grad_first_gain = jnp.sum(grad_first * first_normed, axis=0)
    grad_first_shift = jnp.sum(grad_first, axis=0)
    grad_resid = norm_back(grad_first, first_normed, first_inv, first_gain)
    grad_branch = to_bf(grad_resid)
    grad_b_out = jnp.sum(grad_branch.astype(F32), axis=0)
    grad_w_out = left_product(fw["mixed"], grad_branch)
    key_bias = jnp.where(jnp.arange(row_count) < lengths[0], 0.0, mask_fill).astype(F32)

    def attend_back(first, w_o):
        queries, keys_all, values_all = (fw[n][first : first + heads] for n in ("q", "k", "v"))
        grad_mixed = to_bf(right_product(grad_branch, w_o)).reshape(row_count, heads, HEAD_DIM)
        grad_mixed = grad_mixed.transpose(1, 0, 2)
        scores = jnp.einsum("hke,hqe->hkq", keys_all, queries, preferred_element_type=F32)
        probs = jnp.exp(scores + key_bias[None, :, None] - fw["lse"][first : first + heads])
        grad_probs = jnp.einsum("hke,hqe->hkq", values_all, grad_mixed, preferred_element_type=F32)
        grad_scores = to_bf(
            probs * (grad_probs - jnp.sum(probs * grad_probs, axis=1, keepdims=True))
        )
        grad_queries = to_bf(
            jnp.einsum("hkq,hke->qhe", grad_scores, keys_all, preferred_element_type=F32)
        )
        grad_keys = to_bf(
            jnp.einsum("hkq,hqe->khe", grad_scores, queries, preferred_element_type=F32)
        )
        grad_values = to_bf(
            jnp.einsum("hkq,hqe->khe", to_bf(probs), grad_mixed, preferred_element_type=F32)
        )
        return (
            grad_queries.reshape(row_count, -1) * HEAD_DIM ** (-0.5),
            grad_keys.reshape(row_count, -1),
            grad_values.reshape(row_count, -1),
        )

    gq, gk, gv = attend_back(0, w_out)
    grad_w_query = left_product(inputs, gq)
    grad_w_key = left_product(inputs, gk)
    grad_w_value = left_product(inputs, gv)
    grad_b_query = jnp.sum(gq.astype(F32), axis=0)
    grad_b_value = jnp.sum(gv.astype(F32), axis=0)
    oq, ok, ov = attend_back(heads, fw["wo"])
    own = right_product(gq, w_query) + right_product(gk, w_key) + right_product(gv, w_value)
    other = right_product(oq, fw["wq"]) + right_product(ok, fw["wk"]) + right_product(ov, fw["wv"])
    grad_inputs = grad_resid + (own + other)
    replaced = jnp.sum(place_table.astype(F32), axis=1, keepdims=True) > 0.5
    grad_tokens = jnp.where(replaced, 0.0, grad_inputs)
    tensor = lax.axis_index("tensor")
    half = model_width // 2

    def our_half(value):
        return lax.dynamic_slice(value, (0, tensor * half), (value.shape[0], half))

    at_half = our_half(grad_inputs)
    high = to_bf(at_half)
    low = to_bf(at_half - high.astype(F32))
    grad_swap = left_product(place_table, high) + left_product(place_table, low)
    shared = our_half(
        jnp.stack(
            [
                grad_b_out,
                grad_first_gain,
                grad_first_shift,
                grad_b_down,
                grad_second_gain,
                grad_second_shift,
            ]
        )
    )
    private = jnp.concatenate([grad_b_query, grad_b_value, grad_b_up]).reshape(-1, half)
    heads_width = w_query.shape[1]
    packed = jnp.concatenate([grad_swap, shared, private], axis=0)
    packed = packed.reshape(-1, model_width)
    stack = jnp.concatenate(
        [
            grad_w_down,
            grad_w_up[:, :model_width],
            grad_w_up[:, model_width:],
            grad_w_out,
            jnp.concatenate([grad_w_query, grad_w_key], axis=1),
            jnp.concatenate([grad_w_value[:half], grad_w_value[half:]], axis=1),
            packed,
        ],
        axis=0,
    )
    eighth = 24
    rows = stack.shape[0]
    chunks = -(-rows // (8 * eighth))
    stack = jnp.pad(stack, ((0, chunks * 8 * eighth - rows), (0, 0)))
    ring = Ring(chunks, eighth, model_width)
    summed = comm_only(ring, stack.reshape(chunks, 8, eighth, model_width))
    summed = summed.reshape(-1, model_width)
    if dp_count > 16:
        groups = [list(range(i, dp_count, 16)) for i in range(16)]
        summed = lax.psum(summed, "dp", axis_index_groups=groups)
    at = 0

    def take(count):
        nonlocal at
        at += count
        return summed[at - count : at]

    sum_down = take(grad_w_down.shape[0])
    sum_up = jnp.concatenate([take(model_width), take(model_width)], axis=1)
    sum_out = take(heads_width)
    sum_qk = take(model_width)
    value_part = take(half)
    sum_value = jnp.concatenate([value_part[:, :half], value_part[:, half:]], axis=0)
    small = take(packed.shape[0]).reshape(-1, half)
    repl = swap_rows.shape[0]
    count = repl + shared.shape[0]
    both = small[: count + (-count % 8)]
    other_half = lax.ppermute(both, "tensor", [(0, 1), (1, 0)])
    left = jnp.where(tensor == 0, both, other_half)
    right = jnp.where(tensor == 0, other_half, both)
    whole = jnp.concatenate([left, right], axis=1)
    vectors = small[count : count + private.shape[0]].reshape(-1)
    return (
        to_bf(result),
        grad_tokens,
        whole[:repl],
        sum_qk[:, :heads_width],
        vectors[:heads_width],
        sum_qk[:, heads_width:],
        sum_value,
        vectors[heads_width : 2 * heads_width],
        sum_out,
        whole[repl],
        whole[repl + 1],
        whole[repl + 2],
        sum_up,
        vectors[2 * heads_width :],
        sum_down,
        whole[repl + 3],
        whole[repl + 4],
        whole[repl + 5],
    )


def solution(mesh):
    in_specs = (
        P("dp", None),
        P("dp"),
        P("dp", None),
        P("dp", None),
        P(),
        P(None, "tensor"),
        P("tensor"),
        P(None, "tensor"),
        P(None, "tensor"),
        P("tensor"),
        P("tensor", None),
        P(),
        P(),
        P(),
        P(None, "tensor"),
        P("tensor"),
        P("tensor", None),
        P(),
        P(),
        P(),
        P("dp", None),
    )
    out_specs = (
        P("dp", None),
        P("dp", None),
        P(),
        P(None, "tensor"),
        P("tensor"),
        P(None, "tensor"),
        P(None, "tensor"),
        P("tensor"),
        P("tensor", None),
        P(),
        P(),
        P(),
        P(None, "tensor"),
        P("tensor"),
        P("tensor", None),
        P(),
        P(),
        P(),
    )
    count = mesh.shape["dp"]

    def run(*arrays):
        return local(*arrays, dp_count=count)

    return jax.shard_map(run, mesh=mesh, in_specs=in_specs, out_specs=out_specs, check_vma=False)
```

```python
from types import SimpleNamespace

import jax
import jax.numpy as jnp
from jax import lax
from jax.experimental import pallas as pl
from jax.experimental.pallas import tpu as pltpu
from jax.sharding import PartitionSpec as P

F32 = jnp.float32
MESH = pl.DeviceIdType.MESH

HEAD_DIM = 64


norm_eps = 1e-12
mask_fill = -1000000000.0
half_root = 0.7071067811865476
gauss_norm = 0.3989422804014327


def to_bf(value):
    return value.astype(jnp.bfloat16)


def product(left, right):
    return jnp.dot(left, right, preferred_element_type=jnp.float32)


def left_product(left, right):
    return lax.dot_general(
        left, right, (((0,), (0,)), ((), ())), preferred_element_type=jnp.float32
    )


def right_product(left, right):
    return lax.dot_general(
        left, right, (((1,), (1,)), ((), ())), preferred_element_type=jnp.float32
    )


def layer_norm(hidden, norm_gain, norm_shift):
    row_mean = jnp.mean(hidden, axis=-1, keepdims=True)
    centred = hidden - row_mean
    inv_std = lax.rsqrt(jnp.mean(centred * centred, axis=-1, keepdims=True) + norm_eps)
    normed = centred * inv_std
    return (normed * norm_gain + norm_shift, normed, inv_std)


def norm_back(upstream, normed, inv_std, norm_gain):
    scaled = upstream * norm_gain
    return inv_std * (
        scaled
        - jnp.mean(scaled, axis=-1, keepdims=True)
        - normed * jnp.mean(scaled * normed, axis=-1, keepdims=True)
    )


class Ring:
    RECV = ("rc", "rya", "rzb", "rza", "rma", "rmb", "ryb", "zoa", "yoa", "mob", "zob", "zoc", "co", "la", "lb")
    SLOTS = 8
    STAGES = 8

    def __init__(self, chunks, eighth, width):
        self.n, self.e, self.w = chunks, eighth, width

    def scratch(self):
        def buffer(*lead):
            return pltpu.VMEM((self.SLOTS,) + lead + (self.e, self.w), F32)

        bufs = [buffer(8), buffer(4), buffer(), buffer(2), buffer(), buffer(), buffer(), buffer()]
        sems = pltpu.SemaphoreType.DMA((len(self.RECV), self.SLOTS))
        return bufs + [sems, sems]

    def bind(self, out, g, rc, rya, rzb, rza, rma, rmb, ryb, recv, sent):
        self.out, self.g, self.rc, self.rya, self.rzb = out, g, rc, rya, rzb
        self.rza, self.rma, self.rmb, self.ryb = rza, rma, rmb, ryb
        self.recv, self.sent = recv, sent
        dp = lax.axis_index("dp")
        self.t = lax.axis_index("tensor")
        self.c, self.y, self.z = dp % 2, (dp // 2) % 2, (dp // 4) % 4
        self.inner = ((self.z + 1) // 2) == 1
        self.outer = jnp.logical_not(self.inner)
        self.s = self.z // 2
        self.to_c = dp + 1 - 2 * self.c
        self.to_y = dp + 2 * (1 - 2 * self.y)
        self.to_z = dp + 4 * (1 - 2 * (self.z % 2))
        self.to_m = dp + 4 * (3 - 2 * self.z)

    def slot(self, k):
        return k % self.SLOTS

    def remote(self, name, k, src, dst, to):
        i, j = self.RECV.index(name), self.slot(k)
        return pltpu.make_async_remote_copy(
            src, dst, self.sent.at[i, j], self.recv.at[i, j], device_id=(to, self.t), device_id_type=MESH
        )

    def wait(self, name, k, like):
        pltpu.make_async_copy(like, like, self.recv.at[self.RECV.index(name), self.slot(k)]).wait()

    def gone(self, name, k, like):
        pltpu.make_async_copy(like, like, self.sent.at[self.RECV.index(name), self.slot(k)]).wait()

    def local(self, name, k, src, dst):
        return pltpu.make_async_copy(src, dst, self.recv.at[self.RECV.index(name), self.slot(k)])

    def barrier(self, more):
        bar = pltpu.get_barrier_semaphore()

        def signal(to):
            pl.semaphore_signal(bar, inc=1, device_id=to, device_id_type=MESH)

        for place in (self.to_c, self.to_y, self.to_z):
            signal((place, self.t))
        for to in more:
            signal(to)

        @pl.when(self.inner)
        def _():
            signal((self.to_m, self.t))
            pl.semaphore_wait(bar, 4 + len(more))

        @pl.when(self.outer)
        def _():
            pl.semaphore_wait(bar, 3 + len(more))

    def half(self, k):
        return self.out.at[k, pl.ds(self.c * 4, 4)]

    def oa(self, k, y):
        return self.out.at[k, self.c * 4 + y]

    def ob(self, k, s):
        return self.out.at[k, self.c * 4 + 2 + s]

    def stage0(self, k):
        j = self.slot(k)
        self.remote("rc", k, self.g.at[j, pl.ds((1 - self.c) * 4, 4)], self.rc.at[j], self.to_c).start()

    def stage1(self, k):
        g, c, j = self.g, self.c, self.slot(k)
        self.wait("rc", k, self.rc.at[j])
        for i in range(4):
            g[j, c * 4 + i] = g[j, c * 4 + i] + self.rc[j, i]
        self.remote("rya", k, g.at[j, c * 4 + 1 - self.y], self.rya.at[j], self.to_y).start()

        @pl.when(self.outer)
        def _():
            self.remote("rzb", k, g.at[j, pl.ds(c * 4 + 2, 2)], self.rzb.at[j], self.to_z).start()

    def stage2(self, k):
        g, c, y, s, j = self.g, self.c, self.y, self.s, self.slot(k)
        self.wait("rya", k, self.rya.at[j])
        g[j, c * 4 + y] = g[j, c * 4 + y] + self.rya[j]

        @pl.when(self.outer)
        def _():
            self.remote("rza", k, g.at[j, c * 4 + y], self.rza.at[j], self.to_z).start()

        @pl.when(self.inner)
        def _():
            self.wait("rzb", k, self.rzb.at[j])
            for i in range(2):
                g[j, c * 4 + 2 + i] = g[j, c * 4 + 2 + i] + self.rzb[j, i]
            self.remote("rmb", k, g.at[j, c * 4 + 2 + 1 - s], self.rmb.at[j], self.to_m).start()

    def stage3(self, k):
        g, c, y, s, j = self.g, self.c, self.y, self.s, self.slot(k)

        @pl.when(self.inner)
        def _():
            self.wait("rza", k, self.rza.at[j])
            g[j, c * 4 + y] = g[j, c * 4 + y] + self.rza[j]
            self.remote("rma", k, g.at[j, c * 4 + y], self.rma.at[j], self.to_m).start()
            self.wait("rmb", k, self.rmb.at[j])
            g[j, c * 4 + 2 + s] = g[j, c * 4 + 2 + s] + self.rmb[j]
            self.remote("ryb", k, g.at[j, c * 4 + 2 + s], self.ryb.at[j], self.to_y).start()

    def stage4(self, k):
        g, c, y, s, j = self.g, self.c, self.y, self.s, self.slot(k)

        @pl.when(self.inner)
        def _():
            self.wait("rma", k, self.rma.at[j])
            self.rma[j] = self.rma[j] + g[j, c * 4 + y]
            self.remote("zoa", k, self.rma.at[j], self.oa(k, y), self.to_z).start()
            self.remote("yoa", k, self.rma.at[j], self.oa(k, y), self.to_y).start()
            self.local("la", k, self.rma.at[j], self.oa(k, y)).start()
            self.wait("ryb", k, self.ryb.at[j])
            self.ryb[j] = self.ryb[j] + g[j, c * 4 + 2 + s]
            self.remote("mob", k, self.ryb.at[j], self.ob(k, s), self.to_m).start()
            self.remote("zob", k, self.ryb.at[j], self.ob(k, s), self.to_z).start()
            self.local("lb", k, self.ryb.at[j], self.ob(k, s)).start()

    def stage5(self, k):
        y, s = self.y, self.s

        @pl.when(self.outer)
        def _():
            self.wait("zoa", k, self.oa(k, y))
            self.remote("yoa", k, self.oa(k, y), self.oa(k, y), self.to_y).start()

        @pl.when(self.inner)
        def _():
            self.wait("mob", k, self.ob(k, 1 - s))
            self.remote("zoc", k, self.ob(k, 1 - s), self.ob(k, 1 - s), self.to_z).start()

    def stage6(self, k):
        y, s = self.y, self.s
        self.wait("yoa", k, self.oa(k, 1 - y))

        @pl.when(self.inner)
        def _():
            self.wait("la", k, self.oa(k, y))
            self.wait("lb", k, self.ob(k, s))

        @pl.when(self.outer)
        def _():
            self.wait("zob", k, self.ob(k, s))
            self.wait("zoc", k, self.ob(k, 1 - s))

        self.remote("co", k, self.half(k), self.half(k), self.to_c).start()

    def stage7(self, k):
        j = self.slot(k)
        self.wait("co", k, self.half(k))
        self.gone("rc", k, self.rc.at[j])
        self.gone("co", k, self.rc.at[j])
        self.gone("rya", k, self.rya.at[j])
        self.gone("yoa", k, self.rya.at[j])

        @pl.when(self.inner)
        def _():
            for name in ("rmb", "rma", "ryb", "zoa", "mob", "zob", "zoc"):
                self.gone(name, k, self.rya.at[j])

        @pl.when(self.outer)
        def _():
            self.gone("rzb", k, self.rzb.at[j])
            self.gone("rza", k, self.rza.at[j])

    def tick(self, t):
        stages = (
            self.stage0, self.stage1, self.stage2, self.stage3,
            self.stage4, self.stage5, self.stage6, self.stage7,
        )
        for i in range(self.STAGES - 1, -1, -1):
            k = t - i
            if isinstance(k, int):
                if 0 <= k < self.n:
                    stages[i](k)
            else:

                @pl.when(jnp.logical_and(k >= 0, k < self.n))
                def _():
                    stages[i](k)


class Forward:
    PARTS = 4
    LAG = (2, 4)
    SENDS = ("x", "z", "y", "cx", "cz", "cy")

    def __init__(self, rows, width, heads_width, hidden):
        self.rows, self.width, self.heads_width, self.hidden = rows, width, heads_width, hidden
        self.heads = heads_width // HEAD_DIM
        self.third_hidden = hidden // 3
        self.blocks = hidden // 256
        self.per_core = self.third_hidden // 256
        self.panels = 2 + 2 * self.per_core
        self.chunks = self.panels * self.PARTS
        self.part_rows = width // self.PARTS

    def outs(self):
        r, w, hw, hid = self.rows, self.width, self.heads_width, self.hidden
        bf = jnp.bfloat16
        S = jax.ShapeDtypeStruct
        return dict(
            layer=S((r, w), bf),
            wq=S((w, hw), bf), wk=S((w, hw), bf), wv=S((w, hw), bf), wo=S((hw, w), bf),
            wu=S((w, hid), bf), wd=S((hid, w), bf),
            inp=S((r, w), bf), place=S((r, 256), bf),
            q=S((2 * self.heads, r, HEAD_DIM), bf), k=S((2 * self.heads, r, HEAD_DIM), bf),
            v=S((2 * self.heads, r, HEAD_DIM), bf), lse=S((2 * self.heads, 1, r), F32),
            mixed=S((r, hw), bf),
            first_low=S((r, w), bf), first_normed=S((r, w), F32), first_inv=S((r, 1), F32),
            act=S((self.blocks, r, 256), bf), slope=S((2 * self.blocks, r, 256), bf),
            grad_second=S((r, w), F32), grad_down=S((r, w), bf), sums=S((8, w), F32),
        )

    def call(self, *args):
        outs = self.outs()
        names = list(outs)
        n = self.chunks
        panel = pltpu.VMEM((n, self.part_rows, 128), F32)
        scratch = [pltpu.VMEM(o.shape, o.dtype) for o in outs.values()]
        scratch += [panel] * 7
        scratch += [
            pltpu.VMEM((8, 2 * self.heads_width + self.hidden), F32),
            pltpu.VMEM((self.rows, self.width), F32),
            pltpu.VMEM((self.rows, self.width), F32),
            pltpu.VMEM((self.rows, self.width), F32),
            pltpu.VMEM((self.blocks, self.rows, 256), jnp.bfloat16),
            pltpu.SemaphoreType.DMA((len(self.SENDS), n)),
            pltpu.SemaphoreType.DMA((len(self.SENDS) + 1,)),
            pltpu.SemaphoreType.DMA((1,)),
            pltpu.SemaphoreType.DMA((len(names),)),
        ]
        vm = pl.BlockSpec(memory_space=pltpu.VMEM)
        specs = [pl.BlockSpec(memory_space=pltpu.SMEM)] + [vm] * (len(args) - 1)

        def kern(*refs):
            ins = refs[: len(args)]
            out_refs = SimpleNamespace(**dict(zip(names, refs[len(args) : len(args) + len(names)])))
            rest = refs[len(args) + len(names) :]
            held = SimpleNamespace(**dict(zip(names, rest[: len(names)])))
            self.body(ins, out_refs, held, *rest[len(names) :])

        got = pl.pallas_call(
            kern,
            out_shape=tuple(outs.values()),
            in_specs=specs,
            out_specs=tuple(pl.BlockSpec(memory_space=pl.ANY) for _ in names),
            scratch_shapes=scratch,
            name="forward_gather",
            compiler_params=pltpu.CompilerParams(
                collective_id=4, has_side_effects=True, vmem_limit_bytes=62 * 2**20
            ),
        )(*args)
        return SimpleNamespace(**dict(zip(names, got)))

    def body(self, ins, out_refs, held, xs, lx, lz, ly, sx, sz, sy, bias_o, acc, acc_o, first_out, act_o, recv, sent, brecv, saved):
        (length, tokens, positions, swap_ids, swap_rows, wq, wk, wv, wo, wu, wd, small, cot) = ins
        rows, width, hw, hidden = self.rows, self.width, self.heads_width, self.hidden
        bias = small.at[:, 0 : 2 * hw + hidden]

        def vector(i):
            at = 2 * hw + hidden + i * width
            return small[0:1, at : at + width]

        n, parts, part_rows = self.chunks, self.PARTS, self.part_rows
        bf = jnp.bfloat16
        dp = lax.axis_index("dp")
        tensor = lax.axis_index("tensor")
        c, y, low = dp % 2, (dp // 2) % 2, (dp // 4) % 2

        def flip(unit, bit):
            return dp + unit * (1 - 2 * bit)

        to = {"x": (dp, 1 - tensor), "z": (flip(4, low), tensor), "y": (flip(2, y), tensor)}
        to["cx"] = to["cz"] = to["cy"] = (flip(1, c), tensor)
        own_third = jnp.where(low == 0, y, 2)
        z_third = jnp.where(low == 0, 2, y)
        y_third = 1 - y

        def remote(name, i, src, dst):
            s = self.SENDS.index(name)
            return pltpu.make_async_remote_copy(
                src.at[i], dst.at[i], sent.at[s], recv.at[s, i], device_id=to[name], device_id_type=MESH
            )

        def wait(name, i, dst):
            pltpu.make_async_copy(dst.at[i], dst.at[i], recv.at[self.SENDS.index(name), i]).wait()

        kept = list(vars(held).values())
        kept_out = list(vars(out_refs).values())

        def save(*refs):
            for ref in refs:
                i = [one is ref for one in kept].index(True)
                pltpu.make_async_copy(ref, kept_out[i], saved.at[i]).start()

        bar = pltpu.get_barrier_semaphore()
        for name in ("x", "z", "y", "cx"):
            pl.semaphore_signal(bar, inc=1, device_id=to[name], device_id_type=MESH)

        def put(p, value):
            xs[p * parts : (p + 1) * parts] = value.astype(F32).reshape(parts, part_rows, 128)

        def put_blocks(p, ref, at):
            for b in range(width // 128):
                lo = b * 128
                block = ref[pl.ds(pl.multiple_of(at, 128), 128), lo : lo + 128].astype(F32)
                done = 0
                while done < 128:
                    i, r = divmod(lo + done, part_rows)
                    take = min(128 - done, part_rows - r)
                    xs[p * parts + i, r : r + take] = block[done : done + take]
                    done += take

        def start_x(p):
            for i in range(p * parts, (p + 1) * parts):
                remote("x", i, xs, lx).start()

        def col(at):
            return pl.ds(pl.multiple_of(at, 128), 128)

        at = own_third * 128

        @pl.when(c == 0)
        def _():
            put(0, wq[:, col(at)])
            put(1, wk[:, col(at)])

        @pl.when(c == 1)
        def _():
            put(0, wv[:, col(at)])
            put_blocks(1, wo, at)

        pl.semaphore_wait(bar, 4)
        pltpu.make_async_remote_copy(
            bias, bias_o, sent.at[len(self.SENDS)], brecv.at[0], device_id=to["x"], device_id_type=MESH
        ).start()
        start_x(0)
        start_x(1)
        pc = self.per_core
        for j in range(pc):
            put(2 + j, wu[:, col(own_third * self.third_hidden + (pc * c + j) * 128)])
            start_x(2 + j)
        for j in range(pc):
            put_blocks(2 + pc + j, wd, own_third * self.third_hidden + (pc * c + j) * 128)
            start_x(2 + pc + j)

        def relay_x(i):
            wait("x", i, lx)
            remote("z", i, lx, lz).start()
            remote("cx", i, lx, sx).start()

            @pl.when(low == 0)
            def _():
                remote("y", i, lx, ly).start()

        def relay_z(i):
            wait("z", i, lz)
            remote("cz", i, lz, sz).start()

            @pl.when(low == 1)
            def _():
                remote("y", i, lz, ly).start()

        def relay_y(i):
            wait("y", i, ly)
            remote("cy", i, ly, sy).start()

        def tick(t):
            for relay, k in ((relay_x, t), (relay_z, t - self.LAG[0]), (relay_y, t - self.LAG[1])):
                if isinstance(k, int):
                    if 0 <= k < n:
                        relay(k)
                else:

                    @pl.when(jnp.logical_and(k >= 0, k < n))
                    def _():
                        relay(k)

        place_rows = lax.broadcasted_iota(jnp.int32, (rows, positions.shape[1]), 0)
        hit = jnp.where(place_rows == positions[...], 1.0, 0.0).astype(bf)
        repl_rows = lax.broadcasted_iota(jnp.int32, (swap_rows.shape[0], positions.shape[1]), 0)
        chosen = jnp.where(repl_rows == swap_ids[...], 1.0, 0.0).astype(bf)
        place = right_product(hit, chosen)
        held.place[...] = to_bf(place)
        save(held.place)
        swapped = product(held.place[...], swap_rows[...])
        is_swapped = jnp.sum(place, axis=1, keepdims=True) > 0.5
        held.inp[...] = to_bf(jnp.where(is_swapped, swapped, tokens[...].astype(F32)))
        save(held.inp)
        tick(0)
        inp = held.inp
        scale = HEAD_DIM ** (-0.5)
        qh, kh, vh, lse = held.q, held.k, held.v, held.lse
        heads = self.heads

        def project(first_head, w_q, w_k, w_v, b_ref):
            part = to_bf((product(inp[...], w_q[...]) + b_ref[0:1, :hw]) * scale)
            for h in range(heads):
                qh[first_head + h] = part[:, h * HEAD_DIM : (h + 1) * HEAD_DIM]
            part = to_bf(product(inp[...], w_k[...]))
            for h in range(heads):
                kh[first_head + h] = part[:, h * HEAD_DIM : (h + 1) * HEAD_DIM]
            part = to_bf(product(inp[...], w_v[...]) + b_ref[0:1, hw : 2 * hw])
            for h in range(heads):
                vh[first_head + h] = part[:, h * HEAD_DIM : (h + 1) * HEAD_DIM]

        key_bias = jnp.where(
            lax.broadcasted_iota(jnp.int32, (rows, 1), 0) < length[0], 0.0, mask_fill
        ).astype(F32)

        def attend(h):
            scores = right_product(kh[h], qh[h]) + key_bias
            top = jnp.max(scores, axis=0, keepdims=True)
            exponent = jnp.exp(scores - top)
            total = jnp.sum(exponent, axis=0, keepdims=True)
            lse[h] = top + jnp.log(total)
            probs = to_bf(exponent * (1.0 / total))
            return to_bf(left_product(probs, vh[h]))

        def attend_pairs(first_head, mixed_ref, t0):
            for p in range(heads // 2):
                tick(t0 + 2 * p)
                one = attend(first_head + 2 * p)
                tick(t0 + 2 * p + 1)
                two = attend(first_head + 2 * p + 1)
                mixed_ref[:, p * 128 : (p + 1) * 128] = jnp.concatenate([one, two], axis=1)

        project(0, wq, wk, wv, bias)
        tick(1)
        tick(2)
        attend_pairs(0, held.mixed, 3)
        save(held.mixed)
        acc[...] = product(held.mixed[...], wo[...])
        attn = 2 * parts
        t = 3 + heads
        while t < attn + self.LAG[1]:
            tick(t)
            t += 1
        thirds = ((own_third, lx, sx, "cx"), (z_third, lz, sz, "cz"), (y_third, ly, sy, "cy"))

        def panel_of(ref, p):
            return to_bf(ref[p * parts : (p + 1) * parts].reshape(width, 128))

        def unblock(ref, value, at):
            for b in range(width // 128):
                ref[pl.ds(pl.multiple_of(at, 128), 128), b * 128 : (b + 1) * 128] = value[
                    b * 128 : (b + 1) * 128
                ]

        for third, mine, theirs, name in thirds:
            for i in range(attn):
                wait(name, i, theirs)

            def assemble(first, second):
                held.wq[:, col(third * 128)] = panel_of(first, 0)
                held.wk[:, col(third * 128)] = panel_of(first, 1)
                held.wv[:, col(third * 128)] = panel_of(second, 0)
                unblock(held.wo, panel_of(second, 1), third * 128)

            @pl.when(c == 0)
            def _():
                assemble(mine, theirs)

            @pl.when(c == 1)
            def _():
                assemble(theirs, mine)

        save(held.wq, held.wk, held.wv, held.wo)
        pltpu.make_async_copy(bias_o, bias_o, brecv.at[0]).wait()
        tick(t)
        t += 1
        project(heads, held.wq, held.wk, held.wv, bias_o)
        mixed_o = first_out
        other_parts = []
        for p in range(heads // 2):
            tick(t)
            one = attend(heads + 2 * p)
            tick(t + 1)
            two = attend(heads + 2 * p + 1)
            t += 2
            mixed_o[:, p * 128 : (p + 1) * 128] = jnp.concatenate([one, two], axis=1).astype(F32)
        save(qh, kh, vh, lse)
        acc_o[...] = product(to_bf(mixed_o[:, :hw]), held.wo[...])
        branch = (acc[...] + acc_o[...]) + vector(0)
        first, normed, inv = layer_norm(inp[...].astype(F32) + branch, vector(1), vector(2))
        first_out[...] = first
        held.first_low[...] = to_bf(first)
        held.first_normed[...] = normed
        held.first_inv[...] = inv
        save(held.first_low, held.first_normed, held.first_inv)
        tick(t)
        t += 1
        act, slope = held.act, held.slope

        def feed(b, at, w_ref, b_ref):
            up = (
                product(held.first_low[...], w_ref[:, b * 256 : (b + 1) * 256])
                + b_ref[0:1, 2 * hw + b * 256 : 2 * hw + (b + 1) * 256]
            )
            cdf = 0.5 * (1.0 + lax.erf(up * half_root))
            slope[at] = to_bf(cdf + up * jnp.exp(-0.5 * up * up) * gauss_norm)
            return to_bf(up * cdf)

        for b in range(self.blocks):
            act[b] = feed(b, b, wu, bias)
            if b % 2 == 1:
                tick(t)
                t += 1
        save(act)
        acc[...] = product(act[0], wd[0:256])
        for b in range(1, self.blocks):
            acc[...] += product(act[b], wd[b * 256 : (b + 1) * 256])
        tick(t)
        t += 1
        while t < attn + pc * parts + self.LAG[1]:
            tick(t)
            t += 1
        for third, mine, theirs, name in thirds:
            for i in range(attn, attn + pc * parts):
                wait(name, i, theirs)
            for j in range(pc):
                at = third * self.third_hidden + (pc * c + j) * 128
                held.wu[:, col(at)] = panel_of(mine, 2 + j)
                at = third * self.third_hidden + (pc * (1 - c) + j) * 128
                held.wu[:, col(at)] = panel_of(theirs, 2 + j)
        save(held.wu)
        for b in range(self.blocks):
            tick(t)
            t += 1
            act_o[b] = feed(b, self.blocks + b, held.wu, bias_o)
        save(held.slope)
        while t < n + self.LAG[1]:
            tick(t)
            t += 1
        for third, mine, theirs, name in thirds:
            for i in range(attn + pc * parts, n):
                wait(name, i, theirs)
            for j in range(pc):
                at = third * self.third_hidden + (pc * c + j) * 128
                unblock(held.wd, panel_of(mine, 2 + pc + j), at)
                at = third * self.third_hidden + (pc * (1 - c) + j) * 128
                unblock(held.wd, panel_of(theirs, 2 + pc + j), at)
        save(held.wd)
        acc_o[...] = product(act_o[0], held.wd[0:256])
        for b in range(1, self.blocks):
            acc_o[...] += product(act_o[b], held.wd[b * 256 : (b + 1) * 256])
        down = (acc[...] + acc_o[...]) + vector(3)
        result, normed, inv = layer_norm(first_out[...] + down, vector(4), vector(5))
        held.layer[...] = to_bf(result)
        save(held.layer)
        grad_out = cot[...].astype(F32)
        grad = norm_back(grad_out, normed, inv, vector(4))
        held.grad_second[...] = grad
        save(held.grad_second)
        low_grad = to_bf(grad)
        held.grad_down[...] = low_grad
        save(held.grad_down)
        sums = held.sums
        sums[...] = jnp.zeros_like(sums)
        sums[0:1] = jnp.sum(grad_out * normed, axis=0, keepdims=True)
        sums[1:2] = jnp.sum(grad_out, axis=0, keepdims=True)
        sums[2:3] = jnp.sum(low_grad.astype(F32), axis=0, keepdims=True)
        save(held.sums)
        for name, like in (("x", xs), ("z", lx), ("y", lx), ("cx", lx), ("cz", lx), ("cy", lx)):
            pltpu.make_async_copy(like, like, sent.at[self.SENDS.index(name)]).wait()
        pltpu.make_async_copy(bias_o, bias_o, sent.at[len(self.SENDS)]).wait()
        for i in range(len(kept)):
            pltpu.make_async_copy(kept[i], kept_out[i], saved.at[i]).wait()


class Backward:
    def __init__(self, rows, width, heads_width, hidden):
        self.rows, self.width, self.heads_width, self.hidden = rows, width, heads_width, hidden
        self.heads = heads_width // HEAD_DIM
        self.blocks = hidden // 256
        self.down_at = 0
        self.up_at = self.blocks
        self.out_at = 2 * self.blocks
        self.mixed_at = self.out_at + 1
        self.value_at = self.out_at + 2
        self.first_query = self.out_at + 3
        self.pack_at = self.out_at + 4
        self.query_at = (self.first_query, self.pack_at + 1, self.pack_at + 2)
        self.ring = Ring(self.pack_at + 3, 32, width)

    def call(self, lengths, small, arrays):
        names = list(arrays)
        ring = self.ring
        r, w, hw, hid = self.rows, self.width, self.heads_width, self.hidden
        bf = jnp.bfloat16
        V = pltpu.VMEM
        scratch = [V(a.shape, a.dtype) for a in arrays.values()]
        scratch += [
            V((r, hid), bf), V((r, hid), bf), V((r, w), bf), V((2 * self.heads, r, HEAD_DIM), bf),
            V((2, 3, r, hw), bf), V((r, w), F32), V((8, hid), F32), V((8, w), F32),
            pltpu.SemaphoreType.DMA((len(names),)),
            pltpu.SemaphoreType.DMA((1,)),
            pltpu.SemaphoreType.DMA((2,)),
        ]
        n_scratch = len(scratch)
        scratch += ring.scratch()
        S = jax.ShapeDtypeStruct
        outs = (
            S((ring.n, 8, ring.e, w), F32),
            S((5, ring.e, w), F32),
            S((r, w), F32),
        )
        anywhere = pl.BlockSpec(memory_space=pl.ANY)

        def kern(length, gain_ref, *refs):
            ins = refs[: len(names)]
            out, out_x, grad_tokens = refs[len(names) : len(names) + 3]
            rest = refs[len(names) + 3 :]
            held = SimpleNamespace(**dict(zip(names, rest[: len(names)])))
            ring.bind(out, *rest[n_scratch:])
            self.body(length, gain_ref, ins, held, out, out_x, grad_tokens, *rest[len(names) : n_scratch])

        return pl.pallas_call(
            kern,
            out_shape=outs,
            in_specs=[
                pl.BlockSpec(memory_space=pltpu.SMEM),
                pl.BlockSpec(memory_space=pltpu.VMEM),
            ]
            + [anywhere] * len(names),
            out_specs=(anywhere,) * 3,
            scratch_shapes=scratch,
            name="backward_sum",
            compiler_params=pltpu.CompilerParams(
                collective_id=5, has_side_effects=True, vmem_limit_bytes=63 * 2**20
            ),
        )(lengths, small, *arrays.values())

    def body(
        self, length, gain, ins, held, out, out_x, grad_tokens,
        pre, pre_o, branch, gm, gh, work, up_sums, row_sums, loaded, saved, xsem,
    ):
        ring, rows, width, hw, hidden = self.ring, self.rows, self.width, self.heads_width, self.hidden
        heads, blocks = self.heads, self.blocks
        kept = list(vars(held).values())
        scale = HEAD_DIM ** (-0.5)
        dp, tensor = lax.axis_index("dp"), lax.axis_index("tensor")
        to_x = (dp, 1 - tensor)

        at = 2 * hw + hidden + width
        gain_row = gain[0:1, at : at + width]
        for i in range(len(kept)):
            pltpu.make_async_copy(ins[i], kept[i], loaded.at[i]).start()
        there = set()

        def need(*wanted):
            for ref in wanted:
                i = [one is ref for one in kept].index(True)
                if i not in there:
                    there.add(i)
                    pltpu.make_async_copy(ins[i], kept[i], loaded.at[i]).wait()

        def put(k, value):
            ring.g[k % ring.SLOTS] = value.reshape(8, ring.e, width)

        def put_rows(k, at, lane, value):
            count = value.shape[0] // ring.e
            ring.g[k % ring.SLOTS, at : at + count, :, lane : lane + value.shape[1]] = value.reshape(
                count, ring.e, value.shape[1]
            )

        def make_down(b):
            put(self.down_at + b, left_product(held.act[b], held.grad_down[...]))

        def make_pre(b, w_ref, at, to):
            need(held.slope, w_ref)
            lo = b * 256
            value = right_product(held.grad_down[...], w_ref[lo : lo + 256])
            to[:, lo : lo + 256] = to_bf(value * held.slope[at].astype(F32))

        def make_up(i):
            need(held.first_low)
            half, r = divmod(i, blocks // 2)
            put(
                self.up_at + i,
                left_product(held.first_low[:, r * 256 : (r + 1) * 256], pre[:, half * width : (half + 1) * width]),
            )

        def feed_back():
            need(held.grad_second, held.wu, held.wu_o)
            for b in range(blocks):
                lo = b * 256
                up_sums[0:1, lo : lo + 256] = jnp.sum(
                    pre[:, lo : lo + 256].astype(F32), axis=0, keepdims=True
                )
            grad = held.grad_second
            for lo in range(0, rows, 256):
                at = slice(lo, lo + 256)
                work[at] = right_product(pre[at], held.wu[...])
                grad[at] = grad[at] + (work[at] + right_product(pre_o[at], held.wu_o[...]))

        def norm_step():
            need(held.first_normed, held.first_inv, held.sums, held.wo, held.wo_o)
            grad, normed = held.grad_second, held.first_normed
            row_sums[3:6] = held.sums[0:3]
            total_gain = jnp.zeros((1, width), F32)
            total_shift = jnp.zeros((1, width), F32)
            total_branch = jnp.zeros((1, width), F32)
            for lo in range(0, rows, 128):
                at = slice(lo, lo + 128)
                g, n = grad[at], normed[at]
                total_gain += jnp.sum(g * n, axis=0, keepdims=True)
                total_shift += jnp.sum(g, axis=0, keepdims=True)
                resid = norm_back(g, n, held.first_inv[at], gain_row)
                grad[at] = resid
                low = to_bf(resid)
                branch[at] = low
                total_branch += jnp.sum(low.astype(F32), axis=0, keepdims=True)
            row_sums[0:1] = total_branch
            row_sums[1:2] = total_gain
            row_sums[2:3] = total_shift
            for side, w_ref in enumerate((held.wo, held.wo_o)):
                part = to_bf(right_product(branch[...], w_ref[...]))
                for h in range(heads):
                    gm[side * heads + h] = part[:, h * HEAD_DIM : (h + 1) * HEAD_DIM]

        key_bias = jnp.where(
            lax.broadcasted_iota(jnp.int32, (rows, 1), 0) < length[0], 0.0, mask_fill
        ).astype(F32)

        def head_back(h):
            q, k, v, gmix = held.q[h], held.k[h], held.v[h], gm[h]
            probs = jnp.exp(right_product(k, q) + key_bias - held.lse[h])
            grad_probs = right_product(v, gmix)
            inner = jnp.sum(probs * grad_probs, axis=0, keepdims=True)
            grad_scores = to_bf(probs * (grad_probs - inner))
            return (
                to_bf(left_product(grad_scores, k)) * scale,
                to_bf(product(grad_scores, q)),
                to_bf(product(to_bf(probs), gmix)),
            )

        def pair_back(side, p):
            need(held.q, held.k, held.v, held.lse)
            one = head_back(side * heads + 2 * p)
            two = head_back(side * heads + 2 * p + 1)
            for i in range(3):
                gh[side, i, :, p * 128 : (p + 1) * 128] = jnp.concatenate([one[i], two[i]], axis=1)

        def make_out(first, count, k, at):
            need(held.mixed)
            put_rows(k, at, 0, left_product(held.mixed[:, first : first + count], branch[...]))

        def make_value(first, count, k, at):
            need(held.inp)
            for side in range(2):
                lo = side * (width // 2) + first
                put_rows(k, at, side * hw, left_product(held.inp[:, lo : lo + count], gh[0, 2]))

        def make_query(m):
            k = self.query_at[m]
            need(held.inp)
            for i in range(2):
                put_rows(k, 0, i * hw, left_product(held.inp[:, m * 256 : (m + 1) * 256], gh[0, i]))

        def input_grad():
            need(held.wq, held.wk, held.wv, held.wq_o, held.wk_o, held.wv_o, held.place)
            grad = held.grad_second
            swapped = jnp.sum(held.place[...].astype(F32), axis=1, keepdims=True) > 0.5
            for lo in range(0, rows, 256):
                at = slice(lo, lo + 256)
                work[at] = (
                    right_product(gh[0, 0, at], held.wq[...])
                    + right_product(gh[0, 1, at], held.wk[...])
                    + right_product(gh[0, 2, at], held.wv[...])
                )
                other = (
                    right_product(gh[1, 0, at], held.wq_o[...])
                    + right_product(gh[1, 1, at], held.wk_o[...])
                    + right_product(gh[1, 2, at], held.wv_o[...])
                )
                total = grad[at] + (work[at] + other)
                grad[at] = total
                work[at] = jnp.where(swapped[at], 0.0, total)
            pltpu.make_async_copy(work, grad_tokens, saved.at[0]).start()

        def make_pack():
            k = self.pack_at
            half = width // 2
            ours = held.grad_second[:, pl.ds(pl.multiple_of(tensor * half, 128), half)]
            high = to_bf(ours)
            low = to_bf(ours - high.astype(F32))
            place = held.place
            swap = left_product(place[...], high) + left_product(place[...], low)
            repl = swap.shape[0] // 2
            put_rows(k, 0, 0, swap[:repl])
            put_rows(k, 0, half, swap[repl:])
            at = repl // ring.e
            slot = k % ring.SLOTS
            ring.g[slot, at:] = jnp.zeros((8 - at, ring.e, width), F32)
            shared = jnp.where(tensor == 0, row_sums[0:6, :half], row_sums[0:6, half:])
            ring.g[slot, at, 0:6, 0:half] = shared
            ring.g[slot, at, 0:1, half:] = jnp.sum(gh[0, 0].astype(F32), axis=0, keepdims=True)
            ring.g[slot, at, 1:2, half:] = jnp.sum(gh[0, 2].astype(F32), axis=0, keepdims=True)
            for i in range(hidden // half):
                ring.g[slot, at, 2 + i : 3 + i, half:] = up_sums[0:1, i * half : (i + 1) * half]

        need(held.grad_down, held.act)
        make_down(0)
        ring.barrier([to_x])
        n = ring.n
        work_of = {}

        def plan(t, *jobs):
            work_of.setdefault(t, []).extend(jobs)

        for b in range(1, blocks):
            plan(b - 1, lambda b=b: make_down(b))
        for b in range(blocks):
            plan(b // 2, lambda b=b: make_pre(b, held.wd, b, pre))
            plan(3 + b // 3, lambda b=b: make_pre(b, held.wd_o, blocks + b, pre_o))
        for i in range(blocks):
            plan(self.up_at - 1 + i, lambda i=i: make_up(i))
        plan(5, feed_back)
        plan(6, norm_step)
        for side in range(2):
            for p in range(heads // 2):
                plan(7 + side * (heads // 2) + p, lambda side=side, p=p: pair_back(side, p))
        first_rows = 256
        left = hw - first_rows
        plan(self.out_at - 1, lambda: make_out(0, first_rows, self.out_at, 0))
        plan(self.mixed_at - 1, lambda: make_out(first_rows, left, self.mixed_at, 0))
        plan(self.mixed_at - 1, lambda: make_value(0, 256 - left, self.mixed_at, left // ring.e))
        plan(self.value_at - 1, lambda: make_value(256 - left, 256, self.value_at, 0))
        plan(self.value_at - 1, input_grad)
        for m in range(3):
            plan(self.query_at[m] - 1, lambda m=m: make_query(m))
        plan(self.pack_at - 1, make_pack)
        last = max(work_of) + 1
        for t in range(last):
            ring.tick(t)
            for job in work_of.get(t, ()):
                job()
        exchange = pltpu.make_async_remote_copy(
            out.at[self.pack_at, 0:5], out_x, xsem.at[0], xsem.at[1], device_id=to_x, device_id_type=MESH
        )
        sent_at = self.pack_at + ring.STAGES - 1

        def rest(t, carry):
            ring.tick(t)

            @pl.when(t == sent_at)
            def _():
                exchange.start()

            return carry

        lax.fori_loop(last, n + ring.STAGES - 1, rest, 0)
        exchange.wait()
        pltpu.make_async_copy(work, grad_tokens, saved.at[0]).wait()


def unpack(packed, rows, width, hw, hidden):
    back = Backward(rows, width, hw, hidden)
    blocks = back.blocks
    S = jax.ShapeDtypeStruct
    outs = (
        S((hidden, width), F32), S((width, hidden), F32), S((hw, width), F32),
        S((width, hw), F32), S((width, hw), F32), S((width, hw), F32),
    )
    left = hw - 256
    half = width // 2

    def kern(packed_ref, wd, wu, wo, wq, wk, wv, src, sem_in, sem):
        moves = []
        for b in range(blocks):
            moves.append((b, src.at[b], wd.at[b * 256 : (b + 1) * 256]))
        for b in range(blocks):
            side, r = divmod(b, blocks // 2)
            k = back.up_at + b
            moves.append(
                (k, src.at[k], wu.at[r * 256 : (r + 1) * 256, side * width : (side + 1) * width])
            )
        moves.append((back.out_at, src.at[back.out_at], wo.at[0:256]))
        k = back.mixed_at
        moves.append((k, src.at[k, 0:left], wo.at[256:hw]))
        for side in range(2):
            lo = side * half
            lanes = slice(side * hw, (side + 1) * hw)
            moves.append((k, src.at[k, left:256, lanes], wv.at[lo : lo + 256 - left]))
        k = back.value_at
        for side in range(2):
            lo = side * half
            lanes = slice(side * hw, (side + 1) * hw)
            moves.append((k, src.at[k, :, lanes], wv.at[lo + 256 - left : lo + half]))
        for m, k in enumerate(back.query_at):
            for i, to in enumerate((wq, wk)):
                lanes = slice(i * hw, (i + 1) * hw)
                moves.append((k, src.at[k, :, lanes], to.at[m * 256 : (m + 1) * 256]))
        used = []
        for k, _, _ in moves:
            if k not in used:
                used.append(k)
        for k in used:
            pltpu.make_async_copy(packed_ref.at[k], src.at[k], sem_in.at[k]).start()
        arrived = set()
        copies = []
        for i, (k, a, b) in enumerate(moves):
            if k not in arrived:
                arrived.add(k)
                pltpu.make_async_copy(packed_ref.at[k], src.at[k], sem_in.at[k]).wait()
            copy = pltpu.make_async_copy(a, b, sem.at[i])
            copy.start()
            copies.append(copy)
        for copy in copies:
            copy.wait()

    anywhere = pl.BlockSpec(memory_space=pl.ANY)
    return pl.pallas_call(
        kern,
        out_shape=outs,
        in_specs=[anywhere],
        out_specs=(anywhere,) * 6,
        scratch_shapes=[
            pltpu.VMEM(packed.shape, F32),
            pltpu.SemaphoreType.DMA((packed.shape[0],)),
            pltpu.SemaphoreType.DMA((2 * blocks + 12,)),
        ],
        name="unpack",
        compiler_params=pltpu.CompilerParams(vmem_limit_bytes=60 * 2**20),
    )(packed)


def local(
    tokens,
    lengths,
    positions,
    swap_ids,
    swap_rows,
    w_query,
    b_query,
    w_key,
    w_value,
    b_value,
    w_out,
    b_out,
    first_gain,
    first_shift,
    w_up,
    b_up,
    w_down,
    b_down,
    second_gain,
    second_shift,
    cotangent,
    dp_count,
):
    row_count, model_width = tokens.shape
    heads_width = w_query.shape[1]
    hidden = w_up.shape[1]
    half = model_width // 2
    small = jnp.concatenate(
        [b_query, b_value, b_up, b_out, first_gain, first_shift, b_down, second_gain, second_shift]
    ).astype(F32)
    small = jnp.broadcast_to(small[None, :], (8, small.shape[0]))
    fw = Forward(row_count, model_width, heads_width, hidden).call(
        lengths, tokens, positions, swap_ids, swap_rows, w_query, w_key, w_value, w_out, w_up, w_down,
        small, cotangent,
    )
    result = fw.layer
    arrays = dict(
        grad_down=fw.grad_down, act=fw.act, wd=w_down, slope=fw.slope, wd_o=fw.wd, grad_second=fw.grad_second,
        wu=w_up, wu_o=fw.wu, first_low=fw.first_low, first_normed=fw.first_normed, first_inv=fw.first_inv,
        sums=fw.sums, wo=w_out, wo_o=fw.wo, q=fw.q, k=fw.k, v=fw.v, lse=fw.lse, mixed=fw.mixed, inp=fw.inp,
        wq=w_query, wk=w_key, wv=w_value, wq_o=fw.wq, wk_o=fw.wk, wv_o=fw.wv, place=fw.place,
    )
    back = Backward(row_count, model_width, heads_width, hidden)
    summed, summed_x, grad_tokens = back.call(lengths, small, arrays)
    if dp_count > 16:
        groups = [list(range(i, dp_count, 16)) for i in range(16)]
        summed, summed_x = lax.psum((summed, summed_x), "dp", axis_index_groups=groups)
    packed = summed.reshape(summed.shape[0], 256, model_width)
    sum_down, sum_up, sum_out, sum_query, sum_key, sum_value = unpack(
        packed, row_count, model_width, heads_width, hidden
    )
    tensor = lax.axis_index("tensor")
    ours = packed[back.pack_at]
    theirs = summed_x.reshape(-1, model_width)
    repl = swap_rows.shape[0] // 2

    def sides(part):
        return jnp.concatenate([part[:repl, :half], part[:repl, half:], part[repl : repl + 8, :half]], axis=0)

    ours_part, theirs_part = sides(ours), sides(theirs)
    left = jnp.where(tensor == 0, ours_part, theirs_part)
    right = jnp.where(tensor == 0, theirs_part, ours_part)
    whole = jnp.concatenate([left, right], axis=1)
    repl = 2 * repl
    private = ours[repl // 2 : repl // 2 + 8, half:]
    return (
        result,
        grad_tokens,
        whole[:repl],
        sum_query,
        private[0],
        sum_key,
        sum_value,
        private[1],
        sum_out,
        whole[repl],
        whole[repl + 1],
        whole[repl + 2],
        sum_up,
        private[2:6].reshape(-1),
        sum_down,
        whole[repl + 5],
        whole[repl + 3],
        whole[repl + 4],
    )


def solution(mesh):
    in_specs = (
        P("dp", None),
        P("dp"),
        P("dp", None),
        P("dp", None),
        P(),
        P(None, "tensor"),
        P("tensor"),
        P(None, "tensor"),
        P(None, "tensor"),
        P("tensor"),
        P("tensor", None),
        P(),
        P(),
        P(),
        P(None, "tensor"),
        P("tensor"),
        P("tensor", None),
        P(),
        P(),
        P(),
        P("dp", None),
    )
    out_specs = (
        P("dp", None),
        P("dp", None),
        P(),
        P(None, "tensor"),
        P("tensor"),
        P(None, "tensor"),
        P(None, "tensor"),
        P("tensor"),
        P("tensor", None),
        P(),
        P(),
        P(),
        P(None, "tensor"),
        P("tensor"),
        P("tensor", None),
        P(),
        P(),
        P(),
    )
    count = mesh.shape["dp"]

    def run(*arrays):
        return local(*arrays, dp_count=count)

    return jax.shard_map(run, mesh=mesh, in_specs=in_specs, out_specs=out_specs, check_vma=False)
```

```python
from types import SimpleNamespace

import jax
import jax.numpy as jnp
from jax import lax
from jax.experimental import pallas as pl
from jax.experimental.pallas import tpu as pltpu
from jax.sharding import PartitionSpec as P

F32 = jnp.float32
MESH = pl.DeviceIdType.MESH

HEAD_DIM = 64


norm_eps = 1e-12
mask_fill = -1000000000.0
half_root = 0.7071067811865476
gauss_norm = 0.3989422804014327


def to_bf(value):
    return value.astype(jnp.bfloat16)


def product(left, right):
    return jnp.dot(left, right, preferred_element_type=jnp.float32)


def left_product(left, right):
    return lax.dot_general(
        left, right, (((0,), (0,)), ((), ())), preferred_element_type=jnp.float32
    )


def right_product(left, right):
    return lax.dot_general(
        left, right, (((1,), (1,)), ((), ())), preferred_element_type=jnp.float32
    )


def layer_norm(hidden, norm_gain, norm_shift):
    row_mean = jnp.mean(hidden, axis=-1, keepdims=True)
    centred = hidden - row_mean
    inv_std = lax.rsqrt(jnp.mean(centred * centred, axis=-1, keepdims=True) + norm_eps)
    normed = centred * inv_std
    return (normed * norm_gain + norm_shift, normed, inv_std)


def norm_back(upstream, normed, inv_std, norm_gain):
    scaled = upstream * norm_gain
    return inv_std * (
        scaled
        - jnp.mean(scaled, axis=-1, keepdims=True)
        - normed * jnp.mean(scaled * normed, axis=-1, keepdims=True)
    )


class Ring:
    RECV = ("rc", "rya", "rzb", "rza", "rma", "rmb", "ryb", "zoa", "yoa", "mob", "zob", "zoc", "co", "la", "lb")
    SLOTS = 8
    STAGES = 8

    def __init__(self, chunks, eighth, width):
        self.n, self.e, self.w = chunks, eighth, width

    def scratch(self):
        def buffer(*lead):
            return pltpu.VMEM((self.SLOTS,) + lead + (self.e, self.w), F32)

        bufs = [buffer(8), buffer(4), buffer(), buffer(2), buffer(), buffer(), buffer(), buffer()]
        sems = pltpu.SemaphoreType.DMA((len(self.RECV), self.SLOTS))
        return bufs + [sems, sems]

    def bind(self, out, g, rc, rya, rzb, rza, rma, rmb, ryb, recv, sent):
        self.out, self.g, self.rc, self.rya, self.rzb = out, g, rc, rya, rzb
        self.rza, self.rma, self.rmb, self.ryb = rza, rma, rmb, ryb
        self.recv, self.sent = recv, sent
        dp = lax.axis_index("dp")
        self.t = lax.axis_index("tensor")
        self.c, self.y, self.z = dp % 2, (dp // 2) % 2, (dp // 4) % 4
        self.inner = ((self.z + 1) // 2) == 1
        self.outer = jnp.logical_not(self.inner)
        self.s = self.z // 2
        self.to_c = dp + 1 - 2 * self.c
        self.to_y = dp + 2 * (1 - 2 * self.y)
        self.to_z = dp + 4 * (1 - 2 * (self.z % 2))
        self.to_m = dp + 4 * (3 - 2 * self.z)

    def slot(self, k):
        return k % self.SLOTS

    def remote(self, name, k, src, dst, to):
        i, j = self.RECV.index(name), self.slot(k)
        return pltpu.make_async_remote_copy(
            src, dst, self.sent.at[i, j], self.recv.at[i, j], device_id=(to, self.t), device_id_type=MESH
        )

    def wait(self, name, k, like):
        pltpu.make_async_copy(like, like, self.recv.at[self.RECV.index(name), self.slot(k)]).wait()

    def gone(self, name, k, like):
        pltpu.make_async_copy(like, like, self.sent.at[self.RECV.index(name), self.slot(k)]).wait()

    def local(self, name, k, src, dst):
        return pltpu.make_async_copy(src, dst, self.recv.at[self.RECV.index(name), self.slot(k)])

    def greet(self, more):
        bar = pltpu.get_barrier_semaphore()

        def signal(to):
            pl.semaphore_signal(bar, inc=1, device_id=to, device_id_type=MESH)

        for place in (self.to_c, self.to_y, self.to_z):
            signal((place, self.t))
        for to in more:
            signal(to)

        @pl.when(self.inner)
        def _():
            signal((self.to_m, self.t))

    def await_partners(self, more):
        bar = pltpu.get_barrier_semaphore()

        @pl.when(self.inner)
        def _():
            pl.semaphore_wait(bar, 4 + len(more))

        @pl.when(self.outer)
        def _():
            pl.semaphore_wait(bar, 3 + len(more))

    def half(self, k):
        return self.out.at[k, pl.ds(self.c * 4, 4)]

    def oa(self, k, y):
        return self.out.at[k, self.c * 4 + y]

    def ob(self, k, s):
        return self.out.at[k, self.c * 4 + 2 + s]

    def stage0(self, k):
        j = self.slot(k)
        self.remote("rc", k, self.g.at[j, pl.ds((1 - self.c) * 4, 4)], self.rc.at[j], self.to_c).start()

    def stage1(self, k):
        g, c, j = self.g, self.c, self.slot(k)
        self.wait("rc", k, self.rc.at[j])
        for i in range(4):
            g[j, c * 4 + i] = g[j, c * 4 + i] + self.rc[j, i]
        self.remote("rya", k, g.at[j, c * 4 + 1 - self.y], self.rya.at[j], self.to_y).start()

        @pl.when(self.outer)
        def _():
            self.remote("rzb", k, g.at[j, pl.ds(c * 4 + 2, 2)], self.rzb.at[j], self.to_z).start()

    def stage2(self, k):
        g, c, y, s, j = self.g, self.c, self.y, self.s, self.slot(k)
        self.wait("rya", k, self.rya.at[j])
        g[j, c * 4 + y] = g[j, c * 4 + y] + self.rya[j]

        @pl.when(self.outer)
        def _():
            self.remote("rza", k, g.at[j, c * 4 + y], self.rza.at[j], self.to_z).start()

        @pl.when(self.inner)
        def _():
            self.wait("rzb", k, self.rzb.at[j])
            for i in range(2):
                g[j, c * 4 + 2 + i] = g[j, c * 4 + 2 + i] + self.rzb[j, i]
            self.remote("rmb", k, g.at[j, c * 4 + 2 + 1 - s], self.rmb.at[j], self.to_m).start()

    def stage3(self, k):
        g, c, y, s, j = self.g, self.c, self.y, self.s, self.slot(k)

        @pl.when(self.inner)
        def _():
            self.wait("rza", k, self.rza.at[j])
            g[j, c * 4 + y] = g[j, c * 4 + y] + self.rza[j]
            self.remote("rma", k, g.at[j, c * 4 + y], self.rma.at[j], self.to_m).start()
            self.wait("rmb", k, self.rmb.at[j])
            g[j, c * 4 + 2 + s] = g[j, c * 4 + 2 + s] + self.rmb[j]
            self.remote("ryb", k, g.at[j, c * 4 + 2 + s], self.ryb.at[j], self.to_y).start()

    def stage4(self, k):
        g, c, y, s, j = self.g, self.c, self.y, self.s, self.slot(k)

        @pl.when(self.inner)
        def _():
            self.wait("rma", k, self.rma.at[j])
            self.rma[j] = self.rma[j] + g[j, c * 4 + y]
            self.remote("zoa", k, self.rma.at[j], self.oa(k, y), self.to_z).start()
            self.remote("yoa", k, self.rma.at[j], self.oa(k, y), self.to_y).start()
            self.local("la", k, self.rma.at[j], self.oa(k, y)).start()
            self.wait("ryb", k, self.ryb.at[j])
            self.ryb[j] = self.ryb[j] + g[j, c * 4 + 2 + s]
            self.remote("mob", k, self.ryb.at[j], self.ob(k, s), self.to_m).start()
            self.remote("zob", k, self.ryb.at[j], self.ob(k, s), self.to_z).start()
            self.local("lb", k, self.ryb.at[j], self.ob(k, s)).start()

    def stage5(self, k):
        y, s = self.y, self.s

        @pl.when(self.outer)
        def _():
            self.wait("zoa", k, self.oa(k, y))
            self.remote("yoa", k, self.oa(k, y), self.oa(k, y), self.to_y).start()

        @pl.when(self.inner)
        def _():
            self.wait("mob", k, self.ob(k, 1 - s))
            self.remote("zoc", k, self.ob(k, 1 - s), self.ob(k, 1 - s), self.to_z).start()

    def stage6(self, k):
        y, s = self.y, self.s
        self.wait("yoa", k, self.oa(k, 1 - y))

        @pl.when(self.inner)
        def _():
            self.wait("la", k, self.oa(k, y))
            self.wait("lb", k, self.ob(k, s))

        @pl.when(self.outer)
        def _():
            self.wait("zob", k, self.ob(k, s))
            self.wait("zoc", k, self.ob(k, 1 - s))

        self.remote("co", k, self.half(k), self.half(k), self.to_c).start()

    def stage7(self, k):
        j = self.slot(k)
        self.wait("co", k, self.half(k))
        self.gone("rc", k, self.rc.at[j])
        self.gone("co", k, self.rc.at[j])
        self.gone("rya", k, self.rya.at[j])
        self.gone("yoa", k, self.rya.at[j])

        @pl.when(self.inner)
        def _():
            for name in ("rmb", "rma", "ryb", "zoa", "mob", "zob", "zoc"):
                self.gone(name, k, self.rya.at[j])

        @pl.when(self.outer)
        def _():
            self.gone("rzb", k, self.rzb.at[j])
            self.gone("rza", k, self.rza.at[j])

    def tick(self, t):
        stages = (
            self.stage0, self.stage1, self.stage2, self.stage3,
            self.stage4, self.stage5, self.stage6, self.stage7,
        )
        for i in range(self.STAGES - 1, -1, -1):
            k = t - i
            if isinstance(k, int):
                if 0 <= k < self.n:
                    stages[i](k)
            else:

                @pl.when(jnp.logical_and(k >= 0, k < self.n))
                def _():
                    stages[i](k)


class Forward:
    PARTS = 4
    LAG = (2, 4)
    SENDS = ("x", "z", "y", "cx", "cz", "cy")

    def __init__(self, rows, width, heads_width, hidden):
        self.rows, self.width, self.heads_width, self.hidden = rows, width, heads_width, hidden
        self.heads = heads_width // HEAD_DIM
        self.third_hidden = hidden // 3
        self.blocks = hidden // 256
        self.per_core = self.third_hidden // 256
        self.panels = 2 + 2 * self.per_core
        self.chunks = self.panels * self.PARTS
        self.part_rows = width // self.PARTS

    def outs(self):
        r, w, hw, hid = self.rows, self.width, self.heads_width, self.hidden
        bf = jnp.bfloat16
        S = jax.ShapeDtypeStruct
        return dict(
            layer=S((r, w), bf),
            wq=S((w, hw), bf), wk=S((w, hw), bf), wv=S((w, hw), bf), wo=S((hw, w), bf),
            wu=S((w, hid), bf), wd=S((hid, w), bf),
            inp=S((r, w), bf), place=S((r, 256), bf),
            q=S((2 * self.heads, r, HEAD_DIM), bf), k=S((2 * self.heads, r, HEAD_DIM), bf),
            v=S((2 * self.heads, r, HEAD_DIM), bf), lse=S((2 * self.heads, 1, r), F32),
            mixed=S((r, hw), bf),
            first_low=S((r, w), bf), first_normed=S((r, w), F32), first_inv=S((r, 1), F32),
            act=S((self.blocks, r, 256), bf), slope=S((2 * self.blocks, r, 256), bf),
            grad_second=S((r, w), F32), grad_down=S((r, w), bf), sums=S((8, w), F32),
        )

    def call(self, *args):
        outs = self.outs()
        names = list(outs)
        n = self.chunks
        panel = pltpu.VMEM((n, self.part_rows, 128), F32)
        scratch = [pltpu.VMEM(o.shape, o.dtype) for o in outs.values()]
        scratch += [panel] * 7
        scratch += [
            pltpu.VMEM((8, 2 * self.heads_width + self.hidden), F32),
            pltpu.VMEM((self.rows, self.width), F32),
            pltpu.VMEM((self.rows, self.width), F32),
            pltpu.VMEM((self.rows, self.width), F32),
            pltpu.VMEM((self.blocks, self.rows, 256), jnp.bfloat16),
            pltpu.SemaphoreType.DMA((len(self.SENDS), n)),
            pltpu.SemaphoreType.DMA((len(self.SENDS) + 1,)),
            pltpu.SemaphoreType.DMA((1,)),
            pltpu.SemaphoreType.DMA((len(names),)),
        ]
        late = args[5:12]
        scratch += [pltpu.VMEM(a.shape, a.dtype) for a in late]
        scratch.append(pltpu.SemaphoreType.DMA((len(late),)))
        vm = pl.BlockSpec(memory_space=pltpu.VMEM)
        specs = [pl.BlockSpec(memory_space=pltpu.SMEM)] + [vm] * (len(args) - 1)
        specs[5:12] = [pl.BlockSpec(memory_space=pl.ANY)] * len(late)

        def kern(*refs):
            ins = refs[: len(args)]
            out_refs = SimpleNamespace(**dict(zip(names, refs[len(args) : len(args) + len(names)])))
            rest = refs[len(args) + len(names) :]
            held = SimpleNamespace(**dict(zip(names, rest[: len(names)])))
            self.body(ins, out_refs, held, *rest[len(names) :])

        got = pl.pallas_call(
            kern,
            out_shape=tuple(outs.values()),
            in_specs=specs,
            out_specs=tuple(pl.BlockSpec(memory_space=pl.ANY) for _ in names),
            scratch_shapes=scratch,
            name="forward_gather",
            compiler_params=pltpu.CompilerParams(
                collective_id=4, has_side_effects=True, vmem_limit_bytes=62 * 2**20
            ),
        )(*args)
        return SimpleNamespace(**dict(zip(names, got)))

    def body(self, ins, out_refs, held, xs, lx, lz, ly, sx, sz, sy, bias_o, acc, acc_o, first_out, act_o, recv, sent, brecv, saved, *fetched):
        (length, tokens, positions, swap_ids, swap_rows) = ins[:5]
        far, small = ins[5:12], ins[12]
        *near, fetch_sems = fetched
        fetches = [pltpu.make_async_copy(a, b, fetch_sems.at[i]) for i, (a, b) in enumerate(zip(far, near))]
        for fetch in fetches:
            fetch.start()
        (wq, wk, wv, wo, wu, wd, cot) = near
        rows, width, hw, hidden = self.rows, self.width, self.heads_width, self.hidden

        bias = small.at[:, 0 : 2 * hw + hidden]

        def vector(i):
            at = 2 * hw + hidden + i * width
            return small[0:1, at : at + width]

        n, parts, part_rows = self.chunks, self.PARTS, self.part_rows
        bf = jnp.bfloat16
        dp = lax.axis_index("dp")
        tensor = lax.axis_index("tensor")
        c, y, low = dp % 2, (dp // 2) % 2, (dp // 4) % 2

        def flip(unit, bit):
            return dp + unit * (1 - 2 * bit)

        to = {"x": (dp, 1 - tensor), "z": (flip(4, low), tensor), "y": (flip(2, y), tensor)}
        to["cx"] = to["cz"] = to["cy"] = (flip(1, c), tensor)
        own_third = jnp.where(low == 0, y, 2)
        z_third = jnp.where(low == 0, 2, y)
        y_third = 1 - y

        def remote(name, i, src, dst):
            s = self.SENDS.index(name)
            return pltpu.make_async_remote_copy(
                src.at[i], dst.at[i], sent.at[s], recv.at[s, i], device_id=to[name], device_id_type=MESH
            )

        def wait(name, i, dst):
            pltpu.make_async_copy(dst.at[i], dst.at[i], recv.at[self.SENDS.index(name), i]).wait()

        kept = list(vars(held).values())
        kept_out = list(vars(out_refs).values())

        def save(*refs):
            for ref in refs:
                i = [one is ref for one in kept].index(True)
                pltpu.make_async_copy(ref, kept_out[i], saved.at[i]).start()

        bar = pltpu.get_barrier_semaphore()
        for name in ("x", "z", "y", "cx"):
            pl.semaphore_signal(bar, inc=1, device_id=to[name], device_id_type=MESH)

        def put(p, value):
            xs[p * parts : (p + 1) * parts] = value.astype(F32).reshape(parts, part_rows, 128)

        def put_blocks(p, ref, at):
            for b in range(width // 128):
                lo = b * 128
                block = ref[pl.ds(pl.multiple_of(at, 128), 128), lo : lo + 128].astype(F32)
                done = 0
                while done < 128:
                    i, r = divmod(lo + done, part_rows)
                    take = min(128 - done, part_rows - r)
                    xs[p * parts + i, r : r + take] = block[done : done + take]
                    done += take

        def start_x(p):
            for i in range(p * parts, (p + 1) * parts):
                remote("x", i, xs, lx).start()

        def col(at):
            return pl.ds(pl.multiple_of(at, 128), 128)

        at = own_third * 128
        for fetch in fetches[:4]:
            fetch.wait()

        @pl.when(c == 0)
        def _():
            put(0, wq[:, col(at)])
            put(1, wk[:, col(at)])

        @pl.when(c == 1)
        def _():
            put(0, wv[:, col(at)])
            put_blocks(1, wo, at)

        pl.semaphore_wait(bar, 4)
        pltpu.make_async_remote_copy(
            bias, bias_o, sent.at[len(self.SENDS)], brecv.at[0], device_id=to["x"], device_id_type=MESH
        ).start()
        start_x(0)
        start_x(1)
        pc = self.per_core
        fetches[4].wait()
        for j in range(pc):
            put(2 + j, wu[:, col(own_third * self.third_hidden + (pc * c + j) * 128)])
            start_x(2 + j)
        fetches[5].wait()
        for j in range(pc):
            put_blocks(2 + pc + j, wd, own_third * self.third_hidden + (pc * c + j) * 128)
            start_x(2 + pc + j)

        def relay_x(i):
            wait("x", i, lx)
            remote("z", i, lx, lz).start()
            remote("cx", i, lx, sx).start()

            @pl.when(low == 0)
            def _():
                remote("y", i, lx, ly).start()

        def relay_z(i):
            wait("z", i, lz)
            remote("cz", i, lz, sz).start()

            @pl.when(low == 1)
            def _():
                remote("y", i, lz, ly).start()

        def relay_y(i):
            wait("y", i, ly)
            remote("cy", i, ly, sy).start()

        def tick(t):
            for relay, k in ((relay_x, t), (relay_z, t - self.LAG[0]), (relay_y, t - self.LAG[1])):
                if isinstance(k, int):
                    if 0 <= k < n:
                        relay(k)
                else:

                    @pl.when(jnp.logical_and(k >= 0, k < n))
                    def _():
                        relay(k)

        place_rows = lax.broadcasted_iota(jnp.int32, (rows, positions.shape[1]), 0)
        hit = jnp.where(place_rows == positions[...], 1.0, 0.0).astype(bf)
        repl_rows = lax.broadcasted_iota(jnp.int32, (swap_rows.shape[0], positions.shape[1]), 0)
        chosen = jnp.where(repl_rows == swap_ids[...], 1.0, 0.0).astype(bf)
        place = right_product(hit, chosen)
        held.place[...] = to_bf(place)
        save(held.place)
        swapped = product(held.place[...], swap_rows[...])
        is_swapped = jnp.sum(place, axis=1, keepdims=True) > 0.5
        held.inp[...] = to_bf(jnp.where(is_swapped, swapped, tokens[...].astype(F32)))
        save(held.inp)
        tick(0)
        inp = held.inp
        scale = HEAD_DIM ** (-0.5)
        qh, kh, vh, lse = held.q, held.k, held.v, held.lse
        heads = self.heads

        def project(first_head, w_q, w_k, w_v, b_ref):
            part = to_bf((product(inp[...], w_q[...]) + b_ref[0:1, :hw]) * scale)
            for h in range(heads):
                qh[first_head + h] = part[:, h * HEAD_DIM : (h + 1) * HEAD_DIM]
            part = to_bf(product(inp[...], w_k[...]))
            for h in range(heads):
                kh[first_head + h] = part[:, h * HEAD_DIM : (h + 1) * HEAD_DIM]
            part = to_bf(product(inp[...], w_v[...]) + b_ref[0:1, hw : 2 * hw])
            for h in range(heads):
                vh[first_head + h] = part[:, h * HEAD_DIM : (h + 1) * HEAD_DIM]

        key_bias = jnp.where(
            lax.broadcasted_iota(jnp.int32, (rows, 1), 0) < length[0], 0.0, mask_fill
        ).astype(F32)

        def attend(h):
            scores = right_product(kh[h], qh[h]) + key_bias
            top = jnp.max(scores, axis=0, keepdims=True)
            exponent = jnp.exp(scores - top)
            total = jnp.sum(exponent, axis=0, keepdims=True)
            lse[h] = top + jnp.log(total)
            probs = to_bf(exponent * (1.0 / total))
            return to_bf(left_product(probs, vh[h]))

        def attend_pairs(first_head, mixed_ref, t0):
            for p in range(heads // 2):
                tick(t0 + 2 * p)
                one = attend(first_head + 2 * p)
                tick(t0 + 2 * p + 1)
                two = attend(first_head + 2 * p + 1)
                mixed_ref[:, p * 128 : (p + 1) * 128] = jnp.concatenate([one, two], axis=1)

        project(0, wq, wk, wv, bias)
        tick(1)
        tick(2)
        attend_pairs(0, held.mixed, 3)
        save(held.mixed)
        acc[...] = product(held.mixed[...], wo[...])
        attn = 2 * parts
        t = 3 + heads
        while t < attn + self.LAG[1]:
            tick(t)
            t += 1
        thirds = ((own_third, lx, sx, "cx"), (z_third, lz, sz, "cz"), (y_third, ly, sy, "cy"))

        def panel_of(ref, p):
            return to_bf(ref[p * parts : (p + 1) * parts].reshape(width, 128))

        def unblock(ref, value, at):
            for b in range(width // 128):
                ref[pl.ds(pl.multiple_of(at, 128), 128), b * 128 : (b + 1) * 128] = value[
                    b * 128 : (b + 1) * 128
                ]

        for third, mine, theirs, name in thirds:
            for i in range(attn):
                wait(name, i, theirs)

            def assemble(first, second):
                held.wq[:, col(third * 128)] = panel_of(first, 0)
                held.wk[:, col(third * 128)] = panel_of(first, 1)
                held.wv[:, col(third * 128)] = panel_of(second, 0)
                unblock(held.wo, panel_of(second, 1), third * 128)

            @pl.when(c == 0)
            def _():
                assemble(mine, theirs)

            @pl.when(c == 1)
            def _():
                assemble(theirs, mine)

        save(held.wq, held.wk, held.wv, held.wo)
        pltpu.make_async_copy(bias_o, bias_o, brecv.at[0]).wait()
        tick(t)
        t += 1
        project(heads, held.wq, held.wk, held.wv, bias_o)
        mixed_o = first_out
        other_parts = []
        for p in range(heads // 2):
            tick(t)
            one = attend(heads + 2 * p)
            tick(t + 1)
            two = attend(heads + 2 * p + 1)
            t += 2
            mixed_o[:, p * 128 : (p + 1) * 128] = jnp.concatenate([one, two], axis=1).astype(F32)
        save(qh, kh, vh, lse)
        acc_o[...] = product(to_bf(mixed_o[:, :hw]), held.wo[...])
        branch = (acc[...] + acc_o[...]) + vector(0)
        first, normed, inv = layer_norm(inp[...].astype(F32) + branch, vector(1), vector(2))
        first_out[...] = first
        held.first_low[...] = to_bf(first)
        held.first_normed[...] = normed
        held.first_inv[...] = inv
        save(held.first_low, held.first_normed, held.first_inv)
        tick(t)
        t += 1
        act, slope = held.act, held.slope

        def feed(b, at, w_ref, b_ref):
            up = (
                product(held.first_low[...], w_ref[:, b * 256 : (b + 1) * 256])
                + b_ref[0:1, 2 * hw + b * 256 : 2 * hw + (b + 1) * 256]
            )
            cdf = 0.5 * (1.0 + lax.erf(up * half_root))
            slope[at] = to_bf(cdf + up * jnp.exp(-0.5 * up * up) * gauss_norm)
            return to_bf(up * cdf)

        for b in range(self.blocks):
            act[b] = feed(b, b, wu, bias)
            if b % 2 == 1:
                tick(t)
                t += 1
        save(act)
        acc[...] = product(act[0], wd[0:256])
        for b in range(1, self.blocks):
            acc[...] += product(act[b], wd[b * 256 : (b + 1) * 256])
        tick(t)
        t += 1
        while t < attn + pc * parts + self.LAG[1]:
            tick(t)
            t += 1
        for third, mine, theirs, name in thirds:
            for i in range(attn, attn + pc * parts):
                wait(name, i, theirs)
            for j in range(pc):
                at = third * self.third_hidden + (pc * c + j) * 128
                held.wu[:, col(at)] = panel_of(mine, 2 + j)
                at = third * self.third_hidden + (pc * (1 - c) + j) * 128
                held.wu[:, col(at)] = panel_of(theirs, 2 + j)
        save(held.wu)
        for b in range(self.blocks):
            tick(t)
            t += 1
            act_o[b] = feed(b, self.blocks + b, held.wu, bias_o)
        save(held.slope)
        while t < n + self.LAG[1]:
            tick(t)
            t += 1
        for third, mine, theirs, name in thirds:
            for i in range(attn + pc * parts, n):
                wait(name, i, theirs)
            for j in range(pc):
                at = third * self.third_hidden + (pc * c + j) * 128
                unblock(held.wd, panel_of(mine, 2 + pc + j), at)
                at = third * self.third_hidden + (pc * (1 - c) + j) * 128
                unblock(held.wd, panel_of(theirs, 2 + pc + j), at)
        save(held.wd)
        acc_o[...] = product(act_o[0], held.wd[0:256])
        for b in range(1, self.blocks):
            acc_o[...] += product(act_o[b], held.wd[b * 256 : (b + 1) * 256])
        down = (acc[...] + acc_o[...]) + vector(3)
        result, normed, inv = layer_norm(first_out[...] + down, vector(4), vector(5))
        held.layer[...] = to_bf(result)
        save(held.layer)
        fetches[6].wait()
        grad_out = cot[...].astype(F32)
        grad = norm_back(grad_out, normed, inv, vector(4))
        held.grad_second[...] = grad
        save(held.grad_second)
        low_grad = to_bf(grad)
        held.grad_down[...] = low_grad
        save(held.grad_down)
        sums = held.sums
        sums[...] = jnp.zeros_like(sums)
        sums[0:1] = jnp.sum(grad_out * normed, axis=0, keepdims=True)
        sums[1:2] = jnp.sum(grad_out, axis=0, keepdims=True)
        sums[2:3] = jnp.sum(low_grad.astype(F32), axis=0, keepdims=True)
        save(held.sums)
        for name, like in (("x", xs), ("z", lx), ("y", lx), ("cx", lx), ("cz", lx), ("cy", lx)):
            pltpu.make_async_copy(like, like, sent.at[self.SENDS.index(name)]).wait()
        pltpu.make_async_copy(bias_o, bias_o, sent.at[len(self.SENDS)]).wait()
        for i in range(len(kept)):
            pltpu.make_async_copy(kept[i], kept_out[i], saved.at[i]).wait()


class Backward:
    def __init__(self, rows, width, heads_width, hidden):
        self.rows, self.width, self.heads_width, self.hidden = rows, width, heads_width, hidden
        self.heads = heads_width // HEAD_DIM
        self.blocks = hidden // 256
        self.down_at = 0
        self.up_at = self.blocks
        self.out_at = 2 * self.blocks
        self.mixed_at = self.out_at + 1
        self.pack_at = self.out_at + 2
        self.value_at = self.out_at + 3
        self.query_at = tuple(self.out_at + 4 + m for m in range(3))
        self.ring = Ring(self.out_at + 7, 32, width)

    def call(self, lengths, small, arrays):
        names = list(arrays)
        ring = self.ring
        r, w, hw, hid = self.rows, self.width, self.heads_width, self.hidden
        bf = jnp.bfloat16
        V = pltpu.VMEM
        scratch = [V(a.shape, a.dtype) for a in arrays.values()]
        scratch += [
            V((r, hid), bf), V((r, hid), bf), V((r, w), bf), V((2 * self.heads, r, HEAD_DIM), bf),
            V((2, 3, r, hw), bf), V((r, w), F32), V((8, hid), F32), V((8, w), F32),
            pltpu.SemaphoreType.DMA((len(names),)),
            pltpu.SemaphoreType.DMA((1,)),
            pltpu.SemaphoreType.DMA((2,)),
        ]
        n_scratch = len(scratch)
        scratch += ring.scratch()
        S = jax.ShapeDtypeStruct
        outs = (
            S((ring.n, 8, ring.e, w), F32),
            S((5, ring.e, w), F32),
            S((r, w), F32),
        )
        anywhere = pl.BlockSpec(memory_space=pl.ANY)

        def kern(length, gain_ref, *refs):
            ins = refs[: len(names)]
            out, out_x, grad_tokens = refs[len(names) : len(names) + 3]
            rest = refs[len(names) + 3 :]
            held = SimpleNamespace(**dict(zip(names, rest[: len(names)])))
            ring.bind(out, *rest[n_scratch:])
            self.body(length, gain_ref, ins, held, out, out_x, grad_tokens, *rest[len(names) : n_scratch])

        return pl.pallas_call(
            kern,
            out_shape=outs,
            in_specs=[
                pl.BlockSpec(memory_space=pltpu.SMEM),
                pl.BlockSpec(memory_space=pltpu.VMEM),
            ]
            + [anywhere] * len(names),
            out_specs=(anywhere,) * 3,
            scratch_shapes=scratch,
            name="backward_sum",
            compiler_params=pltpu.CompilerParams(
                collective_id=5, has_side_effects=True, vmem_limit_bytes=63 * 2**20
            ),
        )(lengths, small, *arrays.values())

    def body(
        self, length, gain, ins, held, out, out_x, grad_tokens,
        pre, pre_o, branch, gm, gh, work, up_sums, row_sums, loaded, saved, xsem,
    ):
        ring, rows, width, hw, hidden = self.ring, self.rows, self.width, self.heads_width, self.hidden
        heads, blocks = self.heads, self.blocks
        kept = list(vars(held).values())
        scale = HEAD_DIM ** (-0.5)
        dp, tensor = lax.axis_index("dp"), lax.axis_index("tensor")
        to_x = (dp, 1 - tensor)

        at = 2 * hw + hidden + width
        gain_row = gain[0:1, at : at + width]
        ring.greet([to_x])
        for i in range(len(kept)):
            pltpu.make_async_copy(ins[i], kept[i], loaded.at[i]).start()
        there = set()

        def need(*wanted):
            for ref in wanted:
                i = [one is ref for one in kept].index(True)
                if i not in there:
                    there.add(i)
                    pltpu.make_async_copy(ins[i], kept[i], loaded.at[i]).wait()

        def put(k, value):
            ring.g[k % ring.SLOTS] = value.reshape(8, ring.e, width)

        def put_rows(k, at, lane, value):
            count = value.shape[0] // ring.e
            ring.g[k % ring.SLOTS, at : at + count, :, lane : lane + value.shape[1]] = value.reshape(
                count, ring.e, value.shape[1]
            )

        def make_down(b):
            put(self.down_at + b, left_product(held.act[b], held.grad_down[...]))

        def make_pre(b, w_ref, at, to):
            need(held.slope, w_ref)
            lo = b * 256
            value = right_product(held.grad_down[...], w_ref[lo : lo + 256])
            to[:, lo : lo + 256] = to_bf(value * held.slope[at].astype(F32))

        def make_up(i):
            need(held.first_low)
            half, r = divmod(i, blocks // 2)
            put(
                self.up_at + i,
                left_product(held.first_low[:, r * 256 : (r + 1) * 256], pre[:, half * width : (half + 1) * width]),
            )

        def feed_back():
            need(held.grad_second, held.wu, held.wu_o)
            for b in range(blocks):
                lo = b * 256
                up_sums[0:1, lo : lo + 256] = jnp.sum(
                    pre[:, lo : lo + 256].astype(F32), axis=0, keepdims=True
                )
            grad = held.grad_second
            for lo in range(0, rows, 256):
                at = slice(lo, lo + 256)
                work[at] = right_product(pre[at], held.wu[...])
                grad[at] = grad[at] + (work[at] + right_product(pre_o[at], held.wu_o[...]))

        def norm_step():
            need(held.first_normed, held.first_inv, held.sums, held.wo, held.wo_o)
            grad, normed = held.grad_second, held.first_normed
            row_sums[3:6] = held.sums[0:3]
            total_gain = jnp.zeros((1, width), F32)
            total_shift = jnp.zeros((1, width), F32)
            total_branch = jnp.zeros((1, width), F32)
            for lo in range(0, rows, 128):
                at = slice(lo, lo + 128)
                g, n = grad[at], normed[at]
                total_gain += jnp.sum(g * n, axis=0, keepdims=True)
                total_shift += jnp.sum(g, axis=0, keepdims=True)
                resid = norm_back(g, n, held.first_inv[at], gain_row)
                grad[at] = resid
                low = to_bf(resid)
                branch[at] = low
                total_branch += jnp.sum(low.astype(F32), axis=0, keepdims=True)
            row_sums[0:1] = total_branch
            row_sums[1:2] = total_gain
            row_sums[2:3] = total_shift
            for side, w_ref in enumerate((held.wo, held.wo_o)):
                part = to_bf(right_product(branch[...], w_ref[...]))
                for h in range(heads):
                    gm[side * heads + h] = part[:, h * HEAD_DIM : (h + 1) * HEAD_DIM]

        key_bias = jnp.where(
            lax.broadcasted_iota(jnp.int32, (rows, 1), 0) < length[0], 0.0, mask_fill
        ).astype(F32)

        def head_back(h):
            q, k, v, gmix = held.q[h], held.k[h], held.v[h], gm[h]
            probs = jnp.exp(right_product(k, q) + key_bias - held.lse[h])
            grad_probs = right_product(v, gmix)
            inner = jnp.sum(probs * grad_probs, axis=0, keepdims=True)
            grad_scores = to_bf(probs * (grad_probs - inner))
            return (
                to_bf(left_product(grad_scores, k)) * scale,
                to_bf(product(grad_scores, q)),
                to_bf(product(to_bf(probs), gmix)),
            )

        def pair_back(side, p):
            need(held.q, held.k, held.v, held.lse)
            one = head_back(side * heads + 2 * p)
            two = head_back(side * heads + 2 * p + 1)
            for i in range(3):
                gh[side, i, :, p * 128 : (p + 1) * 128] = jnp.concatenate([one[i], two[i]], axis=1)

        def make_out(first, count, k, at):
            need(held.mixed)
            put_rows(k, at, 0, left_product(held.mixed[:, first : first + count], branch[...]))

        def make_value(first, count, k, at):
            need(held.inp)
            for side in range(2):
                lo = side * (width // 2) + first
                put_rows(k, at, side * hw, left_product(held.inp[:, lo : lo + count], gh[0, 2]))

        def make_query(m):
            k = self.query_at[m]
            need(held.inp)
            for i in range(2):
                put_rows(k, 0, i * hw, left_product(held.inp[:, m * 256 : (m + 1) * 256], gh[0, i]))

        def input_grad():
            need(held.wq, held.wk, held.wv, held.wq_o, held.wk_o, held.wv_o, held.place)
            grad = held.grad_second
            swapped = jnp.sum(held.place[...].astype(F32), axis=1, keepdims=True) > 0.5
            for lo in range(0, rows, 256):
                at = slice(lo, lo + 256)
                work[at] = (
                    right_product(gh[0, 0, at], held.wq[...])
                    + right_product(gh[0, 1, at], held.wk[...])
                    + right_product(gh[0, 2, at], held.wv[...])
                )
                other = (
                    right_product(gh[1, 0, at], held.wq_o[...])
                    + right_product(gh[1, 1, at], held.wk_o[...])
                    + right_product(gh[1, 2, at], held.wv_o[...])
                )
                total = grad[at] + (work[at] + other)
                grad[at] = total
                work[at] = jnp.where(swapped[at], 0.0, total)
            pltpu.make_async_copy(work, grad_tokens, saved.at[0]).start()

        def make_pack():
            k = self.pack_at
            half = width // 2
            ours = held.grad_second[:, pl.ds(pl.multiple_of(tensor * half, 128), half)]
            high = to_bf(ours)
            low = to_bf(ours - high.astype(F32))
            place = held.place
            swap = left_product(place[...], high) + left_product(place[...], low)
            repl = swap.shape[0] // 2
            put_rows(k, 0, 0, swap[:repl])
            put_rows(k, 0, half, swap[repl:])
            at = repl // ring.e
            slot = k % ring.SLOTS
            ring.g[slot, at:] = jnp.zeros((8 - at, ring.e, width), F32)
            shared = jnp.where(tensor == 0, row_sums[0:6, :half], row_sums[0:6, half:])
            ring.g[slot, at, 0:6, 0:half] = shared
            ring.g[slot, at, 0:1, half:] = jnp.sum(gh[0, 0].astype(F32), axis=0, keepdims=True)
            ring.g[slot, at, 1:2, half:] = jnp.sum(gh[0, 2].astype(F32), axis=0, keepdims=True)
            for i in range(hidden // half):
                ring.g[slot, at, 2 + i : 3 + i, half:] = up_sums[0:1, i * half : (i + 1) * half]

        need(held.grad_down, held.act)
        make_down(0)
        ring.await_partners([to_x])
        n = ring.n
        work_of = {}

        def plan(t, *jobs):
            work_of.setdefault(t, []).extend(jobs)

        for b in range(1, blocks):
            plan(b - 1, lambda b=b: make_down(b))
        for b in range(blocks):
            plan(b // 2, lambda b=b: make_pre(b, held.wd, b, pre))
            plan(3 + b // 3, lambda b=b: make_pre(b, held.wd_o, blocks + b, pre_o))
        for i in range(blocks):
            plan(self.up_at - 1 + i, lambda i=i: make_up(i))
        plan(5, feed_back)
        plan(6, norm_step)
        for side in range(2):
            for p in range(heads // 2):
                plan(max(7, 6 + side * (heads // 2) + p), lambda side=side, p=p: pair_back(side, p))
        first_rows = 256
        left = hw - first_rows
        plan(self.out_at - 1, lambda: make_out(0, first_rows, self.out_at, 0))
        plan(self.mixed_at - 1, lambda: make_out(first_rows, left, self.mixed_at, 0))
        plan(self.mixed_at - 1, lambda: make_value(0, 256 - left, self.mixed_at, left // ring.e))
        plan(self.value_at - 1, lambda: make_value(256 - left, 256, self.value_at, 0))
        plan(self.pack_at - 2, input_grad)
        for m in range(3):
            plan(self.query_at[m] - 1, lambda m=m: make_query(m))
        plan(self.pack_at - 1, make_pack)
        last = max(work_of) + 1
        for t in range(last):
            ring.tick(t)
            for job in work_of.get(t, ()):
                job()
        exchange = pltpu.make_async_remote_copy(
            out.at[self.pack_at, 0:5], out_x, xsem.at[0], xsem.at[1], device_id=to_x, device_id_type=MESH
        )
        sent_at = self.pack_at + ring.STAGES - 1

        def rest(t, carry):
            ring.tick(t)

            @pl.when(t == sent_at)
            def _():
                exchange.start()

            return carry

        lax.fori_loop(last, n + ring.STAGES - 1, rest, 0)
        exchange.wait()
        pltpu.make_async_copy(work, grad_tokens, saved.at[0]).wait()


def unpack(packed, packed_x, rows, width, hw, hidden, repl):
    back = Backward(rows, width, hw, hidden)
    blocks = back.blocks
    S = jax.ShapeDtypeStruct
    outs = (
        S((hidden, width), F32), S((width, hidden), F32), S((hw, width), F32),
        S((width, hw), F32), S((width, hw), F32), S((width, hw), F32),
        S((repl, width), F32), S((8, width), F32), S((8, width // 2), F32),
    )
    left = hw - 256
    half = width // 2

    def kern(packed_ref, x_ref, wd, wu, wo, wq, wk, wv, swap, shared, private, src, src_x, sem_in, sem):
        tensor = lax.axis_index("tensor")
        moves = []
        for b in range(blocks):
            moves.append((b, src.at[b], wd.at[b * 256 : (b + 1) * 256]))
        for b in range(blocks):
            side, r = divmod(b, blocks // 2)
            k = back.up_at + b
            moves.append(
                (k, src.at[k], wu.at[r * 256 : (r + 1) * 256, side * width : (side + 1) * width])
            )
        moves.append((back.out_at, src.at[back.out_at], wo.at[0:256]))
        k = back.mixed_at
        moves.append((k, src.at[k, 0:left], wo.at[256:hw]))
        for side in range(2):
            lo = side * half
            lanes = slice(side * hw, (side + 1) * hw)
            moves.append((k, src.at[k, left:256, lanes], wv.at[lo : lo + 256 - left]))
        k = back.value_at
        for side in range(2):
            lo = side * half
            lanes = slice(side * hw, (side + 1) * hw)
            moves.append((k, src.at[k, :, lanes], wv.at[lo + 256 - left : lo + half]))
        for m, k in enumerate(back.query_at):
            for i, to in enumerate((wq, wk)):
                lanes = slice(i * hw, (i + 1) * hw)
                moves.append((k, src.at[k, :, lanes], to.at[m * 256 : (m + 1) * 256]))
        top = repl // 2
        for k, ref, place in ((back.pack_at, src.at[back.pack_at], tensor), (-1, src_x, 1 - tensor)):
            lanes = pl.ds(pl.multiple_of(place * half, 128), half)
            moves.append((k, ref.at[0:top, 0:half], swap.at[0:top, lanes]))
            moves.append((k, ref.at[0:top, half:width], swap.at[top:repl, lanes]))
            moves.append((k, ref.at[top : top + 8, 0:half], shared.at[:, lanes]))
        moves.append((back.pack_at, src.at[back.pack_at, top : top + 8, half:width], private))

        def fetch(k):
            if k < 0:
                return pltpu.make_async_copy(x_ref, src_x, sem_in.at[packed.shape[0]])
            return pltpu.make_async_copy(packed_ref.at[k], src.at[k], sem_in.at[k])

        used = []
        for k, _, _ in moves:
            if k not in used:
                used.append(k)
        for k in used:
            fetch(k).start()
        arrived = set()
        copies = []
        for i, (k, a, b) in enumerate(moves):
            if k not in arrived:
                arrived.add(k)
                fetch(k).wait()
            copy = pltpu.make_async_copy(a, b, sem.at[i])
            copy.start()
            copies.append(copy)
        for copy in copies:
            copy.wait()

    anywhere = pl.BlockSpec(memory_space=pl.ANY)
    return pl.pallas_call(
        kern,
        out_shape=outs,
        in_specs=[anywhere] * 2,
        out_specs=(anywhere,) * len(outs),
        scratch_shapes=[
            pltpu.VMEM(packed.shape, F32),
            pltpu.VMEM(packed_x.shape, F32),
            pltpu.SemaphoreType.DMA((packed.shape[0] + 1,)),
            pltpu.SemaphoreType.DMA((2 * blocks + 19,)),
        ],
        name="unpack",
        compiler_params=pltpu.CompilerParams(vmem_limit_bytes=60 * 2**20),
    )(packed, packed_x)


def local(
    tokens,
    lengths,
    positions,
    swap_ids,
    swap_rows,
    w_query,
    b_query,
    w_key,
    w_value,
    b_value,
    w_out,
    b_out,
    first_gain,
    first_shift,
    w_up,
    b_up,
    w_down,
    b_down,
    second_gain,
    second_shift,
    cotangent,
    dp_count,
):
    row_count, model_width = tokens.shape
    heads_width = w_query.shape[1]
    hidden = w_up.shape[1]
    vectors = (b_query, b_value, b_up, b_out, first_gain, first_shift, b_down, second_gain, second_shift)
    length = sum(one.shape[0] for one in vectors)
    small = jnp.zeros((length,), F32)
    at = 0
    for one in vectors:
        small += jnp.pad(one.astype(F32), (at, length - at - one.shape[0]))
        at += one.shape[0]
    small = jnp.broadcast_to(small[None, :], (8, length))
    fw = Forward(row_count, model_width, heads_width, hidden).call(
        lengths, tokens, positions, swap_ids, swap_rows, w_query, w_key, w_value, w_out, w_up, w_down,
        cotangent, small,
    )
    arrays = dict(
        grad_down=fw.grad_down, act=fw.act, wd=w_down, slope=fw.slope, wd_o=fw.wd, grad_second=fw.grad_second,
        wu=w_up, wu_o=fw.wu, first_low=fw.first_low, first_normed=fw.first_normed, first_inv=fw.first_inv,
        sums=fw.sums, wo=w_out, wo_o=fw.wo, q=fw.q, k=fw.k, v=fw.v, lse=fw.lse, mixed=fw.mixed, inp=fw.inp,
        wq=w_query, wk=w_key, wv=w_value, wq_o=fw.wq, wk_o=fw.wk, wv_o=fw.wv, place=fw.place,
    )
    back = Backward(row_count, model_width, heads_width, hidden)
    summed, summed_x, grad_tokens = back.call(lengths, small, arrays)
    if dp_count > 16:
        groups = [list(range(i, dp_count, 16)) for i in range(16)]
        summed, summed_x = lax.psum((summed, summed_x), "dp", axis_index_groups=groups)
    packed = summed.reshape(summed.shape[0], 256, model_width)
    packed_x = summed_x.reshape(-1, model_width)
    repl = swap_rows.shape[0]
    sum_down, sum_up, sum_out, sum_query, sum_key, sum_value, sum_swap, shared, private = unpack(
        packed, packed_x, row_count, model_width, heads_width, hidden, repl
    )
    return (
        fw.layer,
        grad_tokens,
        sum_swap,
        sum_query,
        private[0],
        sum_key,
        sum_value,
        private[1],
        sum_out,
        shared[0],
        shared[1],
        shared[2],
        sum_up,
        private[2:6].reshape(-1),
        sum_down,
        shared[5],
        shared[3],
        shared[4],
    )


def solution(mesh):
    in_specs = (
        P("dp", None),
        P("dp"),
        P("dp", None),
        P("dp", None),
        P(),
        P(None, "tensor"),
        P("tensor"),
        P(None, "tensor"),
        P(None, "tensor"),
        P("tensor"),
        P("tensor", None),
        P(),
        P(),
        P(),
        P(None, "tensor"),
        P("tensor"),
        P("tensor", None),
        P(),
        P(),
        P(),
        P("dp", None),
    )
    out_specs = (
        P("dp", None),
        P("dp", None),
        P(),
        P(None, "tensor"),
        P("tensor"),
        P(None, "tensor"),
        P(None, "tensor"),
        P("tensor"),
        P("tensor", None),
        P(),
        P(),
        P(),
        P(None, "tensor"),
        P("tensor"),
        P("tensor", None),
        P(),
        P(),
        P(),
    )
    count = mesh.shape["dp"]

    def run(*arrays):
        return local(*arrays, dp_count=count)

    return jax.shard_map(run, mesh=mesh, in_specs=in_specs, out_specs=out_specs, check_vma=False)
```

```python
from types import SimpleNamespace

import jax
import jax.numpy as jnp
from jax import lax
from jax.experimental import pallas as pl
from jax.experimental.pallas import tpu as pltpu
from jax.sharding import PartitionSpec as P

F32 = jnp.float32
MESH = pl.DeviceIdType.MESH

HEAD_DIM = 64


norm_eps = 1e-12
mask_fill = -1000000000.0
half_root = 0.7071067811865476
gauss_norm = 0.3989422804014327


def to_bf(value):
    return value.astype(jnp.bfloat16)


def product(left, right):
    return jnp.dot(left, right, preferred_element_type=jnp.float32)


def left_product(left, right):
    return lax.dot_general(
        left, right, (((0,), (0,)), ((), ())), preferred_element_type=jnp.float32
    )


def right_product(left, right):
    return lax.dot_general(
        left, right, (((1,), (1,)), ((), ())), preferred_element_type=jnp.float32
    )


def layer_norm(hidden, norm_gain, norm_shift):
    row_mean = jnp.mean(hidden, axis=-1, keepdims=True)
    centred = hidden - row_mean
    inv_std = lax.rsqrt(jnp.mean(centred * centred, axis=-1, keepdims=True) + norm_eps)
    normed = centred * inv_std
    return (normed * norm_gain + norm_shift, normed, inv_std)


def norm_back(upstream, normed, inv_std, norm_gain):
    scaled = upstream * norm_gain
    return inv_std * (
        scaled
        - jnp.mean(scaled, axis=-1, keepdims=True)
        - normed * jnp.mean(scaled * normed, axis=-1, keepdims=True)
    )


class Ring:
    RECV = ("rc", "rya", "rzb", "rza", "rma", "rmb", "ryb", "zoa", "yoa", "mob", "zob", "zoc", "co", "la", "lb")
    SLOTS = 8
    STAGES = 8

    def __init__(self, chunks, eighth, width):
        self.n, self.e, self.w = chunks, eighth, width

    def scratch(self):
        def buffer(*lead):
            return pltpu.VMEM((self.SLOTS,) + lead + (self.e, self.w), F32)

        bufs = [buffer(8), buffer(4), buffer(), buffer(2), buffer(), buffer(), buffer(), buffer()]
        sems = pltpu.SemaphoreType.DMA((len(self.RECV), self.SLOTS))
        return bufs + [sems, sems]

    def bind(self, out, g, rc, rya, rzb, rza, rma, rmb, ryb, recv, sent):
        self.out, self.g, self.rc, self.rya, self.rzb = out, g, rc, rya, rzb
        self.rza, self.rma, self.rmb, self.ryb = rza, rma, rmb, ryb
        self.recv, self.sent = recv, sent
        dp = lax.axis_index("dp")
        self.t = lax.axis_index("tensor")
        self.c, self.y, self.z = dp % 2, (dp // 2) % 2, (dp // 4) % 4
        self.inner = ((self.z + 1) // 2) == 1
        self.outer = jnp.logical_not(self.inner)
        self.s = self.z // 2
        self.to_c = dp + 1 - 2 * self.c
        self.to_y = dp + 2 * (1 - 2 * self.y)
        self.to_z = dp + 4 * (1 - 2 * (self.z % 2))
        self.to_m = dp + 4 * (3 - 2 * self.z)

    def slot(self, k):
        return k % self.SLOTS

    def remote(self, name, k, src, dst, to):
        i, j = self.RECV.index(name), self.slot(k)
        return pltpu.make_async_remote_copy(
            src, dst, self.sent.at[i, j], self.recv.at[i, j], device_id=(to, self.t), device_id_type=MESH
        )

    def wait(self, name, k, like):
        pltpu.make_async_copy(like, like, self.recv.at[self.RECV.index(name), self.slot(k)]).wait()

    def gone(self, name, k, like):
        pltpu.make_async_copy(like, like, self.sent.at[self.RECV.index(name), self.slot(k)]).wait()

    def local(self, name, k, src, dst):
        return pltpu.make_async_copy(src, dst, self.recv.at[self.RECV.index(name), self.slot(k)])

    def greet(self, more):
        bar = pltpu.get_barrier_semaphore()

        def signal(to):
            pl.semaphore_signal(bar, inc=1, device_id=to, device_id_type=MESH)

        for place in (self.to_c, self.to_y, self.to_z):
            signal((place, self.t))
        for to in more:
            signal(to)

        @pl.when(self.inner)
        def _():
            signal((self.to_m, self.t))

    def await_partners(self, more):
        bar = pltpu.get_barrier_semaphore()

        @pl.when(self.inner)
        def _():
            pl.semaphore_wait(bar, 4 + len(more))

        @pl.when(self.outer)
        def _():
            pl.semaphore_wait(bar, 3 + len(more))

    def half(self, k):
        return self.out.at[k, pl.ds(self.c * 4, 4)]

    def oa(self, k, y):
        return self.out.at[k, self.c * 4 + y]

    def ob(self, k, s):
        return self.out.at[k, self.c * 4 + 2 + s]

    def stage0(self, k):
        j = self.slot(k)
        self.remote("rc", k, self.g.at[j, pl.ds((1 - self.c) * 4, 4)], self.rc.at[j], self.to_c).start()

    def stage1(self, k):
        g, c, j = self.g, self.c, self.slot(k)
        self.wait("rc", k, self.rc.at[j])
        for i in range(4):
            g[j, c * 4 + i] = g[j, c * 4 + i] + self.rc[j, i]
        self.remote("rya", k, g.at[j, c * 4 + 1 - self.y], self.rya.at[j], self.to_y).start()

        @pl.when(self.outer)
        def _():
            self.remote("rzb", k, g.at[j, pl.ds(c * 4 + 2, 2)], self.rzb.at[j], self.to_z).start()

    def stage2(self, k):
        g, c, y, s, j = self.g, self.c, self.y, self.s, self.slot(k)
        self.wait("rya", k, self.rya.at[j])
        g[j, c * 4 + y] = g[j, c * 4 + y] + self.rya[j]

        @pl.when(self.outer)
        def _():
            self.remote("rza", k, g.at[j, c * 4 + y], self.rza.at[j], self.to_z).start()

        @pl.when(self.inner)
        def _():
            self.wait("rzb", k, self.rzb.at[j])
            for i in range(2):
                g[j, c * 4 + 2 + i] = g[j, c * 4 + 2 + i] + self.rzb[j, i]
            self.remote("rmb", k, g.at[j, c * 4 + 2 + 1 - s], self.rmb.at[j], self.to_m).start()

    def stage3(self, k):
        g, c, y, s, j = self.g, self.c, self.y, self.s, self.slot(k)

        @pl.when(self.inner)
        def _():
            self.wait("rza", k, self.rza.at[j])
            g[j, c * 4 + y] = g[j, c * 4 + y] + self.rza[j]
            self.remote("rma", k, g.at[j, c * 4 + y], self.rma.at[j], self.to_m).start()
            self.wait("rmb", k, self.rmb.at[j])
            g[j, c * 4 + 2 + s] = g[j, c * 4 + 2 + s] + self.rmb[j]
            self.remote("ryb", k, g.at[j, c * 4 + 2 + s], self.ryb.at[j], self.to_y).start()

    def stage4(self, k):
        g, c, y, s, j = self.g, self.c, self.y, self.s, self.slot(k)

        @pl.when(self.inner)
        def _():
            self.wait("rma", k, self.rma.at[j])
            self.rma[j] = self.rma[j] + g[j, c * 4 + y]
            self.remote("zoa", k, self.rma.at[j], self.oa(k, y), self.to_z).start()
            self.remote("yoa", k, self.rma.at[j], self.oa(k, y), self.to_y).start()
            self.local("la", k, self.rma.at[j], self.oa(k, y)).start()
            self.wait("ryb", k, self.ryb.at[j])
            self.ryb[j] = self.ryb[j] + g[j, c * 4 + 2 + s]
            self.remote("mob", k, self.ryb.at[j], self.ob(k, s), self.to_m).start()
            self.remote("zob", k, self.ryb.at[j], self.ob(k, s), self.to_z).start()
            self.local("lb", k, self.ryb.at[j], self.ob(k, s)).start()

    def stage5(self, k):
        y, s = self.y, self.s

        @pl.when(self.outer)
        def _():
            self.wait("zoa", k, self.oa(k, y))
            self.remote("yoa", k, self.oa(k, y), self.oa(k, y), self.to_y).start()

        @pl.when(self.inner)
        def _():
            self.wait("mob", k, self.ob(k, 1 - s))
            self.remote("zoc", k, self.ob(k, 1 - s), self.ob(k, 1 - s), self.to_z).start()

    def stage6(self, k):
        y, s = self.y, self.s
        self.wait("yoa", k, self.oa(k, 1 - y))

        @pl.when(self.inner)
        def _():
            self.wait("la", k, self.oa(k, y))
            self.wait("lb", k, self.ob(k, s))

        @pl.when(self.outer)
        def _():
            self.wait("zob", k, self.ob(k, s))
            self.wait("zoc", k, self.ob(k, 1 - s))

        self.remote("co", k, self.half(k), self.half(k), self.to_c).start()

    def stage7(self, k):
        j = self.slot(k)
        self.wait("co", k, self.half(k))
        self.gone("rc", k, self.rc.at[j])
        self.gone("co", k, self.rc.at[j])
        self.gone("rya", k, self.rya.at[j])
        self.gone("yoa", k, self.rya.at[j])

        @pl.when(self.inner)
        def _():
            for name in ("rmb", "rma", "ryb", "zoa", "mob", "zob", "zoc"):
                self.gone(name, k, self.rya.at[j])

        @pl.when(self.outer)
        def _():
            self.gone("rzb", k, self.rzb.at[j])
            self.gone("rza", k, self.rza.at[j])

    def tick(self, t):
        stages = (
            self.stage0, self.stage1, self.stage2, self.stage3,
            self.stage4, self.stage5, self.stage6, self.stage7,
        )
        for i in range(self.STAGES - 1, -1, -1):
            k = t - i
            if isinstance(k, int):
                if 0 <= k < self.n:
                    stages[i](k)
            else:

                @pl.when(jnp.logical_and(k >= 0, k < self.n))
                def _():
                    stages[i](k)


class Forward:
    PARTS = 4
    LAG = (2, 4)
    SENDS = ("x", "z", "y", "cx", "cz", "cy")

    def __init__(self, rows, width, heads_width, hidden):
        self.rows, self.width, self.heads_width, self.hidden = rows, width, heads_width, hidden
        self.heads = heads_width // HEAD_DIM
        self.third_hidden = hidden // 3
        self.blocks = hidden // 256
        self.per_core = self.third_hidden // 256
        self.panels = 2 + 2 * self.per_core
        self.chunks = self.panels * self.PARTS
        self.part_rows = width // self.PARTS

    def outs(self):
        r, w, hw, hid = self.rows, self.width, self.heads_width, self.hidden
        bf = jnp.bfloat16
        S = jax.ShapeDtypeStruct
        return dict(
            layer=S((r, w), bf),
            wq=S((w, hw), bf), wk=S((w, hw), bf), wv=S((w, hw), bf), wo=S((hw, w), bf),
            wu=S((w, hid), bf), wd=S((hid, w), bf),
            inp=S((r, w), bf), place=S((r, 256), bf),
            q=S((2 * self.heads, r, HEAD_DIM), bf), k=S((2 * self.heads, r, HEAD_DIM), bf),
            v=S((2 * self.heads, r, HEAD_DIM), bf), lse=S((2 * self.heads, 1, r), F32),
            mixed=S((r, hw), bf),
            first_low=S((r, w), bf), first_normed=S((r, w), F32), first_inv=S((r, 1), F32),
            act=S((r, hid), bf), slope=S((2 * self.blocks, r, 256), bf),
            grad_second=S((r, w), F32), grad_down=S((r, w), bf), sums=S((8, w), F32),
        )

    def call(self, *args):
        outs = self.outs()
        names = list(outs)
        n = self.chunks
        panel = pltpu.VMEM((n, self.part_rows, 128), F32)
        scratch = [pltpu.VMEM(o.shape, o.dtype) for o in outs.values()]
        scratch += [panel] * 7
        scratch += [
            pltpu.VMEM((8, 2 * self.heads_width + self.hidden), F32),
            pltpu.VMEM((self.rows, self.width), F32),
            pltpu.VMEM((self.rows, self.width), F32),
            pltpu.VMEM((self.rows, self.width), F32),
            pltpu.VMEM((self.rows, self.hidden), jnp.bfloat16),
            pltpu.SemaphoreType.DMA((len(self.SENDS), n)),
            pltpu.SemaphoreType.DMA((len(self.SENDS) + 1,)),
            pltpu.SemaphoreType.DMA((1,)),
            pltpu.SemaphoreType.DMA((len(names),)),
        ]
        late = args[5:12]
        scratch += [pltpu.VMEM(a.shape, a.dtype) for a in late]
        scratch.append(pltpu.SemaphoreType.DMA((len(late),)))
        vm = pl.BlockSpec(memory_space=pltpu.VMEM)
        specs = [pl.BlockSpec(memory_space=pltpu.SMEM)] + [vm] * (len(args) - 1)
        specs[5:12] = [pl.BlockSpec(memory_space=pl.ANY)] * len(late)

        def kern(*refs):
            ins = refs[: len(args)]
            out_refs = SimpleNamespace(**dict(zip(names, refs[len(args) : len(args) + len(names)])))
            rest = refs[len(args) + len(names) :]
            held = SimpleNamespace(**dict(zip(names, rest[: len(names)])))
            self.body(ins, out_refs, held, *rest[len(names) :])

        got = pl.pallas_call(
            kern,
            out_shape=tuple(outs.values()),
            in_specs=specs,
            out_specs=tuple(pl.BlockSpec(memory_space=pl.ANY) for _ in names),
            scratch_shapes=scratch,
            name="forward_gather",
            compiler_params=pltpu.CompilerParams(
                collective_id=4, has_side_effects=True, vmem_limit_bytes=62 * 2**20
            ),
        )(*args)
        return SimpleNamespace(**dict(zip(names, got)))

    def body(self, ins, out_refs, held, xs, lx, lz, ly, sx, sz, sy, bias_o, acc, acc_o, first_out, act_o, recv, sent, brecv, saved, *fetched):
        (length, tokens, positions, swap_ids, swap_rows) = ins[:5]
        far, small = ins[5:12], ins[12]
        *near, fetch_sems = fetched
        fetches = [pltpu.make_async_copy(a, b, fetch_sems.at[i]) for i, (a, b) in enumerate(zip(far, near))]
        for fetch in fetches[:4]:
            fetch.start()
        (wq, wk, wv, wo, wu, wd, cot) = near
        rows, width, hw, hidden = self.rows, self.width, self.heads_width, self.hidden

        bias = small.at[:, 0 : 2 * hw + hidden]

        def vector(i):
            at = 2 * hw + hidden + i * width
            return small[0:1, at : at + width]

        n, parts, part_rows = self.chunks, self.PARTS, self.part_rows
        bf = jnp.bfloat16
        dp = lax.axis_index("dp")
        tensor = lax.axis_index("tensor")
        c, y, low = dp % 2, (dp // 2) % 2, (dp // 4) % 2

        def flip(unit, bit):
            return dp + unit * (1 - 2 * bit)

        to = {"x": (dp, 1 - tensor), "z": (flip(4, low), tensor), "y": (flip(2, y), tensor)}
        to["cx"] = to["cz"] = to["cy"] = (flip(1, c), tensor)
        own_third = jnp.where(low == 0, y, 2)
        z_third = jnp.where(low == 0, 2, y)
        y_third = 1 - y

        def remote(name, i, src, dst):
            s = self.SENDS.index(name)
            return pltpu.make_async_remote_copy(
                src.at[i], dst.at[i], sent.at[s], recv.at[s, i], device_id=to[name], device_id_type=MESH
            )

        def wait(name, i, dst):
            pltpu.make_async_copy(dst.at[i], dst.at[i], recv.at[self.SENDS.index(name), i]).wait()

        kept = list(vars(held).values())
        kept_out = list(vars(out_refs).values())

        def save(*refs):
            for ref in refs:
                i = [one is ref for one in kept].index(True)
                pltpu.make_async_copy(ref, kept_out[i], saved.at[i]).start()

        def save_rows(at, *refs):
            for ref in refs:
                i = [one is ref for one in kept].index(True)
                pltpu.make_async_copy(ref.at[at], kept_out[i].at[at], saved.at[i]).start()

        bar = pltpu.get_barrier_semaphore()
        for name in ("x", "z", "y", "cx"):
            pl.semaphore_signal(bar, inc=1, device_id=to[name], device_id_type=MESH)

        def put(p, value):
            xs[p * parts : (p + 1) * parts] = value.astype(F32).reshape(parts, part_rows, 128)

        def put_blocks(p, ref, at):
            for b in range(width // 128):
                lo = b * 128
                block = ref[pl.ds(pl.multiple_of(at, 128), 128), lo : lo + 128].astype(F32)
                done = 0
                while done < 128:
                    i, r = divmod(lo + done, part_rows)
                    take = min(128 - done, part_rows - r)
                    xs[p * parts + i, r : r + take] = block[done : done + take]
                    done += take

        def start_x(p):
            for i in range(p * parts, (p + 1) * parts):
                remote("x", i, xs, lx).start()

        def col(at):
            return pl.ds(pl.multiple_of(at, 128), 128)

        at = own_third * 128
        for fetch in fetches[:4]:
            fetch.wait()
        for fetch in fetches[4:]:
            fetch.start()

        @pl.when(c == 0)
        def _():
            put(0, wq[:, col(at)])
            put(1, wk[:, col(at)])

        @pl.when(c == 1)
        def _():
            put(0, wv[:, col(at)])
            put_blocks(1, wo, at)

        pl.semaphore_wait(bar, 4)
        pltpu.make_async_remote_copy(
            bias, bias_o, sent.at[len(self.SENDS)], brecv.at[0], device_id=to["x"], device_id_type=MESH
        ).start()
        start_x(0)
        start_x(1)
        pc = self.per_core
        fetches[4].wait()
        for j in range(pc):
            put(2 + j, wu[:, col(own_third * self.third_hidden + (pc * c + j) * 128)])
            start_x(2 + j)
        fetches[5].wait()
        for j in range(pc):
            put_blocks(2 + pc + j, wd, own_third * self.third_hidden + (pc * c + j) * 128)
            start_x(2 + pc + j)

        def relay_x(i):
            wait("x", i, lx)
            remote("z", i, lx, lz).start()
            remote("cx", i, lx, sx).start()

            @pl.when(low == 0)
            def _():
                remote("y", i, lx, ly).start()

        def relay_z(i):
            wait("z", i, lz)
            remote("cz", i, lz, sz).start()

            @pl.when(low == 1)
            def _():
                remote("y", i, lz, ly).start()

        def relay_y(i):
            wait("y", i, ly)
            remote("cy", i, ly, sy).start()

        def tick(t):
            for relay, k in ((relay_x, t), (relay_z, t - self.LAG[0]), (relay_y, t - self.LAG[1])):
                if isinstance(k, int):
                    if 0 <= k < n:
                        relay(k)
                else:

                    @pl.when(jnp.logical_and(k >= 0, k < n))
                    def _():
                        relay(k)

        place_rows = lax.broadcasted_iota(jnp.int32, (rows, positions.shape[1]), 0)
        hit = jnp.where(place_rows == positions[...], 1.0, 0.0).astype(bf)
        repl_rows = lax.broadcasted_iota(jnp.int32, (swap_rows.shape[0], positions.shape[1]), 0)
        chosen = jnp.where(repl_rows == swap_ids[...], 1.0, 0.0).astype(bf)
        place = right_product(hit, chosen)
        held.place[...] = to_bf(place)
        save(held.place)
        swapped = product(held.place[...], swap_rows[...])
        is_swapped = jnp.sum(place, axis=1, keepdims=True) > 0.5
        held.inp[...] = to_bf(jnp.where(is_swapped, swapped, tokens[...].astype(F32)))
        save(held.inp)
        tick(0)
        inp = held.inp
        scale = HEAD_DIM ** (-0.5)
        qh, kh, vh, lse = held.q, held.k, held.v, held.lse
        heads = self.heads

        def project(first_head, w_q, w_k, w_v, b_ref):
            part = to_bf((product(inp[...], w_q[...]) + b_ref[0:1, :hw]) * scale)
            for h in range(heads):
                qh[first_head + h] = part[:, h * HEAD_DIM : (h + 1) * HEAD_DIM]
            part = to_bf(product(inp[...], w_k[...]))
            for h in range(heads):
                kh[first_head + h] = part[:, h * HEAD_DIM : (h + 1) * HEAD_DIM]
            part = to_bf(product(inp[...], w_v[...]) + b_ref[0:1, hw : 2 * hw])
            for h in range(heads):
                vh[first_head + h] = part[:, h * HEAD_DIM : (h + 1) * HEAD_DIM]

        key_bias = jnp.where(
            lax.broadcasted_iota(jnp.int32, (rows, 1), 0) < length[0], 0.0, mask_fill
        ).astype(F32)

        def attend(h):
            scores = right_product(kh[h], qh[h]) + key_bias
            top = jnp.max(scores, axis=0, keepdims=True)
            exponent = jnp.exp(scores - top)
            total = jnp.sum(exponent, axis=0, keepdims=True)
            lse[h] = top + jnp.log(total)
            probs = to_bf(exponent * (1.0 / total))
            return to_bf(left_product(probs, vh[h]))

        def attend_pairs(first_head, mixed_ref, t0):
            for p in range(heads // 2):
                tick(t0 + 2 * p)
                one = attend(first_head + 2 * p)
                tick(t0 + 2 * p + 1)
                two = attend(first_head + 2 * p + 1)
                mixed_ref[:, p * 128 : (p + 1) * 128] = jnp.concatenate([one, two], axis=1)

        project(0, wq, wk, wv, bias)
        tick(1)
        tick(2)
        attend_pairs(0, held.mixed, 3)
        save(held.mixed)
        acc[...] = product(held.mixed[...], wo[...])
        attn = 2 * parts
        t = 3 + heads
        while t < attn + self.LAG[1]:
            tick(t)
            t += 1
        thirds = ((own_third, lx, sx, "cx"), (z_third, lz, sz, "cz"), (y_third, ly, sy, "cy"))

        def panel_of(ref, p):
            return to_bf(ref[p * parts : (p + 1) * parts].reshape(width, 128))

        def unblock(ref, value, at):
            for b in range(width // 128):
                ref[pl.ds(pl.multiple_of(at, 128), 128), b * 128 : (b + 1) * 128] = value[
                    b * 128 : (b + 1) * 128
                ]

        for third, mine, theirs, name in thirds:
            for i in range(attn):
                wait(name, i, theirs)

            def assemble(first, second):
                held.wq[:, col(third * 128)] = panel_of(first, 0)
                held.wk[:, col(third * 128)] = panel_of(first, 1)
                held.wv[:, col(third * 128)] = panel_of(second, 0)
                unblock(held.wo, panel_of(second, 1), third * 128)

            @pl.when(c == 0)
            def _():
                assemble(mine, theirs)

            @pl.when(c == 1)
            def _():
                assemble(theirs, mine)

        save(held.wq, held.wk, held.wv, held.wo)
        pltpu.make_async_copy(bias_o, bias_o, brecv.at[0]).wait()
        tick(t)
        t += 1
        project(heads, held.wq, held.wk, held.wv, bias_o)
        mixed_o = first_out
        other_parts = []
        for p in range(heads // 2):
            tick(t)
            one = attend(heads + 2 * p)
            tick(t + 1)
            two = attend(heads + 2 * p + 1)
            t += 2
            mixed_o[:, p * 128 : (p + 1) * 128] = jnp.concatenate([one, two], axis=1).astype(F32)
        save(qh, kh, vh, lse)
        acc_o[...] = product(to_bf(mixed_o[:, :hw]), held.wo[...])
        branch = (acc[...] + acc_o[...]) + vector(0)
        first, normed, inv = layer_norm(inp[...].astype(F32) + branch, vector(1), vector(2))
        first_out[...] = first
        held.first_low[...] = to_bf(first)
        held.first_normed[...] = normed
        held.first_inv[...] = inv
        save(held.first_low, held.first_normed, held.first_inv)
        tick(t)
        t += 1
        act, slope = held.act, held.slope

        def feed(b, at, w_ref, b_ref):
            up = (
                product(held.first_low[...], w_ref[:, b * 256 : (b + 1) * 256])
                + b_ref[0:1, 2 * hw + b * 256 : 2 * hw + (b + 1) * 256]
            )
            cdf = 0.5 * (1.0 + lax.erf(up * half_root))
            slope[at] = to_bf(cdf + up * jnp.exp(-0.5 * up * up) * gauss_norm)
            return to_bf(up * cdf)

        for b in range(self.blocks):
            act[:, b * 256 : (b + 1) * 256] = feed(b, b, wu, bias)
            if b % 2 == 1:
                tick(t)
                t += 1
        save(act)
        acc[...] = product(act[...], wd[...])
        tick(t)
        t += 1
        while t < attn + pc * parts + self.LAG[1]:
            tick(t)
            t += 1
        for third, mine, theirs, name in thirds:
            for i in range(attn, attn + pc * parts):
                wait(name, i, theirs)
            for j in range(pc):
                at = third * self.third_hidden + (pc * c + j) * 128
                held.wu[:, col(at)] = panel_of(mine, 2 + j)
                at = third * self.third_hidden + (pc * (1 - c) + j) * 128
                held.wu[:, col(at)] = panel_of(theirs, 2 + j)
        save(held.wu)
        for b in range(self.blocks):
            tick(t)
            t += 1
            act_o[:, b * 256 : (b + 1) * 256] = feed(b, self.blocks + b, held.wu, bias_o)
        save(held.slope)
        while t < n + self.LAG[1]:
            tick(t)
            t += 1
        for order, (third, mine, theirs, name) in enumerate(thirds):
            for i in range(attn + pc * parts, n):
                wait(name, i, theirs)
            for j in range(pc):
                at = third * self.third_hidden + (pc * c + j) * 128
                unblock(held.wd, panel_of(mine, 2 + pc + j), at)
                at = third * self.third_hidden + (pc * (1 - c) + j) * 128
                unblock(held.wd, panel_of(theirs, 2 + pc + j), at)
            units = pl.ds(pl.multiple_of(third * self.third_hidden, 128), self.third_hidden)
            part = product(act_o[:, units], held.wd[units])
            if order == 0:
                acc_o[...] = part
            else:
                acc_o[...] += part
        save(held.wd)
        fetches[6].wait()
        sums = held.sums
        totals = [jnp.zeros((1, width), F32)] * 3
        down_bias, last_gain, last_shift = vector(3), vector(4), vector(5)
        for lo in range(0, rows, 128):
            at = slice(lo, lo + 128)
            down = (acc[at] + acc_o[at]) + down_bias
            result, normed, inv = layer_norm(first_out[at] + down, last_gain, last_shift)
            held.layer[at] = to_bf(result)
            grad_out = cot[at].astype(F32)
            grad = norm_back(grad_out, normed, inv, last_gain)
            held.grad_second[at] = grad
            low_grad = to_bf(grad)
            held.grad_down[at] = low_grad
            save_rows(at, held.layer, held.grad_second, held.grad_down)
            for i, one in enumerate((grad_out * normed, grad_out, low_grad.astype(F32))):
                totals[i] = totals[i] + jnp.sum(one, axis=0, keepdims=True)
        sums[...] = jnp.zeros_like(sums)
        for i in range(3):
            sums[i : i + 1] = totals[i]
        save(sums)
        for name, like in (("x", xs), ("z", lx), ("y", lx), ("cx", lx), ("cz", lx), ("cy", lx)):
            pltpu.make_async_copy(like, like, sent.at[self.SENDS.index(name)]).wait()
        pltpu.make_async_copy(bias_o, bias_o, sent.at[len(self.SENDS)]).wait()
        for i in range(len(kept)):
            pltpu.make_async_copy(kept[i], kept_out[i], saved.at[i]).wait()


class Backward:
    def __init__(self, rows, width, heads_width, hidden):
        self.rows, self.width, self.heads_width, self.hidden = rows, width, heads_width, hidden
        self.heads = heads_width // HEAD_DIM
        self.blocks = hidden // 256
        self.down_at = 0
        self.up_at = self.blocks
        self.out_at = 2 * self.blocks
        self.mixed_at = self.out_at + 1
        self.pack_at = self.out_at + 2
        self.value_at = self.out_at + 3
        self.query_at = tuple(self.out_at + 4 + m for m in range(3))
        self.ring = Ring(self.out_at + 7, 32, width)

    def call(self, lengths, small, arrays):
        names = list(arrays)
        ring = self.ring
        r, w, hw, hid = self.rows, self.width, self.heads_width, self.hidden
        bf = jnp.bfloat16
        V = pltpu.VMEM
        scratch = [V(a.shape, a.dtype) for a in arrays.values()]
        scratch += [
            V((r, hid), bf), V((r, hid), bf), V((r, w), bf), V((2 * self.heads, r, HEAD_DIM), bf),
            V((2, 3, r, hw), bf), V((r, w), F32), V((8, hid), F32), V((8, w), F32),
            pltpu.SemaphoreType.DMA((len(names),)),
            pltpu.SemaphoreType.DMA((1,)),
            pltpu.SemaphoreType.DMA((2,)),
        ]
        n_scratch = len(scratch)
        scratch += ring.scratch()
        S = jax.ShapeDtypeStruct
        outs = (
            S((ring.n, 8, ring.e, w), F32),
            S((5, ring.e, w), F32),
            S((r, w), F32),
        )
        anywhere = pl.BlockSpec(memory_space=pl.ANY)

        def kern(length, gain_ref, *refs):
            ins = refs[: len(names)]
            out, out_x, grad_tokens = refs[len(names) : len(names) + 3]
            rest = refs[len(names) + 3 :]
            held = SimpleNamespace(**dict(zip(names, rest[: len(names)])))
            ring.bind(out, *rest[n_scratch:])
            self.body(length, gain_ref, ins, held, out, out_x, grad_tokens, *rest[len(names) : n_scratch])

        return pl.pallas_call(
            kern,
            out_shape=outs,
            in_specs=[
                pl.BlockSpec(memory_space=pltpu.SMEM),
                pl.BlockSpec(memory_space=pltpu.VMEM),
            ]
            + [anywhere] * len(names),
            out_specs=(anywhere,) * 3,
            scratch_shapes=scratch,
            name="backward_sum",
            compiler_params=pltpu.CompilerParams(
                collective_id=5, has_side_effects=True, vmem_limit_bytes=63 * 2**20
            ),
        )(lengths, small, *arrays.values())

    def body(
        self, length, gain, ins, held, out, out_x, grad_tokens,
        pre, pre_o, branch, gm, gh, work, up_sums, row_sums, loaded, saved, xsem,
    ):
        ring, rows, width, hw, hidden = self.ring, self.rows, self.width, self.heads_width, self.hidden
        heads, blocks = self.heads, self.blocks
        kept = list(vars(held).values())
        scale = HEAD_DIM ** (-0.5)
        dp, tensor = lax.axis_index("dp"), lax.axis_index("tensor")
        to_x = (dp, 1 - tensor)

        at = 2 * hw + hidden + width
        gain_row = gain[0:1, at : at + width]
        ring.greet([to_x])
        for i in range(len(kept)):
            pltpu.make_async_copy(ins[i], kept[i], loaded.at[i]).start()
        there = set()

        def need(*wanted):
            for ref in wanted:
                i = [one is ref for one in kept].index(True)
                if i not in there:
                    there.add(i)
                    pltpu.make_async_copy(ins[i], kept[i], loaded.at[i]).wait()

        def put(k, value):
            ring.g[k % ring.SLOTS] = value.reshape(8, ring.e, width)

        def put_rows(k, at, lane, value):
            count = value.shape[0] // ring.e
            ring.g[k % ring.SLOTS, at : at + count, :, lane : lane + value.shape[1]] = value.reshape(
                count, ring.e, value.shape[1]
            )

        def make_down(b):
            put(self.down_at + b, left_product(held.act[:, b * 256 : (b + 1) * 256], held.grad_down[...]))

        def make_pre(b, w_ref, at, to):
            need(held.slope, w_ref)
            lo = b * 256
            value = right_product(held.grad_down[...], w_ref[lo : lo + 256])
            to[:, lo : lo + 256] = to_bf(value * held.slope[at].astype(F32))

        def make_up(i):
            need(held.first_low)
            half, r = divmod(i, blocks // 2)
            put(
                self.up_at + i,
                left_product(held.first_low[:, r * 256 : (r + 1) * 256], pre[:, half * width : (half + 1) * width]),
            )

        def feed_back():
            need(held.grad_second, held.wu, held.wu_o)
            for b in range(blocks):
                lo = b * 256
                up_sums[0:1, lo : lo + 256] = jnp.sum(
                    pre[:, lo : lo + 256].astype(F32), axis=0, keepdims=True
                )
            grad = held.grad_second
            for lo in range(0, rows, 256):
                at = slice(lo, lo + 256)
                work[at] = right_product(pre[at], held.wu[...])
                grad[at] = grad[at] + (work[at] + right_product(pre_o[at], held.wu_o[...]))

        def norm_step():
            need(held.first_normed, held.first_inv, held.sums, held.wo, held.wo_o)
            grad, normed = held.grad_second, held.first_normed
            row_sums[3:6] = held.sums[0:3]
            total_gain = jnp.zeros((1, width), F32)
            total_shift = jnp.zeros((1, width), F32)
            total_branch = jnp.zeros((1, width), F32)
            for lo in range(0, rows, 128):
                at = slice(lo, lo + 128)
                g, n = grad[at], normed[at]
                total_gain += jnp.sum(g * n, axis=0, keepdims=True)
                total_shift += jnp.sum(g, axis=0, keepdims=True)
                resid = norm_back(g, n, held.first_inv[at], gain_row)
                grad[at] = resid
                low = to_bf(resid)
                branch[at] = low
                total_branch += jnp.sum(low.astype(F32), axis=0, keepdims=True)
            row_sums[0:1] = total_branch
            row_sums[1:2] = total_gain
            row_sums[2:3] = total_shift
            for side, w_ref in enumerate((held.wo, held.wo_o)):
                part = to_bf(right_product(branch[...], w_ref[...]))
                for h in range(heads):
                    gm[side * heads + h] = part[:, h * HEAD_DIM : (h + 1) * HEAD_DIM]

        key_bias = jnp.where(
            lax.broadcasted_iota(jnp.int32, (rows, 1), 0) < length[0], 0.0, mask_fill
        ).astype(F32)

        def head_back(h):
            q, k, v, gmix = held.q[h], held.k[h], held.v[h], gm[h]
            probs = jnp.exp(right_product(k, q) + key_bias - held.lse[h])
            grad_probs = right_product(v, gmix)
            inner = jnp.sum(probs * grad_probs, axis=0, keepdims=True)
            grad_scores = to_bf(probs * (grad_probs - inner))
            return (
                to_bf(left_product(grad_scores, k)) * scale,
                to_bf(product(grad_scores, q)),
                to_bf(product(to_bf(probs), gmix)),
            )

        def pair_back(side, p):
            need(held.q, held.k, held.v, held.lse)
            one = head_back(side * heads + 2 * p)
            two = head_back(side * heads + 2 * p + 1)
            for i in range(3):
                gh[side, i, :, p * 128 : (p + 1) * 128] = jnp.concatenate([one[i], two[i]], axis=1)

        def make_out(first, count, k, at):
            need(held.mixed)
            put_rows(k, at, 0, left_product(held.mixed[:, first : first + count], branch[...]))

        def make_value(first, count, k, at):
            need(held.inp)
            for side in range(2):
                lo = side * (width // 2) + first
                put_rows(k, at, side * hw, left_product(held.inp[:, lo : lo + count], gh[0, 2]))

        def make_query(m):
            k = self.query_at[m]
            need(held.inp)
            for i in range(2):
                put_rows(k, 0, i * hw, left_product(held.inp[:, m * 256 : (m + 1) * 256], gh[0, i]))

        def input_grad():
            need(held.wq, held.wk, held.wv, held.wq_o, held.wk_o, held.wv_o, held.place)
            grad = held.grad_second
            swapped = jnp.sum(held.place[...].astype(F32), axis=1, keepdims=True) > 0.5
            for lo in range(0, rows, 256):
                at = slice(lo, lo + 256)
                work[at] = (
                    right_product(gh[0, 0, at], held.wq[...])
                    + right_product(gh[0, 1, at], held.wk[...])
                    + right_product(gh[0, 2, at], held.wv[...])
                )
                other = (
                    right_product(gh[1, 0, at], held.wq_o[...])
                    + right_product(gh[1, 1, at], held.wk_o[...])
                    + right_product(gh[1, 2, at], held.wv_o[...])
                )
                total = grad[at] + (work[at] + other)
                grad[at] = total
                work[at] = jnp.where(swapped[at], 0.0, total)
            pltpu.make_async_copy(work, grad_tokens, saved.at[0]).start()

        def make_pack():
            k = self.pack_at
            half = width // 2
            ours = held.grad_second[:, pl.ds(pl.multiple_of(tensor * half, 128), half)]
            high = to_bf(ours)
            low = to_bf(ours - high.astype(F32))
            place = held.place
            swap = left_product(place[...], high) + left_product(place[...], low)
            repl = swap.shape[0] // 2
            put_rows(k, 0, 0, swap[:repl])
            put_rows(k, 0, half, swap[repl:])
            at = repl // ring.e
            slot = k % ring.SLOTS
            ring.g[slot, at:] = jnp.zeros((8 - at, ring.e, width), F32)
            shared = jnp.where(tensor == 0, row_sums[0:6, :half], row_sums[0:6, half:])
            ring.g[slot, at, 0:6, 0:half] = shared
            ring.g[slot, at, 0:1, half:] = jnp.sum(gh[0, 0].astype(F32), axis=0, keepdims=True)
            ring.g[slot, at, 1:2, half:] = jnp.sum(gh[0, 2].astype(F32), axis=0, keepdims=True)
            for i in range(hidden // half):
                ring.g[slot, at, 2 + i : 3 + i, half:] = up_sums[0:1, i * half : (i + 1) * half]

        need(held.grad_down, held.act)
        make_down(0)
        ring.await_partners([to_x])
        n = ring.n
        work_of = {}

        def plan(t, *jobs):
            work_of.setdefault(t, []).extend(jobs)

        for b in range(1, blocks):
            plan(b - 1, lambda b=b: make_down(b))
        for b in range(blocks):
            plan(b // 2, lambda b=b: make_pre(b, held.wd, b, pre))
            plan(3 + b // 3, lambda b=b: make_pre(b, held.wd_o, blocks + b, pre_o))
        for i in range(blocks):
            plan(self.up_at - 1 + i, lambda i=i: make_up(i))
        plan(5, feed_back)
        plan(6, norm_step)
        for side in range(2):
            for p in range(heads // 2):
                plan(max(7, 6 + side * (heads // 2) + p), lambda side=side, p=p: pair_back(side, p))
        first_rows = 256
        left = hw - first_rows
        plan(self.out_at - 1, lambda: make_out(0, first_rows, self.out_at, 0))
        plan(self.mixed_at - 1, lambda: make_out(first_rows, left, self.mixed_at, 0))
        plan(self.mixed_at - 1, lambda: make_value(0, 256 - left, self.mixed_at, left // ring.e))
        plan(self.value_at - 1, lambda: make_value(256 - left, 256, self.value_at, 0))
        plan(self.pack_at - 2, input_grad)
        for m in range(3):
            plan(self.query_at[m] - 1, lambda m=m: make_query(m))
        plan(self.pack_at - 1, make_pack)
        last = max(work_of) + 1
        for t in range(last):
            ring.tick(t)
            for job in work_of.get(t, ()):
                job()
        exchange = pltpu.make_async_remote_copy(
            out.at[self.pack_at, 0:5], out_x, xsem.at[0], xsem.at[1], device_id=to_x, device_id_type=MESH
        )
        sent_at = self.pack_at + ring.STAGES - 1

        def rest(t, carry):
            ring.tick(t)

            @pl.when(t == sent_at)
            def _():
                exchange.start()

            return carry

        lax.fori_loop(last, n + ring.STAGES - 1, rest, 0)
        exchange.wait()
        pltpu.make_async_copy(work, grad_tokens, saved.at[0]).wait()


def unpack(packed, packed_x, rows, width, hw, hidden, repl):
    back = Backward(rows, width, hw, hidden)
    blocks = back.blocks
    S = jax.ShapeDtypeStruct
    outs = (
        S((hidden, width), F32), S((width, hidden), F32), S((hw, width), F32),
        S((width, hw), F32), S((width, hw), F32), S((width, hw), F32),
        S((repl, width), F32), S((8, width), F32), S((8, width // 2), F32),
    )
    left = hw - 256
    half = width // 2

    def kern(packed_ref, x_ref, wd, wu, wo, wq, wk, wv, swap, shared, private, src, src_x, sem_in, sem):
        tensor = lax.axis_index("tensor")
        moves = []
        for b in range(blocks):
            moves.append((b, src.at[b], wd.at[b * 256 : (b + 1) * 256]))
        for b in range(blocks):
            side, r = divmod(b, blocks // 2)
            k = back.up_at + b
            moves.append(
                (k, src.at[k], wu.at[r * 256 : (r + 1) * 256, side * width : (side + 1) * width])
            )
        moves.append((back.out_at, src.at[back.out_at], wo.at[0:256]))
        k = back.mixed_at
        moves.append((k, src.at[k, 0:left], wo.at[256:hw]))
        for side in range(2):
            lo = side * half
            lanes = slice(side * hw, (side + 1) * hw)
            moves.append((k, src.at[k, left:256, lanes], wv.at[lo : lo + 256 - left]))
        k = back.value_at
        for side in range(2):
            lo = side * half
            lanes = slice(side * hw, (side + 1) * hw)
            moves.append((k, src.at[k, :, lanes], wv.at[lo + 256 - left : lo + half]))
        for m, k in enumerate(back.query_at):
            for i, to in enumerate((wq, wk)):
                lanes = slice(i * hw, (i + 1) * hw)
                moves.append((k, src.at[k, :, lanes], to.at[m * 256 : (m + 1) * 256]))
        top = repl // 2
        for k, ref, place in ((back.pack_at, src.at[back.pack_at], tensor), (-1, src_x, 1 - tensor)):
            lanes = pl.ds(pl.multiple_of(place * half, 128), half)
            moves.append((k, ref.at[0:top, 0:half], swap.at[0:top, lanes]))
            moves.append((k, ref.at[0:top, half:width], swap.at[top:repl, lanes]))
            moves.append((k, ref.at[top : top + 8, 0:half], shared.at[:, lanes]))
        moves.append((back.pack_at, src.at[back.pack_at, top : top + 8, half:width], private))

        def fetch(k):
            if k < 0:
                return pltpu.make_async_copy(x_ref, src_x, sem_in.at[packed.shape[0]])
            return pltpu.make_async_copy(packed_ref.at[k], src.at[k], sem_in.at[k])

        used = []
        for k, _, _ in moves:
            if k not in used:
                used.append(k)
        for k in used:
            fetch(k).start()
        arrived = set()
        copies = []
        for i, (k, a, b) in enumerate(moves):
            if k not in arrived:
                arrived.add(k)
                fetch(k).wait()
            copy = pltpu.make_async_copy(a, b, sem.at[i])
            copy.start()
            copies.append(copy)
        for copy in copies:
            copy.wait()

    anywhere = pl.BlockSpec(memory_space=pl.ANY)
    return pl.pallas_call(
        kern,
        out_shape=outs,
        in_specs=[anywhere] * 2,
        out_specs=(anywhere,) * len(outs),
        scratch_shapes=[
            pltpu.VMEM(packed.shape, F32),
            pltpu.VMEM(packed_x.shape, F32),
            pltpu.SemaphoreType.DMA((packed.shape[0] + 1,)),
            pltpu.SemaphoreType.DMA((2 * blocks + 19,)),
        ],
        name="unpack",
        compiler_params=pltpu.CompilerParams(vmem_limit_bytes=60 * 2**20),
    )(packed, packed_x)


def local(
    tokens,
    lengths,
    positions,
    swap_ids,
    swap_rows,
    w_query,
    b_query,
    w_key,
    w_value,
    b_value,
    w_out,
    b_out,
    first_gain,
    first_shift,
    w_up,
    b_up,
    w_down,
    b_down,
    second_gain,
    second_shift,
    cotangent,
    dp_count,
):
    row_count, model_width = tokens.shape
    heads_width = w_query.shape[1]
    hidden = w_up.shape[1]
    vectors = (b_query, b_value, b_up, b_out, first_gain, first_shift, b_down, second_gain, second_shift)
    length = sum(one.shape[0] for one in vectors)
    small = jnp.zeros((length,), F32)
    at = 0
    for one in vectors:
        small += jnp.pad(one.astype(F32), (at, length - at - one.shape[0]))
        at += one.shape[0]
    small = jnp.broadcast_to(small[None, :], (8, length))
    fw = Forward(row_count, model_width, heads_width, hidden).call(
        lengths, tokens, positions, swap_ids, swap_rows, w_query, w_key, w_value, w_out, w_up, w_down,
        cotangent, small,
    )
    arrays = dict(
        grad_down=fw.grad_down, act=fw.act, wd=w_down, slope=fw.slope, wd_o=fw.wd, grad_second=fw.grad_second,
        wu=w_up, wu_o=fw.wu, first_low=fw.first_low, first_normed=fw.first_normed, first_inv=fw.first_inv,
        sums=fw.sums, wo=w_out, wo_o=fw.wo, q=fw.q, k=fw.k, v=fw.v, lse=fw.lse, mixed=fw.mixed, inp=fw.inp,
        wq=w_query, wk=w_key, wv=w_value, wq_o=fw.wq, wk_o=fw.wk, wv_o=fw.wv, place=fw.place,
    )
    back = Backward(row_count, model_width, heads_width, hidden)
    summed, summed_x, grad_tokens = back.call(lengths, small, arrays)
    if dp_count > 16:
        groups = [list(range(i, dp_count, 16)) for i in range(16)]
        summed, summed_x = lax.psum((summed, summed_x), "dp", axis_index_groups=groups)
    packed = summed.reshape(summed.shape[0], 256, model_width)
    packed_x = summed_x.reshape(-1, model_width)
    repl = swap_rows.shape[0]
    sum_down, sum_up, sum_out, sum_query, sum_key, sum_value, sum_swap, shared, private = unpack(
        packed, packed_x, row_count, model_width, heads_width, hidden, repl
    )
    return (
        fw.layer,
        grad_tokens,
        sum_swap,
        sum_query,
        private[0],
        sum_key,
        sum_value,
        private[1],
        sum_out,
        shared[0],
        shared[1],
        shared[2],
        sum_up,
        private[2:6].reshape(-1),
        sum_down,
        shared[5],
        shared[3],
        shared[4],
    )


def solution(mesh):
    in_specs = (
        P("dp", None),
        P("dp"),
        P("dp", None),
        P("dp", None),
        P(),
        P(None, "tensor"),
        P("tensor"),
        P(None, "tensor"),
        P(None, "tensor"),
        P("tensor"),
        P("tensor", None),
        P(),
        P(),
        P(),
        P(None, "tensor"),
        P("tensor"),
        P("tensor", None),
        P(),
        P(),
        P(),
        P("dp", None),
    )
    out_specs = (
        P("dp", None),
        P("dp", None),
        P(),
        P(None, "tensor"),
        P("tensor"),
        P(None, "tensor"),
        P(None, "tensor"),
        P("tensor"),
        P("tensor", None),
        P(),
        P(),
        P(),
        P(None, "tensor"),
        P("tensor"),
        P("tensor", None),
        P(),
        P(),
        P(),
    )
    count = mesh.shape["dp"]

    def run(*arrays):
        return local(*arrays, dp_count=count)

    return jax.shard_map(run, mesh=mesh, in_specs=in_specs, out_specs=out_specs, check_vma=False)
```
